32 devices in a mesh: dp: 4 (over y, x), fsdp: 8 (over z, core).
Axes of the slice: x: 2, y: 2, z: 4, core: 2. Of those that a mesh axis runs over, the one named last changes fastest.
Arguments:
- tokens: bfloat16 [32768, 768], P(('dp', 'fsdp')), may hold values from -12 to 12
- cotangent: bfloat16 [32768, 768], P(('dp', 'fsdp')), may hold values from -6 to 6
- lengths: int32 [32, 16], P(('dp', 'fsdp')), may hold values from 1 to 781, 1024 in all within a row
- qkv_weight: float32 [3, 768, 768], P(None, ('dp', 'fsdp')), may hold values from -0.109375 to 0.109375
- out_weight: float32 [768, 768], P(('dp', 'fsdp')), may hold values from -0.4375 to 0.4375
- in_weight: float32 [768, 3072], P(('dp', 'fsdp')), may hold values from -0.25980762 to 0.25980762
- down_weight: float32 [3072, 768], P(('dp', 'fsdp')), may hold values from -0.109375 to 0.109375
- vectors: float32 [12, 768], P(None, ('dp', 'fsdp')), may hold values from -1 to 2.5
- qkv_first: float32 [3, 768, 768], P(None, ('dp', 'fsdp')), may hold values from -8.59375e-05 to 8.59375e-05
- out_first: float32 [768, 768], P(('dp', 'fsdp')), may hold values from -3.3854165e-05 to 3.3854165e-05
- in_first: float32 [768, 3072], P(('dp', 'fsdp')), may hold values from -0.00011458333 to 0.00011458333
- down_first: float32 [3072, 768], P(('dp', 'fsdp')), may hold values from -0.00028645832 to 0.00028645832
- vec_first: float32 [12, 768], P(None, ('dp', 'fsdp')), may hold values from -0.00013020834 to 0.00013020834
- qkv_second: float32 [3, 768, 768], P(None, ('dp', 'fsdp')), may hold values from 9.536743e-12 to 3.814697e-11
- out_second: float32 [768, 768], P(('dp', 'fsdp')), may hold values from 1.5258789e-12 to 6.1035157e-12
- in_second: float32 [768, 3072], P(('dp', 'fsdp')), may hold values from 1.695421e-11 to 6.781684e-11
- down_second: float32 [3072, 768], P(('dp', 'fsdp')), may hold values from 1.05963814e-10 to 4.2385526e-10
- vec_second: float32 [12, 768], P(None, ('dp', 'fsdp')), may hold values from 2.6490954e-11 to 1.05963814e-10
Outputs:
- layer_out: bfloat16 [32768, 768], P(('dp', 'fsdp'))
- input_grad: bfloat16 [32768, 768], P(('dp', 'fsdp'))
- grad_norm: float32 [], replicated
- qkv_new: float32 [3, 768, 768], P(None, ('dp', 'fsdp'))
- out_new: float32 [768, 768], P(('dp', 'fsdp'))
- in_new: float32 [768, 3072], P(('dp', 'fsdp'))
- down_new: float32 [3072, 768], P(('dp', 'fsdp'))
- vectors_new: float32 [12, 768], P(None, ('dp', 'fsdp'))
- qkv_first_new: float32 [3, 768, 768], P(None, ('dp', 'fsdp'))
- out_first_new: float32 [768, 768], P(('dp', 'fsdp'))
- in_first_new: float32 [768, 3072], P(('dp', 'fsdp'))
- down_first_new: float32 [3072, 768], P(('dp', 'fsdp'))
- vec_first_new: float32 [12, 768], P(None, ('dp', 'fsdp'))
- qkv_second_new: float32 [3, 768, 768], P(None, ('dp', 'fsdp'))
- out_second_new: float32 [768, 768], P(('dp', 'fsdp'))
- in_second_new: float32 [768, 3072], P(('dp', 'fsdp'))
- down_second_new: float32 [3072, 768], P(('dp', 'fsdp'))
- vec_second_new: float32 [12, 768], P(None, ('dp', 'fsdp'))
The draws below stay inside these ranges and needn't reach their ends.
Inputs may be any that keep to these rules, and one draw needn't show every extreme that they name: Each device's 16 lengths sum to 1024; its longest is 781.
All inputs are finite; a program needn't handle non-finite values.
Results may differ from the reference program's by a relative error of at most 0.015.
The reference program's roundings to bfloat16 on the way count: a program that leaves them out, or rounds other values in their place, can miss the bound.
Values may be sent and summed in bfloat16 or wider, within the bound.
A program may use at most 256 MiB of HBM per device.

```python
import math
import jax
import jax.numpy as jnp
import numpy as np
from jax import lax

D = 768
H = 12
HD = 64
FF = 3072
TOK_DEV = 1024
SEQS = 16
LONGEST = 781
STEP = 10
TOKENS = 32768
N_DP = 4
N_FSDP = 8


def draw_tokens(key, part):
    key = jax.random.fold_in(key, 11)
    column = jnp.arange(D, dtype=jnp.float32) / max(D - 1, 1)
    base = jnp.clip(jax.random.normal(key, (TOKENS, D), jnp.float32), -4.0, 4.0)
    rising = 1.0 + 2.0 * column
    return (base * rising[None, :]).astype(jnp.bfloat16)


def draw_in_weight(key, part):
    key = jax.random.fold_in(key, 12)
    column = jnp.arange(FF, dtype=jnp.float32) / max(FF - 1, 1)
    base = jnp.clip(jax.random.normal(key, (D, FF), jnp.float32), -4.0, 4.0)
    rising = 0.6 + 1.2 * column
    return base * rising[None, :] * D ** (-0.5)


def draw_vectors(key, part):
    key = jax.random.fold_in(key, 13)
    key_bias, key_gain, key_other = jax.random.split(key, 3)
    column = jnp.arange(D, dtype=jnp.float32) / max(D - 1, 1)
    biases = 0.2 * jnp.clip(jax.random.normal(key_bias, (12, D), jnp.float32), -4.0, 4.0)
    rising = 0.5 + column
    gain_first = rising * jax.random.uniform(key_gain, (D,), jnp.float32, 0.8, 1.2)
    gain_second = jax.random.uniform(key_other, (D,), jnp.float32, 0.7, 1.3)
    return biases.at[4].set(gain_first).at[6].set(gain_second)


def block_scale(rng, dims, shards, least, largest):
    loudness, own = 1.0, jax.random.fold_in(rng, 6)
    for dim, parts in shards:
        heights = jnp.exp(jax.random.uniform(jax.random.fold_in(own, dim), (parts,), jnp.float32, least / len(shards), largest / len(shards)))
        loudness = loudness * jnp.repeat(heights, dims[dim] // parts).reshape([-1 if axis == dim else 1 for axis in range(len(dims))])
    return loudness


def profile(count, total, reach, skew):
    portions = [(1 << 20) // math.isqrt(standing ** skew) + 1 for standing in range(2, count + 1)]
    spare, holding = total - reach - (count - 1), [1] * (count - 1)
    while spare > 0:
        movable = [i for i in range(count - 1) if holding[i] < reach]
        whole, budget = sum([portions[i] for i in movable]), spare
        for i in movable:
            more = min(reach - holding[i], max(1, budget * portions[i] // whole), spare)
            holding[i] = holding[i] + more
            spare = spare - more
    return np.array([reach] + holding)


def uneven_parts(own_key, count, total, bound, slope):
    if count == 2:
        one = jax.random.randint(own_key, (), max(1, total - bound), min(bound, total - 1) + 1)
        return jnp.stack([one, total - one])
    sizes = jnp.asarray(profile(count, total, bound, slope), jnp.int32)
    twos = (count - 1) // 2
    source_of, receiver = sizes[1:1 + 2 * twos:2], sizes[2:2 + 2 * twos:2]
    room = jnp.minimum(source_of - 1, bound - receiver)
    passed = jax.random.randint(jax.random.fold_in(own_key, 1), (twos,), 0, 1 << 20) % (room + 1)
    sizes = sizes.at[1:1 + 2 * twos:2].set(source_of - passed).at[2:2 + 2 * twos:2].set(receiver + passed)
    return sizes[jax.random.permutation(jax.random.fold_in(own_key, 2), count)]


def normal_values(rng, shape, width, bound, pieces=(), kind=jnp.bfloat16):
    gain = block_scale(rng, shape, pieces, -0.22, 0.18) if pieces else 1.0
    drawn = jax.random.normal(rng, shape, jnp.float32) * width * gain
    return jnp.minimum(jnp.maximum(drawn, -bound), bound).astype(kind)


def setup_inputs(seed: int = 0) -> dict:
    keys = jax.random.split(jax.random.key(seed), 19)
    tokens = draw_tokens(jax.random.fold_in(keys[18], 71), 0)
    cotangent = normal_values(keys[1], (TOKENS, D), 1.0, 6.0, ((0, 32),))
    lengths = jax.vmap(lambda own: uneven_parts(own, SEQS, TOK_DEV, LONGEST, 2))(jax.random.split(keys[2], (N_DP * N_FSDP))).reshape((N_DP * N_FSDP, SEQS)).astype(jnp.int32)
    qkv_weight = normal_values(keys[3], (3, D, D), (4 * D) ** -0.5, 0.109375, ((1, 32),), jnp.float32)
    out_weight = normal_values(keys[4], (D, D), (D // 4) ** -0.5, 0.4375, ((0, 32),), jnp.float32)
    in_weight = draw_in_weight(jax.random.fold_in(keys[18], 71), 0)
    down_weight = normal_values(keys[6], (FF, D), FF ** -0.5, 0.109375, ((0, 32),), jnp.float32)
    vectors = draw_vectors(jax.random.fold_in(keys[18], 71), 0)
    qkv_first = normal_values(keys[8], (3, D, D), (0.033 * (D * FF) ** -0.5), 8.593749953433871e-05, ((1, 32),), jnp.float32)
    out_first = normal_values(keys[9], (D, D), (0.013 * (D * FF) ** -0.5), 3.385416493983939e-05, ((0, 32),), jnp.float32)
    in_first = normal_values(keys[10], (D, FF), (0.044 * (D * FF) ** -0.5), 0.00011458333, ((0, 32),), jnp.float32)
    down_first = normal_values(keys[11], (FF, D), (0.11 * (D * FF) ** -0.5), 0.00028645832, ((0, 32),), jnp.float32)
    vec_first = normal_values(keys[12], (12, D), (0.05 * (D * FF) ** -0.5), 0.00013020834, ((1, 32),), jnp.float32)
    qkv_second = jnp.clip(jnp.exp(math.log(3.8146971692576415e-11) - 1.3862944 * jax.random.uniform(keys[13], (3, D, D), jnp.float32) ** block_scale(keys[13], (3, D, D), ((1, 32),), -0.2, 0.2)), 9.536742923144104e-12, 3.8146971692576415e-11)
    out_second = jnp.clip(jnp.exp(math.log(6.103515696326278e-12) - 1.3862944 * jax.random.uniform(keys[14], (D, D), jnp.float32) ** block_scale(keys[14], (D, D), ((0, 32),), -0.2, 0.2)), 1.5258789240815696e-12, 6.103515696326278e-12)
    in_second = jnp.clip(jnp.exp(math.log(6.781684241952135e-11) - 1.3862944 * jax.random.uniform(keys[15], (D, FF), jnp.float32) ** block_scale(keys[15], (D, FF), ((0, 32),), -0.2, 0.2)), 1.6954210604880338e-11, 6.781684241952135e-11)
    down_second = jnp.clip(jnp.exp(math.log(4.2385525644839106e-10) - 1.3862944 * jax.random.uniform(keys[16], (FF, D), jnp.float32) ** block_scale(keys[16], (FF, D), ((0, 32),), -0.2, 0.2)), 1.0596381411209777e-10, 4.2385525644839106e-10)
    vec_second = jnp.clip(jnp.exp(math.log(1.0596381411209777e-10) - 1.3862944 * jax.random.uniform(keys[17], (12, D), jnp.float32) ** block_scale(keys[17], (12, D), ((1, 32),), -0.2, 0.2)), 2.649095352802444e-11, 1.0596381411209777e-10)
    return dict(tokens=tokens, cotangent=cotangent, lengths=lengths, qkv_weight=qkv_weight, out_weight=out_weight, in_weight=in_weight, down_weight=down_weight, vectors=vectors, qkv_first=qkv_first, out_first=out_first, in_first=in_first, down_first=down_first, vec_first=vec_first, qkv_second=qkv_second, out_second=out_second, in_second=in_second, down_second=down_second, vec_second=vec_second)


@jax.custom_vjp
def low(v):
    return lax.optimization_barrier(v.astype(jnp.bfloat16)).astype(jnp.float32)

@jax.custom_vjp
def low_back(v):
    return v

def low_keep(v):
    return (low(v), None)

def low_pass(kept, grad):
    return (grad,)

def back_keep(v):
    return (v, None)

def back_low(kept, grad):
    return (low(grad),)
low.defvjp(low_keep, low_pass)
low_back.defvjp(back_keep, back_low)
highest = lax.Precision.HIGHEST
moment_decay = 0.9
square_decay = 0.999
learn_rate = 0.02
vector_rate = 0.15
weight_decay = 0.01
adam_epsilon = 1e-08
clip_limit = 1.0
norm_epsilon = 1e-05

def layer_norm(hidden, gain_vec, shift_vec):
    center = hidden - lax.optimization_barrier(jnp.mean(hidden, axis=-1, keepdims=True))
    spread = lax.optimization_barrier(jnp.mean(center * center, axis=-1, keepdims=True))
    return center * lax.rsqrt(spread + norm_epsilon) * gain_vec + shift_vec

def segment_ids(lengths):
    bounds = jnp.cumsum(lengths, axis=-1).astype(jnp.int32)
    places = jnp.arange(TOK_DEV, dtype=jnp.int32)
    return lax.optimization_barrier(jnp.sum((places[None, :, None] >= bounds[:, None, :]).astype(jnp.int32), axis=-1))

def product(left, right):
    return jnp.dot(left, right, precision=highest)

def attend_pack(inputs):
    queries, keys_in, values, segment = inputs
    query_heads = queries.reshape(TOK_DEV, H, HD)
    key_heads = keys_in.reshape(TOK_DEV, H, HD)
    value_heads = values.reshape(TOK_DEV, H, HD)
    scores = jnp.einsum('qhd,khd->hqk', query_heads, key_heads, precision=highest) * HD ** (-0.5)
    scores = low_back(scores)
    allowed = segment[:, None] == segment[None, :]
    scores = jnp.where(allowed[None], scores, -1e+30)
    weights = jax.nn.softmax(scores, axis=-1)
    context = jnp.einsum('hqk,khd->qhd', low(weights), value_heads, precision=highest)
    return context.reshape(TOK_DEV, D)

def adam_step(weight, gradient, first_old, second_old, decay_rate, step_rate):
    first_new = moment_decay * first_old + (1.0 - moment_decay) * gradient
    second_new = square_decay * second_old + (1.0 - square_decay) * gradient * gradient
    first_hat = first_new / (1.0 - moment_decay ** STEP)
    second_hat = second_new / (1.0 - square_decay ** STEP)
    weight_new = weight - step_rate * (first_hat / (jnp.sqrt(second_hat) + adam_epsilon) + decay_rate * weight)
    return (weight_new, first_new, second_new)

def reference(tokens, cotangent, lengths, qkv_weight, out_weight, in_weight, down_weight, vectors, qkv_first, out_first, in_first, down_first, vec_first, qkv_second, out_second, in_second, down_second, vec_second):
    segments = segment_ids(lengths)
    pack_count = lengths.shape[0]

    def forward(inputs, qkv_all, out_all, in_all, down_all, vec_all):
        qkv_low = low(qkv_all)
        out_low = low(out_all)
        in_low = low(in_all)
        down_low = low(down_all)
        vec_low = low(vec_all)
        bias_hidden = vec_low[8:12].reshape(FF)
        queries = low(low_back(product(inputs, qkv_low[0]) + vec_low[0]))
        keys_all = low(low_back(product(inputs, qkv_low[1])))
        values = low(low_back(product(inputs, qkv_low[2]) + vec_low[1]))
        context = lax.map(jax.checkpoint(attend_pack), (queries.reshape(pack_count, TOK_DEV, D), keys_all.reshape(pack_count, TOK_DEV, D), values.reshape(pack_count, TOK_DEV, D), segments))
        context = low(low_back(context.reshape(pack_count * TOK_DEV, D)))
        branch = low_back(product(context, out_low) + vec_low[2])
        normed = layer_norm(inputs + branch, vec_low[4], vec_low[5])
        hidden_pre = low_back(product(low(normed), in_low) + bias_hidden)
        hidden = low(jax.nn.gelu(hidden_pre, approximate=False))
        ffn_out = low_back(product(hidden, down_low) + vec_low[3])
        return layer_norm(normed + ffn_out, vec_low[6], vec_low[7])
    outputs, pullback = jax.vjp(forward, tokens.astype(jnp.float32), qkv_weight, out_weight, in_weight, down_weight, vectors)
    grads = pullback(cotangent.astype(jnp.float32))
    input_grad = grads[0]
    qkv_grad, out_grad, in_grad, down_grad, vec_grad = (grads[1], grads[2], grads[3], grads[4], grads[5])
    squares = jnp.sum(qkv_grad * qkv_grad) + jnp.sum(out_grad * out_grad) + jnp.sum(in_grad * in_grad) + jnp.sum(down_grad * down_grad) + jnp.sum(vec_grad * vec_grad)
    grad_norm = jnp.sqrt(squares)
    factor = jnp.minimum(1.0, clip_limit / (grad_norm + 1e-06))
    qkv_new, qkv_first_new, qkv_second_new = adam_step(qkv_weight, factor * qkv_grad, qkv_first, qkv_second, weight_decay, learn_rate)
    out_new, out_first_new, out_second_new = adam_step(out_weight, factor * out_grad, out_first, out_second, weight_decay, learn_rate)
    in_new, in_first_new, in_second_new = adam_step(in_weight, factor * in_grad, in_first, in_second, weight_decay, learn_rate)
    down_new, down_first_new, down_second_new = adam_step(down_weight, factor * down_grad, down_first, down_second, weight_decay, learn_rate)
    vectors_new, vec_first_new, vec_second_new = adam_step(vectors, factor * vec_grad, vec_first, vec_second, 0.0, vector_rate)
    return (outputs.astype(jnp.bfloat16), input_grad.astype(jnp.bfloat16), grad_norm, qkv_new, out_new, in_new, down_new, vectors_new, qkv_first_new, out_first_new, in_first_new, down_first_new, vec_first_new, qkv_second_new, out_second_new, in_second_new, down_second_new, vec_second_new)
```

```python
import functools

import jax
import jax.numpy as jnp
from jax import lax
from jax.experimental import pallas as pl
from jax.experimental.pallas import tpu as pltpu
from jax.sharding import PartitionSpec as P

D = 768
H = 12
HD = 64
FF = 3072
T = 1024
STEP = 10
PAIRS = H // 2
W3 = 384

moment_decay = 0.9
square_decay = 0.999
learn_rate = 0.02
vector_rate = 0.15
weight_decay = 0.01
adam_epsilon = 1e-08
clip_limit = 1.0
norm_epsilon = 1e-05

bf = jnp.bfloat16
f32 = jnp.float32
MESH = pl.DeviceIdType.MESH
VM = pl.BlockSpec(memory_space=pltpu.VMEM)
ANY = pl.BlockSpec(memory_space=pl.ANY)
MIB = 2**20


def S(shape, dtype):
    return jax.ShapeDtypeStruct(shape, dtype)


def nn(a, b):
    return lax.dot_general(a, b, (((1,), (0,)), ((), ())), preferred_element_type=f32)


def nt(a, b):
    return lax.dot_general(a, b, (((1,), (1,)), ((), ())), preferred_element_type=f32)


def tn(a, b):
    return lax.dot_general(a, b, (((0,), (0,)), ((), ())), preferred_element_type=f32)


def colsum(x):
    return jnp.sum(x, axis=0, keepdims=True)


class Place:
    def __init__(self):
        self.dp = lax.axis_index("dp")
        self.fs = lax.axis_index("fsdp")
        self.z = self.fs // 2
        self.k = self.fs % 2
        dp, k = self.dp, self.k
        xn = dp + 1 - 2 * (dp % 2)
        yn = (dp + 2) % 4
        self.dp1 = xn * (1 - k) + yn * k
        self.dp2 = yn * (1 - k) + xn * k
        self.dp3 = 3 - dp
        self.n1 = (self.dp1, self.fs)
        self.n2 = (self.dp2, self.fs)
        self.sib = (dp, self.z * 2 + 1 - k)
        self.zp = [(dp, ((self.z + i) % 4) * 2 + k) for i in (1, 2, 3)]
        self.m = dp * 2 + k
        self.others = []
        for j in range(1, 8):
            other = (self.m + j) % 8
            self.others.append((other // 2, self.z * 2 + other % 2))


def enter(peers):
    barrier = pltpu.get_barrier_semaphore()
    for peer in peers:
        pl.semaphore_signal(barrier, inc=1, device_id=peer, device_id_type=MESH)
    pl.semaphore_wait(barrier, len(peers))


def rcopy(src, dst, ssem, rsem, peer):
    return pltpu.make_async_remote_copy(src, dst, ssem, rsem, device_id=peer, device_id_type=MESH)


def gather_kernel(
    qkv, out, inw, down, vec, wqkv, wo, wi, w2, vt,
    sx_qkv, sx_out, sx_in, sx_down, sx_vec, myvec, own_qkv, own_out, own_in, own_down, own_vec,
    xs, xr, gs, gr, ls,
):
    p = Place()
    k = p.k
    enter([p.sib, p.n1, p.n2] + p.zp)
    pad = jnp.concatenate([vec[...], jnp.zeros((128 - 12, 24), f32)], axis=0)
    myvec[...] = jnp.concatenate([pad, jnp.zeros((128, 104), f32)], axis=1).T[:24, :]
    half = lambda w, c: pl.ds(pl.multiple_of(c * w, 128), w)
    far = 1 - k
    swaps = [
        rcopy(qkv.at[:, :, half(W3, far)], sx_qkv, xs.at[0], xr.at[0], p.sib),
        rcopy(myvec, sx_vec, xs.at[4], xr.at[4], p.sib),
        rcopy(out.at[:, half(W3, far)], sx_out, xs.at[1], xr.at[1], p.sib),
        rcopy(inw.at[:, half(4 * W3, far)], sx_in, xs.at[2], xr.at[2], p.sib),
        rcopy(down.at[:, half(W3, far)], sx_down, xs.at[3], xr.at[3], p.sib),
    ]
    for c in swaps:
        c.start()
    for c in swaps:
        c.wait()

    def both(mine, other):
        lo = jnp.where(k == 0, mine, other)
        hi = jnp.where(k == 0, other, mine)
        return jnp.concatenate([lo, hi], axis=0).astype(bf)

    for j in range(3):
        mat = both(qkv[j, :, half(W3, k)], sx_qkv[j])
        for t in range(3):
            own_qkv[:, t * W3 + j * 128 : t * W3 + (j + 1) * 128] = mat[:, t * 128 : (t + 1) * 128]
    own_vec[...] = both(myvec[...], sx_vec[...])
    own_out[...] = both(out[:, half(W3, k)], sx_out[...])
    own_in[...] = both(inw[:, half(4 * W3, k)], sx_in[...])
    own_down[...] = both(down[:, half(W3, k)], sx_down[...])
    chip = p.dp * 4 + p.z
    rows48 = pl.ds(pl.multiple_of(chip * 48, 16), 48)
    rows192 = pl.ds(pl.multiple_of(chip * 192, 16), 192)
    local = [
        pltpu.make_async_copy(own_qkv, wqkv.at[rows48, half(3 * W3, k)], ls.at[0]),
        pltpu.make_async_copy(own_out, wo.at[rows48, half(W3, k)], ls.at[1]),
        pltpu.make_async_copy(own_in, wi.at[rows48, half(4 * W3, k)], ls.at[2]),
        pltpu.make_async_copy(own_down, w2.at[rows192, half(W3, k)], ls.at[3]),
        pltpu.make_async_copy(own_vec, vt.at[rows48, :], ls.at[4]),
    ]
    for c in local:
        c.start()
    for c in local:
        c.wait()

    chunks = [(vt, 48, pl.ds(0, 128))]
    for t in range(3):
        chunks.append((wqkv, 48, pl.ds(pl.multiple_of((t + 3 * k) * W3, 128), W3)))
    chunks.append((wo, 48, pl.ds(pl.multiple_of(k * W3, 128), W3)))
    for t in range(4):
        chunks.append((wi, 48, pl.ds(pl.multiple_of((t + 4 * k) * W3, 128), W3)))
    for t in range(3):
        chunks.append((w2, 192, pl.ds(pl.multiple_of(k * W3 + t * 128, 128), 128)))

    def rowsof(rc, dp, z=None):
        if z is None:
            return pl.ds(pl.multiple_of(dp * 4 * rc, 16), 4 * rc)
        return pl.ds(pl.multiple_of((dp * 4 + z) * rc, 16), rc)

    def same(i, j, rows, peer):
        ref, rc, cols = chunks[i]
        view = ref.at[rows, cols]
        return rcopy(view, view, gs.at[i, j], gr.at[i, j], peer)

    sent = []

    def go(c):
        c.start()
        sent.append(c)
        return c

    n = len(chunks)
    zc, c1, c2, c3, c4 = {}, {}, {}, {}, {}
    for s in range(n + 4):
        if s < n:
            rc = chunks[s][1]
            zc[s] = [go(same(s, i, rowsof(rc, p.dp, p.z), p.zp[i])) for i in range(3)]
        i = s - 1
        if 0 <= i < n:
            rc = chunks[i][1]
            for c in zc[i]:
                c.wait_recv()
            c1[i] = go(same(i, 3, rowsof(rc, p.dp), p.n1))
            c2[i] = go(same(i, 4, rowsof(rc, p.dp), p.n2))
        i = s - 2
        if 0 <= i < n:
            rc = chunks[i][1]
            c1[i].wait_recv()
            c3[i] = go(same(i, 5, rowsof(rc, p.dp1), p.n2))
        i = s - 3
        if 0 <= i < n:
            rc = chunks[i][1]
            c2[i].wait_recv()
            c3[i].wait_recv()
            if i > 0:
                c4[i] = go(same(i, 6, pl.ds(0, 16 * rc), p.sib))
        i = s - 4
        if 0 < i < n:
            c4[i].wait_recv()
    for c in sent:
        c.wait_send()


def gather_weights(qkv, out, inw, down, vec):
    return pl.pallas_call(
        gather_kernel,
        in_specs=[VM] * 5,
        out_specs=[ANY] * 5,
        out_shape=[S((D, 3 * D), bf), S((D, D), bf), S((D, FF), bf), S((FF, D), bf), S((D, 128), bf)],
        scratch_shapes=[
            pltpu.VMEM((3, 24, W3), f32), pltpu.VMEM((24, W3), f32), pltpu.VMEM((24, 4 * W3), f32),
            pltpu.VMEM((96, W3), f32), pltpu.VMEM((24, 128), f32), pltpu.VMEM((24, 128), f32),
            pltpu.VMEM((48, 3 * W3), bf), pltpu.VMEM((48, W3), bf), pltpu.VMEM((48, 4 * W3), bf),
            pltpu.VMEM((192, W3), bf), pltpu.VMEM((48, 128), bf),
            pltpu.SemaphoreType.DMA((5,)), pltpu.SemaphoreType.DMA((5,)),
            pltpu.SemaphoreType.DMA((12, 7)), pltpu.SemaphoreType.DMA((12, 7)), pltpu.SemaphoreType.DMA((5,)),
        ],
        compiler_params=pltpu.CompilerParams(collective_id=0, has_side_effects=True, vmem_limit_bytes=40 * MIB),
        name="gather_weights",
    )(qkv, out, inw, down, vec)


def forward_kernel(block, tok, w, bias, onehot, neg, q_o, k_o, v_o, ctx_o, lse_o, qa, ka, va):
    lane = lax.broadcasted_iota(jnp.int32, (1, 128), 1)
    y = nn(tok[...], w[...]) + bias[...]
    q = y[:, :128].astype(bf)
    key = y[:, 128:256].astype(bf)
    val = y[:, 256:].astype(bf)
    q_o[...] = q
    k_o[...] = key
    v_o[...] = val
    qs = (q.astype(f32) * HD ** (-0.5)).astype(bf)
    ka[:, :128] = key
    ka[:, 128:] = neg[...]
    va[:, :128] = val
    va[:, 128:] = jnp.ones((T, 128), bf)
    qa[:, 128:] = onehot[...]
    for h in range(2):
        sel = (lane // 64) == h
        qa[:, :128] = jnp.where(sel, qs, jnp.zeros_like(qs))
        for b in range(T // block):
            r = slice(b * block, (b + 1) * block)
            s = nt(qa[r, :], ka[...])
            m = jnp.max(s, axis=1, keepdims=True)
            e = jnp.exp(s - m).astype(bf)
            o = nn(e, va[...])
            tot = o[:, 128:]
            c = o[:, :128] / tot
            l = m + jnp.log(tot)
            if h == 0:
                ctx_o[r, :] = c
                lse_o[0, r, :] = l
            else:
                ctx_o[r, :] = jnp.where(sel, c, ctx_o[r, :])
                lse_o[0, r, :] = jnp.where(lane == 1, l, lse_o[0, r, :])


def attend(tok, w, bias, onehot, neg, block=256):
    full = lambda s: pl.BlockSpec(s, lambda i: (0,) * len(s))
    col = pl.BlockSpec((T, 128), lambda i: (0, i))
    return pl.pallas_call(
        functools.partial(forward_kernel, block),
        grid=(PAIRS,),
        in_specs=[
            full((T, D)), pl.BlockSpec((D, W3), lambda i: (0, i)), pl.BlockSpec((1, W3), lambda i: (0, i)),
            full((T, 128)), full((T, 128)),
        ],
        out_specs=[col, col, col, col, pl.BlockSpec((1, T, 128), lambda i: (i, 0, 0))],
        out_shape=[S((T, D), bf)] * 3 + [S((T, D), f32), S((PAIRS, T, 128), f32)],
        scratch_shapes=[pltpu.VMEM((T, 256), bf)] * 3,
        compiler_params=pltpu.CompilerParams(vmem_limit_bytes=50 * MIB),
        name="attend",
    )(tok, w, bias, onehot, neg)


def split3(x):
    hi = x.astype(bf).astype(f32)
    mid = (x - hi).astype(bf).astype(f32)
    return hi, mid, x - hi - mid


def backward_kernel(
    block, tok, w, dh1, q_i, k_i, v_i, dctx_i, ctx_i, lse_i, onehot, neg,
    g_o, ig_o, vg_o, qa, ka, va, da, kT, dqT, dka, dva, tokT, ig,
):
    lane = lax.broadcasted_iota(jnp.int32, (1, 128), 1)
    step = pl.program_id(0)

    @pl.when(step == 0)
    def _():
        tokT[...] = tok[...].T
        ig[...] = dh1[...]

    key = k_i[...]
    val = v_i[...]
    qs = (q_i[...].astype(f32) * HD ** (-0.5)).astype(bf)
    minus = jnp.where((lane >= 16) & (lane < 19), -1.0, 0.0)
    ka[:, :128] = key
    ka[:, 128:] = (neg[...].astype(f32) + minus).astype(bf)
    va[:, :128] = val
    va[:, 128:] = jnp.broadcast_to(minus, (T, 128)).astype(bf)
    kT[...] = key.T
    d = dctx_i[...]
    prod = d.astype(f32) * ctx_i[...]
    for h in range(2):
        sel = (lane // 64) == h
        inner = jnp.sum(jnp.where(sel, prod, 0.0), axis=1, keepdims=True)
        lse = jnp.sum(jnp.where(lane == h, lse_i[0], 0.0), axis=1, keepdims=True)

        def extra(base, parts):
            for j, part in enumerate(parts):
                base = jnp.where(lane == 16 + j, part, base)
            return base.astype(bf)

        qa[:, :128] = jnp.where(sel, qs, jnp.zeros_like(qs))
        qa[:, 128:] = extra(onehot[...].astype(f32), split3(lse))
        da[:, :128] = jnp.where(sel, d, jnp.zeros_like(d))
        da[:, 128:] = extra(jnp.zeros((T, 128), f32), split3(inner))
        for b in range(T // block):
            r = slice(b * block, (b + 1) * block)
            pt = jnp.exp(nt(ka[...], qa[r, :]))
            dpt = nt(va[...], da[r, :])
            ds = (pt * dpt).astype(bf)
            x = nn(pt.astype(bf), da[r, :128])
            y = nn(ds, qa[r, :128])
            dqT[h * 64 : (h + 1) * 64, r] = nn(kT[h * 64 : (h + 1) * 64, :], ds)
            if h == 0 and b == 0:
                dva[...] = x
                dka[...] = y
            else:
                dva[...] += x
                dka[...] += y
    dv = dva[...].astype(bf)
    dk = dka[...].astype(bf)
    dq = (dqT[...].T * HD ** (-0.5)).astype(bf)
    vg_o[...] = jnp.zeros_like(vg_o)
    vg_o[0:1, :] = colsum(dq.astype(f32))
    vg_o[1:2, :] = colsum(dv.astype(f32))
    cat = jnp.concatenate([dq, dk, dv], axis=1)
    g_o[...] = nn(tokT[...], cat).astype(bf)
    ig[...] += nt(cat, w[...])

    @pl.when(step == PAIRS - 1)
    def _():
        ig_o[...] = ig[...].astype(bf)


def attend_back(tok, w, dh1, q, k, v, dctx, ctx, lse, onehot, neg, block=512):
    full = lambda s: pl.BlockSpec(s, lambda i: (0,) * len(s))
    col = pl.BlockSpec((T, 128), lambda i: (0, i))
    return pl.pallas_call(
        functools.partial(backward_kernel, block),
        grid=(PAIRS,),
        in_specs=[
            full((T, D)), pl.BlockSpec((D, W3), lambda i: (0, i)), full((T, D)),
            col, col, col, col, col, pl.BlockSpec((1, T, 128), lambda i: (i, 0, 0)), full((T, 128)), full((T, 128)),
        ],
        out_specs=[pl.BlockSpec((D, W3), lambda i: (0, i)), full((T, D)), pl.BlockSpec((16, 128), lambda i: (0, i))],
        out_shape=[S((D, 3 * D), bf), S((T, D), bf), S((16, D), f32)],
        scratch_shapes=[pltpu.VMEM((T, 256), bf)] * 4
        + [pltpu.VMEM((128, T), bf), pltpu.VMEM((128, T), f32)]
        + [pltpu.VMEM((T, 128), f32)] * 2
        + [pltpu.VMEM((D, T), bf), pltpu.VMEM((T, D), f32)],
        compiler_params=pltpu.CompilerParams(vmem_limit_bytes=56 * MIB),
        name="attend_back",
    )(tok, w, dh1, q, k, v, dctx, ctx, lse, onehot, neg)


def gelu_parts(x):
    e = jnp.exp(x * x * (-0.5))
    t = 1.0 / (1.0 + (0.3275911 * 0.7071067811865476) * jnp.abs(x))
    poly = 0.5 * 1.061405429
    for a in (-1.453152027, 1.421413741, -0.284496736, 0.254829592):
        poly = 0.5 * a + t * poly
    tail = t * poly * e
    return jnp.where(x >= 0, 1.0 - tail, tail), e * 0.3989422804014327


def norm_forward(h):
    c = h - jnp.mean(h, axis=1, keepdims=True)
    r = lax.rsqrt(jnp.mean(c * c, axis=1, keepdims=True) + norm_epsilon)
    return c * r, r


def norm_backward(dy, xh, r, g):
    dx = dy * g
    return r * (dx - jnp.mean(dx, axis=1, keepdims=True) - xh * jnp.mean(dx * xh, axis=1, keepdims=True))


def ffn_kernel(
    block, tok, ctx, cot, vec, wo_h, wi_h, w2_h, out_o, dh1_o, dctx_o, vg_o, gwo_h, gwi_h, gw2_h,
    wo, wi, w2, cb, x1b, hb, gp, dfb, dhp, dab, stage, tr, insem, outsem,
):
    loads = [
        pltpu.make_async_copy(wo_h, wo, insem.at[0]),
        pltpu.make_async_copy(wi_h, wi, insem.at[1]),
        pltpu.make_async_copy(w2_h, w2, insem.at[2]),
    ]
    for c in loads:
        c.start()
    vg_o[...] = jnp.zeros_like(vg_o)
    row = lambda i: vec[i : i + 1, :]
    for c in loads:
        c.wait()

    def one_block(b, carry):
        r = pl.ds(pl.multiple_of(b * block, block), block)
        c = ctx[r, :].astype(bf)
        cb[r, :] = c
        xh1, r1 = norm_forward(tok[r, :].astype(f32) + (nn(c, wo[...]) + row(2)))
        x1 = xh1 * row(4) + row(5)
        xb = x1.astype(bf)
        x1b[r, :] = xb
        acc = x1 + row(3)
        for j in range(4):
            cs = slice(j * D, (j + 1) * D)
            hp = nn(xb, wi[:, cs]) + row(8 + j)
            big, dense = gelu_parts(hp)
            h = (hp * big).astype(bf)
            hb[r, cs] = h
            gp[:, cs] = big + hp * dense
            acc = acc + nn(h, w2[cs, :])
        xh2, r2 = norm_forward(acc)
        out_o[r, :] = (xh2 * row(6) + row(7)).astype(bf)
        dy = cot[r, :].astype(f32)
        vg_o[6:7, :] += colsum(dy * xh2)
        vg_o[7:8, :] += colsum(dy)
        dh2 = norm_backward(dy, xh2, r2, row(6))
        df = dh2.astype(bf)
        dfb[r, :] = df
        vg_o[3:4, :] += colsum(df.astype(f32))
        dx1 = dh2
        for j in range(4):
            cs = slice(j * D, (j + 1) * D)
            dh = (gp[:, cs] * nt(df, w2[cs, :])).astype(bf)
            dhp[r, cs] = dh
            vg_o[8 + j : 9 + j, :] += colsum(dh.astype(f32))
            dx1 = dx1 + nt(dh, wi[:, cs])
        vg_o[4:5, :] += colsum(dx1 * xh1)
        vg_o[5:6, :] += colsum(dx1)
        dh1 = norm_backward(dx1, xh1, r1, row(4))
        dh1_o[r, :] = dh1
        da = dh1.astype(bf)
        dab[r, :] = da
        vg_o[2:3, :] += colsum(da.astype(f32))
        dctx_o[r, :] = nt(da, wo[...]).astype(bf)
        return carry

    lax.fori_loop(0, T // block, one_block, 0)
    outs = []

    def emit(val, dst):
        i = len(outs)
        if i >= 2:
            outs[i - 2].wait()
        stage[i % 2] = val.astype(bf)
        c = pltpu.make_async_copy(stage.at[i % 2], dst, outsem.at[i % 2])
        c.start()
        outs.append(c)

    for j in range(4):
        cs = slice(j * D, (j + 1) * D)
        emit(tn(hb[:, cs], dfb[...]), gw2_h.at[cs, :])
    tr[...] = x1b[...].T
    for j in range(4):
        cs = slice(j * D, (j + 1) * D)
        emit(nn(tr[...], dhp[:, cs]), gwi_h.at[:, cs])
    emit(tn(cb[...], dab[...]), gwo_h)
    outs[7].wait()
    outs[8].wait()


def feed_forward(tok, ctx, cot, vec, wo, wi, w2, block=256):
    return pl.pallas_call(
        functools.partial(ffn_kernel, block),
        in_specs=[VM] * 4 + [ANY] * 3,
        out_specs=[VM] * 4 + [ANY] * 3,
        out_shape=[
            S((T, D), bf), S((T, D), f32), S((T, D), bf), S((16, D), f32), S((D, D), bf), S((D, FF), bf), S((FF, D), bf),
        ],
        scratch_shapes=[
            pltpu.VMEM((D, D), bf), pltpu.VMEM((D, FF), bf), pltpu.VMEM((FF, D), bf), pltpu.VMEM((T, D), bf),
            pltpu.VMEM((T, D), bf), pltpu.VMEM((T, FF), bf), pltpu.VMEM((block, FF), f32), pltpu.VMEM((T, D), bf),
            pltpu.VMEM((T, FF), bf), pltpu.VMEM((T, D), bf), pltpu.VMEM((2, D, D), bf), pltpu.VMEM((D, T), bf),
            pltpu.SemaphoreType.DMA((3,)), pltpu.SemaphoreType.DMA((2,)),
        ],
        compiler_params=pltpu.CompilerParams(vmem_limit_bytes=60 * MIB),
        name="feed_forward",
    )(tok, ctx, cot, vec, wo, wi, w2)


def reduce_kernel(
    gqkv, gwo, gwi, gw2, gvt, s_qkv, s_out, s_in, s_down, s_vec, total,
    acc_a, rs_a, r2_a, r1_a, rz_a, acc_d, rs_d, r2_d, r1_d, rz_d, acc_v, rs_v, r2_v, r1_v, rz_v,
    fin_a, fin_d, rx_a, rx_d, tile, nb1, nb2, gs, gr, ls, xs, xr, ns, nr,
):
    p = Place()
    k = p.k
    far = 1 - k
    enter(p.others + p.zp)
    sent = []

    def go(c):
        c.start()
        sent.append(c)
        return c

    def cols(start, w):
        return pl.ds(pl.multiple_of(start, 128), w)

    items = [(gvt, lambda c: 0, 128, 48, acc_v, rs_v, r2_v, r1_v, rz_v, None)]
    for t in range(3):
        items.append((gw2, lambda c, t=t: c * W3 + t * 128, 128, 192, acc_d.at[t], rs_d.at[t], r2_d.at[t], r1_d.at[t], rz_d.at[t], fin_d.at[t]))
    a = 0
    for t in range(4):
        items.append((gwi, lambda c, t=t: (t + 4 * c) * W3, W3, 48, acc_a.at[a], rs_a.at[a], r2_a.at[a], r1_a.at[a], rz_a.at[a], fin_a.at[a]))
        a += 1
    items.append((gwo, lambda c: c * W3, W3, 48, acc_a.at[a], rs_a.at[a], r2_a.at[a], r1_a.at[a], rz_a.at[a], fin_a.at[a]))
    a += 1
    for t in range(3):
        items.append((gqkv, lambda c, t=t: (t + 3 * c) * W3, W3, 48, acc_a.at[a], rs_a.at[a], r2_a.at[a], r1_a.at[a], rz_a.at[a], fin_a.at[a]))
        a += 1
    n = len(items)

    def add(dst, row0, src, rows):
        step = 96 if rows % 96 == 0 else rows
        def body(i, carry):
            d = pl.ds(pl.multiple_of(row0 + i * step, 16), step)
            s = pl.ds(pl.multiple_of(i * step, 16), step)
            dst[d, :] = (dst[d, :].astype(f32) + src[s, :].astype(f32)).astype(bf)
            return carry
        lax.fori_loop(0, rows // step, body, 0)

    cS, cL, cP, cQ, cZ = {}, {}, {}, {}, {}
    squares = jnp.zeros((8, 128), f32)

    def fold(x):
        rows, width = x.shape
        x = x * x
        tot = jnp.zeros((8, 128), f32)
        for i in range(rows // 8):
            for j in range(width // 128):
                tot = tot + x[i * 8 : (i + 1) * 8, j * 128 : (j + 1) * 128]
        return tot

    for i, (g, col, w, rc, acc, rs, r2, r1, rz, fin) in enumerate(items):
        cL[i] = pltpu.make_async_copy(g.at[:, cols(col(k), w)], acc, ls.at[i])
        cL[i].start()
        cS[i] = go(rcopy(g.at[:, cols(col(far), w)], rs, gs.at[i, 0], gr.at[i, 0], p.sib))
    for s in range(n + 3):
        i = s
        if i < n:
            g, col, w, rc, acc, rs, r2, r1, rz, fin = items[i]
            cL[i].wait()
            cS[i].wait_recv()
            add(acc, 0, rs, 16 * rc)
            grp = lambda dp: pl.ds(pl.multiple_of(dp * 4 * rc, 16), 4 * rc)
            cP[i] = [
                go(rcopy(acc.at[grp(p.dp2), :], r2.at[0], gs.at[i, 1], gr.at[i, 1], p.n2)),
                go(rcopy(acc.at[grp(p.dp3), :], r2.at[1], gs.at[i, 2], gr.at[i, 2], p.n2)),
            ]
        i = s - 1
        if 0 <= i < n:
            g, col, w, rc, acc, rs, r2, r1, rz, fin = items[i]
            cP[i][1].wait_recv()
            add(acc, p.dp1 * 4 * rc, r2.at[1], 4 * rc)
            cQ[i] = go(rcopy(acc.at[pl.ds(pl.multiple_of(p.dp1 * 4 * rc, 16), 4 * rc), :], r1, gs.at[i, 3], gr.at[i, 3], p.n1))
            cP[i][0].wait_recv()
            add(acc, p.dp * 4 * rc, r2.at[0], 4 * rc)
        i = s - 2
        if 0 <= i < n:
            g, col, w, rc, acc, rs, r2, r1, rz, fin = items[i]
            cQ[i].wait_recv()
            add(acc, p.dp * 4 * rc, r1, 4 * rc)
            cZ[i] = []
            for j in range(3):
                there = p.dp * 4 + (p.z + j + 1) % 4
                cZ[i].append(go(rcopy(acc.at[pl.ds(pl.multiple_of(there * rc, 16), rc), :], rz.at[j], gs.at[i, 4 + j], gr.at[i, 4 + j], p.zp[j])))
        i = s - 3
        if 0 <= i < n:
            g, col, w, rc, acc, rs, r2, r1, rz, fin = items[i]
            for c in cZ[i]:
                c.wait_recv()
            own = acc[pl.ds(pl.multiple_of((p.dp * 4 + p.z) * rc, 16), rc), :].astype(f32)
            for j in range(3):
                own = own + rz[j].astype(f32)
            if fin is None:
                mine = jnp.where(k == 0, own[:24], own[24:])
                s_vec[...] = mine
                squares = squares + fold(mine)
            else:
                fin[...] = own
                squares = squares + fold(own)
    cX = []
    for a in range(8):
        cX.append(go(rcopy(fin_a.at[a, pl.ds(pl.multiple_of(far * 24, 8), 24), :], rx_a.at[a], xs.at[a], xr.at[a], p.sib)))
    for t in range(3):
        cX.append(go(rcopy(fin_d.at[t, pl.ds(pl.multiple_of(far * 96, 8), 96), :], rx_d.at[t], xs.at[8 + t], xr.at[8 + t], p.sib)))
    part = jnp.sum(jnp.sum(squares, axis=1, keepdims=True), axis=0, keepdims=True)
    tile[0] = jnp.broadcast_to(part, (8, 128))
    cN = []
    for j in range(3):
        cN.append(go(rcopy(tile.at[0], nb1.at[j], ns.at[j], nr.at[j], p.zp[j])))
    for c in cN:
        c.wait_recv()
    zsum = jnp.zeros((8, 128), f32)
    for zz in range(4):
        val = tile[0]
        for j in range(3):
            val = jnp.where((p.z + 3 - j) % 4 == zz, nb1[j], val)
        zsum = zsum + val
    tile[1] = zsum
    cN = []
    for j in range(7):
        cN.append(go(rcopy(tile.at[1], nb2.at[j], ns.at[3 + j], nr.at[3 + j], p.others[j])))
    keep = lambda c: pl.ds(pl.multiple_of(c * W3, 128), W3)
    my24 = pl.ds(pl.multiple_of(k * 24, 8), 24)
    my96 = pl.ds(pl.multiple_of(k * 96, 8), 96)
    for c in cX:
        c.wait_recv()
    for src, side in ((lambda a: fin_a[a, my24, :], k), (lambda a: rx_a[a], far)):
        for t in range(4):
            s_in[:, cols((t + 4 * side) * W3, W3)] = src(t)
        s_out[:, keep(side)] = src(4)
        for t in range(3):
            val = src(5 + t)
            for j in range(3):
                s_qkv[j, :, cols(side * W3 + t * 128, 128)] = val[:, j * 128 : (j + 1) * 128]
    for t in range(3):
        s_down[:, cols(k * W3 + t * 128, 128)] = fin_d[t, my96, :]
        s_down[:, cols(far * W3 + t * 128, 128)] = rx_d[t]
    for c in cN:
        c.wait_recv()
    msum = jnp.zeros((8, 128), f32)
    for mm in range(8):
        val = tile[1]
        for j in range(7):
            val = jnp.where((p.m + 7 - j) % 8 == mm, nb2[j], val)
        msum = msum + val
    total[...] = msum
    for c in sent:
        c.wait_send()


def reduce_gradients(gqkv, gwo, gwi, gw2, gvt):
    scratch = []
    for count, rows, w in ((8, D, W3), (3, FF, 128), (0, D, 128)):
        lead = (count,) if count else ()
        scratch += [
            pltpu.VMEM(lead + (rows, w), bf), pltpu.VMEM(lead + (rows, w), bf), pltpu.VMEM(lead + (2, rows // 4, w), bf),
            pltpu.VMEM(lead + (rows // 4, w), bf), pltpu.VMEM(lead + (3, rows // 16, w), bf),
        ]
    scratch += [
        pltpu.VMEM((8, 48, W3), f32), pltpu.VMEM((3, 192, 128), f32), pltpu.VMEM((8, 24, W3), f32), pltpu.VMEM((3, 96, 128), f32),
        pltpu.VMEM((2, 8, 128), f32), pltpu.VMEM((3, 8, 128), f32), pltpu.VMEM((7, 8, 128), f32),
        pltpu.SemaphoreType.DMA((12, 7)), pltpu.SemaphoreType.DMA((12, 7)), pltpu.SemaphoreType.DMA((12,)),
        pltpu.SemaphoreType.DMA((11,)), pltpu.SemaphoreType.DMA((11,)), pltpu.SemaphoreType.DMA((10,)), pltpu.SemaphoreType.DMA((10,)),
    ]
    return pl.pallas_call(
        reduce_kernel,
        in_specs=[ANY] * 5,
        out_specs=[VM] * 6,
        out_shape=[
            S((3, 24, D), f32), S((24, D), f32), S((24, FF), f32), S((96, D), f32), S((24, 128), f32), S((8, 128), f32),
        ],
        scratch_shapes=scratch,
        compiler_params=pltpu.CompilerParams(collective_id=1, has_side_effects=True, vmem_limit_bytes=56 * MIB),
        name="reduce_gradients",
    )(gqkv, gwo, gwi, gw2, gvt)


def adam_step(weight, gradient, first_old, second_old, decay_rate, step_rate):
    first_new = moment_decay * first_old + (1.0 - moment_decay) * gradient
    second_new = square_decay * second_old + (1.0 - square_decay) * gradient * gradient
    first_hat = first_new / (1.0 - moment_decay**STEP)
    second_hat = second_new / (1.0 - square_decay**STEP)
    weight_new = weight - step_rate * (first_hat / (jnp.sqrt(second_hat) + adam_epsilon) + decay_rate * weight)
    return (weight_new, first_new, second_new)


def update_kernel(total, *refs):
    w, g, m, u = refs[0:5], refs[5:10], refs[10:15], refs[15:20]
    norm_o, new, first, second = refs[20], refs[21:26], refs[26:31], refs[31:36]
    norm = jnp.sqrt(total[...])
    norm_o[...] = norm
    factor = jnp.minimum(1.0, clip_limit / (norm + 1e-06))[0:1, 0:1]
    for i in range(4):
        n, f, s = adam_step(w[i][...], factor * g[i][...], m[i][...], u[i][...], weight_decay, learn_rate)
        new[i][...] = n
        first[i][...] = f
        second[i][...] = s
    wide = jnp.concatenate([g[4][...], jnp.zeros((104, 128), f32)], axis=0).T[:12, :24]
    n, f, s = adam_step(w[4][...], factor * wide, m[4][...], u[4][...], 0.0, vector_rate)
    new[4][...] = n
    first[4][...] = f
    second[4][...] = s


def update(total, weights, grads, firsts, seconds):
    shapes = [S(w.shape, f32) for w in weights]
    return pl.pallas_call(
        update_kernel,
        in_specs=[VM] * 21,
        out_specs=[VM] * 16,
        out_shape=[S((8, 128), f32)] + shapes * 3,
        compiler_params=pltpu.CompilerParams(vmem_limit_bytes=40 * MIB),
        name="clip_and_update",
    )(total, *weights, *grads, *firsts, *seconds)


def segment_ids(lengths):
    bounds = jnp.cumsum(lengths, axis=-1)
    places = jnp.arange(T, dtype=jnp.int32)
    return jnp.sum((places[:, None] >= bounds[None, :]).astype(jnp.int32), axis=-1)


def pairs_last(a):
    return a.reshape(3, D, PAIRS, 128).transpose(1, 2, 0, 3).reshape(D, 3 * D)


def per_device(
    small, tokens, cotangent, lengths, qkv_weight, out_weight, in_weight, down_weight, vectors,
    qkv_first, out_first, in_first, down_first, vec_first, qkv_second, out_second, in_second, down_second, vec_second,
):
    weights = (qkv_weight, out_weight, in_weight, down_weight, vectors)
    firsts = (qkv_first, out_first, in_first, down_first, vec_first)
    seconds = (qkv_second, out_second, in_second, down_second, vec_second)
    axes = ("dp", "fsdp")
    if small:
        wqkv, wo, wi, w2, vt = gather_weights(*weights)
        vec = vt[:, :16].astype(f32).T
    else:
        gather = lambda a, axis: lax.all_gather(a.astype(bf), axes, axis=axis, tiled=True)
        wqkv = pairs_last(gather(qkv_weight, 1))
        wo, wi, w2 = gather(out_weight, 0), gather(in_weight, 0), gather(down_weight, 0)
        vec = jnp.concatenate([gather(vectors, 1).astype(f32), jnp.zeros((4, D), f32)], axis=0)
    bias = jnp.stack([vec[0], jnp.zeros_like(vec[0]), vec[1]]).reshape(3, PAIRS, 128).transpose(1, 0, 2).reshape(1, 3 * D)
    seg = segment_ids(lengths[0])
    lane = jnp.arange(128)
    match = seg[:, None] == lane[None, :]
    onehot = match.astype(bf)
    neg = jnp.where(match | (lane >= lengths.shape[1])[None, :], 0.0, -1e30).astype(bf)
    q, k, v, ctx, lse = attend(tokens, wqkv, bias, onehot, neg)
    result, dh1, dctx, vg, gwo, gwi, gw2 = feed_forward(tokens, ctx, cotangent, vec, wo, wi, w2)
    gqkv, input_grad, vg_qv = attend_back(tokens, wqkv, dh1, q, k, v, dctx, ctx, lse, onehot, neg)
    vg = vg + vg_qv
    if small:
        gvt = jnp.concatenate([vg.T.astype(bf), jnp.zeros((D, 112), bf)], axis=1)
        *grads, total = reduce_gradients(gqkv, gwo, gwi, gw2, gvt)
        updated = update(total, weights, grads, firsts, seconds)
        return (result, input_grad, updated[0][0, 0], *updated[1:])
    scatter = lambda a, axis: lax.psum_scatter(a.astype(f32), axes, scatter_dimension=axis, tiled=True)
    gqkv = gqkv.reshape(D, PAIRS, 3, 128).transpose(2, 0, 1, 3).reshape(3, D, D)
    grads = (scatter(gqkv, 1), scatter(gwo, 0), scatter(gwi, 0), scatter(gw2, 0), scatter(vg[:12], 1))
    grad_norm = jnp.sqrt(lax.psum(sum(jnp.sum(g * g) for g in grads), axes))
    factor = jnp.minimum(1.0, clip_limit / (grad_norm + 1e-06))
    updated = []
    for i in range(5):
        rates = (0.0, vector_rate) if i == 4 else (weight_decay, learn_rate)
        updated.append(adam_step(weights[i], factor * grads[i], firsts[i], seconds[i], *rates))
    return (result, input_grad, grad_norm, *[u[j] for j in range(3) for u in updated])


def solution(mesh):
    rows = P(("dp", "fsdp"), None)
    deep = P(None, ("dp", "fsdp"), None)
    wide = P(None, ("dp", "fsdp"))
    group = (deep, rows, rows, rows, wide)
    small = mesh.shape["dp"] == 4 and mesh.shape["fsdp"] == 8
    return jax.shard_map(
        functools.partial(per_device, small),
        mesh=mesh,
        in_specs=(rows, rows, rows) + group * 3,
        out_specs=(rows, rows, P()) + group * 3,
        check_vma=False,
    )
```

```python
import functools

import jax
import jax.numpy as jnp
from jax import lax
from jax.experimental import pallas as pl
from jax.experimental.pallas import tpu as pltpu
from jax.sharding import PartitionSpec as P

D = 768
H = 12
HD = 64
FF = 3072
T = 1024
STEP = 10
PAIRS = H // 2
W3 = 384

moment_decay = 0.9
square_decay = 0.999
learn_rate = 0.02
vector_rate = 0.15
weight_decay = 0.01
adam_epsilon = 1e-08
clip_limit = 1.0
norm_epsilon = 1e-05

bf = jnp.bfloat16
f32 = jnp.float32
MESH = pl.DeviceIdType.MESH
VM = pl.BlockSpec(memory_space=pltpu.VMEM)
ANY = pl.BlockSpec(memory_space=pl.ANY)
MIB = 2**20


def S(shape, dtype):
    return jax.ShapeDtypeStruct(shape, dtype)


def nn(a, b):
    return lax.dot_general(a, b, (((1,), (0,)), ((), ())), preferred_element_type=f32)


def nt(a, b):
    return lax.dot_general(a, b, (((1,), (1,)), ((), ())), preferred_element_type=f32)


def tn(a, b):
    return lax.dot_general(a, b, (((0,), (0,)), ((), ())), preferred_element_type=f32)


def colsum(x):
    return jnp.sum(x, axis=0, keepdims=True)


class Place:
    def __init__(self):
        self.dp = lax.axis_index("dp")
        self.fs = lax.axis_index("fsdp")
        self.z = self.fs // 2
        self.k = self.fs % 2
        dp, k = self.dp, self.k
        xn = dp + 1 - 2 * (dp % 2)
        yn = (dp + 2) % 4
        self.dp1 = xn * (1 - k) + yn * k
        self.dp2 = yn * (1 - k) + xn * k
        self.dp3 = 3 - dp
        self.n1 = (self.dp1, self.fs)
        self.n2 = (self.dp2, self.fs)
        self.sib = (dp, self.z * 2 + 1 - k)
        self.zp = [(dp, ((self.z + i) % 4) * 2 + k) for i in (1, 2, 3)]
        self.m = dp * 2 + k
        self.others = []
        for j in range(1, 8):
            other = (self.m + j) % 8
            self.others.append((other // 2, self.z * 2 + other % 2))


def enter(peers):
    barrier = pltpu.get_barrier_semaphore()
    for peer in peers:
        pl.semaphore_signal(barrier, inc=1, device_id=peer, device_id_type=MESH)
    pl.semaphore_wait(barrier, len(peers))


def rcopy(src, dst, ssem, rsem, peer):
    return pltpu.make_async_remote_copy(src, dst, ssem, rsem, device_id=peer, device_id_type=MESH)


def half(w, c):
    return pl.ds(pl.multiple_of(c * w, 128), w)


def band(rows, index):
    return pl.ds(pl.multiple_of(rows * index, 16), rows)


class Gather:
    def __init__(self, p, chunks, gs, gr):
        self.p, self.chunks, self.gs, self.gr = p, chunks, gs, gr
        self.sent = []

    def go(self, part, j, rows, peer):
        n, ref, rc, cols, swap = part
        view = ref.at[rows, cols]
        c = rcopy(view, view, self.gs.at[n, j], self.gr.at[n, j], peer)
        c.start()
        self.sent.append(c)
        return c

    def first(self, i):
        p = self.p
        out = []
        for part in self.chunks[i]:
            rc = part[2]
            out.append([self.go(part, j, band(rc, p.dp * 4 + p.z), p.zp[j]) for j in range(3)])
        return out

    def slots(self, ahead):
        p, n = self.p, len(self.chunks)
        zc, c1, c2, c3, c4 = {}, {}, {}, {}, {}
        for i in range(min(ahead, n)):
            zc[i] = self.first(i)
        yield -1
        for s in range(1, n + 4):
            i = s - 1 + ahead
            if i < n:
                zc[i] = self.first(i)
            i = s - 1
            if 0 <= i < n:
                c1[i], c2[i] = [], []
                for q, part in enumerate(self.chunks[i]):
                    for c in zc[i][q]:
                        c.wait_recv()
                    c1[i].append(self.go(part, 3, band(4 * part[2], p.dp), p.n1))
                    c2[i].append(self.go(part, 4, band(4 * part[2], p.dp), p.n2))
            i = s - 2
            if 0 <= i < n:
                c3[i] = []
                for q, part in enumerate(self.chunks[i]):
                    c1[i][q].wait_recv()
                    c3[i].append(self.go(part, 5, band(4 * part[2], p.dp1), p.n2))
            i = s - 3
            if 0 <= i < n:
                c4[i] = []
                for q, part in enumerate(self.chunks[i]):
                    c2[i][q].wait_recv()
                    c3[i][q].wait_recv()
                    if part[4]:
                        c4[i].append(self.go(part, 6, pl.ds(0, 16 * part[2]), p.sib))
            i = s - 4
            if 0 <= i < n:
                for c in c4[i]:
                    c.wait_recv()
            yield s - 4
        for c in self.sent:
            c.wait_send()
        yield n


def forward_kernel(
    block, tok_h, onehot, neg, qkv, out, inw, down, vec,
    wqkv_h, wo, wi, w2, vrow, q_h, k_h, v_h, ctx_h, lse,
    tok, wq, vt, qs_, ks_, vs_, ctx, qa, ka, va,
    m_qkv, m_out, m_in, m_down, m_vec, x_qkv, x_out, x_in, x_down, x_vec, myvec,
    own_out, own_in, own_down, xs, xr, gs, gr, ls, os,
):
    p = Place()
    k = p.k
    far = 1 - k
    loads = [
        pltpu.make_async_copy(vec, m_vec, ls.at[4]),
        pltpu.make_async_copy(qkv.at[:, :, half(W3, k)], m_qkv, ls.at[0]),
        pltpu.make_async_copy(out.at[:, half(W3, k)], m_out, ls.at[1]),
        pltpu.make_async_copy(inw.at[:, half(4 * W3, k)], m_in, ls.at[2]),
        pltpu.make_async_copy(down.at[:, half(W3, k)], m_down, ls.at[3]),
        pltpu.make_async_copy(tok_h, tok, ls.at[5]),
    ]
    for c in loads:
        c.start()
    enter([p.sib, p.n1, p.n2] + p.zp)
    swaps = [
        rcopy(qkv.at[:, :, half(W3, far)], x_qkv, xs.at[0], xr.at[0], p.sib),
        rcopy(out.at[:, half(W3, far)], x_out, xs.at[1], xr.at[1], p.sib),
        rcopy(inw.at[:, half(4 * W3, far)], x_in, xs.at[2], xr.at[2], p.sib),
        rcopy(down.at[:, half(W3, far)], x_down, xs.at[3], xr.at[3], p.sib),
        rcopy(myvec, x_vec, xs.at[4], xr.at[4], p.sib),
    ]
    for c in swaps[:4]:
        c.start()
    loads[0].wait()
    pad = jnp.concatenate([m_vec[...], jnp.zeros((128 - 12, 24), f32)], axis=0)
    myvec[...] = jnp.concatenate([pad, jnp.zeros((128, 104), f32)], axis=1).T[:24, :]
    swaps[4].start()

    def both(mine, other):
        lo = jnp.where(k == 0, mine, other)
        hi = jnp.where(k == 0, other, mine)
        return jnp.concatenate([lo, hi], axis=0).astype(bf)

    chip = p.dp * 4 + p.z
    loads[1].wait()
    swaps[0].wait_recv()
    for j in range(3):
        mat = both(m_qkv[j], x_qkv[j])
        for t in range(3):
            wq[band(48, chip), pl.ds(pl.multiple_of((3 * k + t) * W3 + j * 128, 128), 128)] = mat[:, t * 128 : (t + 1) * 128]
    swaps[4].wait_recv()
    vt[band(48, chip), :] = both(myvec[...], x_vec[...])

    chunks = []
    for t in range(3):
        chunks.append([(len(chunks), wq, 48, half(W3, t + 3 * k), True)])
    chunks.append([(len(chunks), wo, 48, half(W3, k), True)])
    for t in range(4):
        chunks.append([(len(chunks), wi, 48, half(W3, t + 4 * k), True)])
    for t in range(3):
        chunks.append([(len(chunks), w2, 192, half(128, 3 * k + t), True)])
    chunks[0].append((11, vt, 48, pl.ds(0, 128), False))
    gather = Gather(p, chunks, gs, gr)
    slots = gather.slots(3)
    done = [next(slots)]
    for i in range(3):
        loads[2 + i].wait()
        swaps[1 + i].wait_recv()
    own_out[...] = both(m_out[...], x_out[...])
    own_in[...] = both(m_in[...], x_in[...])
    own_down[...] = both(m_down[...], x_down[...])
    local = [
        pltpu.make_async_copy(own_out, wo.at[band(48, chip), half(W3, k)], ls.at[1]),
        pltpu.make_async_copy(own_in, wi.at[band(48, chip), half(4 * W3, k)], ls.at[2]),
        pltpu.make_async_copy(own_down, w2.at[band(192, chip), half(W3, k)], ls.at[3]),
    ]
    for c in local:
        c.start()
    for c in local:
        c.wait()
    loads[5].wait()

    def upto(i):
        while done[0] < i:
            done[0] = next(slots)

    upto(0)
    vrow[...] = vt[...].astype(f32).T
    lane = lax.broadcasted_iota(jnp.int32, (1, 128), 1)
    ka[:, 128:] = neg[...]
    va[:, 128:] = jnp.ones((T, 128), bf)
    qa[:, 128:] = onehot[...]
    outs = []
    count = 0
    for turn, pair in enumerate((0, 3, 1, 4, 2, 5)):
        upto(turn // 2)
        cs = slice(pair * 128, (pair + 1) * 128)
        y = nn(tok[...], wq[:, pair * W3 : (pair + 1) * W3])
        q = (y[:, :128] + vrow[0:1, cs]).astype(bf)
        key = y[:, 128:256].astype(bf)
        val = (y[:, 256:] + vrow[1:2, cs]).astype(bf)
        qs_[:, cs] = q
        ks_[:, cs] = key
        vs_[:, cs] = val
        for n, (src, dst) in enumerate(((qs_, q_h), (ks_, k_h), (vs_, v_h))):
            outs.append(pltpu.make_async_copy(src.at[:, cs], dst.at[:, cs], os.at[n, pair]))
            outs[-1].start()
        qs = (q.astype(f32) * HD ** (-0.5)).astype(bf)
        ka[:, :128] = key
        va[:, :128] = val
        for h in range(2):
            sel = (lane // 64) == h
            qa[:, :128] = jnp.where(sel, qs, jnp.zeros_like(qs))
            for b in range(T // block):
                r = slice(b * block, (b + 1) * block)
                s = nt(qa[r, :], ka[...])
                m = jnp.max(s, axis=1, keepdims=True)
                e = jnp.exp(s - m).astype(bf)
                o = nn(e, va[...])
                tot = o[:, 128:]
                c = o[:, :128] / tot
                l = m + jnp.log(tot)
                ctx[r, cs] = c if h == 0 else jnp.where(sel, c, ctx[r, cs])
                lse[r, :] = l if turn + h == 0 else jnp.where(lane == 2 * pair + h, l, lse[r, :])
                count += 1
                if count % 4 == 0 and done[0] < len(chunks) - 1:
                    done[0] = next(slots)
        outs.append(pltpu.make_async_copy(ctx.at[:, cs], ctx_h.at[:, cs], os.at[3, pair]))
        outs[-1].start()
    outs.append(pltpu.make_async_copy(wq, wqkv_h, ls.at[0]))
    outs[-1].start()
    for c in slots:
        pass
    for c in swaps:
        c.wait_send()
    for c in outs:
        c.wait()


def forward(tok, onehot, neg, weights, block=256):
    vb = lambda *shape: pltpu.VMEM(shape, bf)
    vf = lambda *shape: pltpu.VMEM(shape, f32)
    dma = lambda *shape: pltpu.SemaphoreType.DMA(shape)
    return pl.pallas_call(
        functools.partial(forward_kernel, block),
        in_specs=[ANY, VM, VM] + [ANY] * 5,
        out_specs=[ANY] * 4 + [VM] + [ANY] * 4 + [VM],
        out_shape=[S((D, 3 * D), bf), S((D, D), bf), S((D, FF), bf), S((FF, D), bf), S((128, D), f32)]
        + [S((T, D), bf)] * 3 + [S((T, D), f32), S((T, 128), f32)],
        scratch_shapes=[
            vb(T, D), vb(D, 3 * D), vb(D, 128), vb(T, D), vb(T, D), vb(T, D), vf(T, D), vb(T, 256), vb(T, 256), vb(T, 256),
            vf(3, 24, W3), vf(24, W3), vf(24, 4 * W3), vf(96, W3), vf(12, 24),
            vf(3, 24, W3), vf(24, W3), vf(24, 4 * W3), vf(96, W3), vf(24, 128), vf(24, 128),
            vb(48, W3), vb(48, 4 * W3), vb(192, W3),
            dma(5), dma(5), dma(12, 7), dma(12, 7), dma(6), dma(4, 6),
        ],
        compiler_params=pltpu.CompilerParams(collective_id=0, has_side_effects=True, vmem_limit_bytes=60 * MIB),
        name="forward",
    )(tok, onehot, neg, *weights)


def attend_kernel(block, tok, w, bias, onehot, neg, q_o, k_o, v_o, ctx_o, lse_o, qa, ka, va):
    lane = lax.broadcasted_iota(jnp.int32, (1, 128), 1)
    pair = pl.program_id(0)
    y = nn(tok[...], w[...]) + bias[...]
    q = y[:, :128].astype(bf)
    key = y[:, 128:256].astype(bf)
    val = y[:, 256:].astype(bf)
    q_o[...] = q
    k_o[...] = key
    v_o[...] = val
    qs = (q.astype(f32) * HD ** (-0.5)).astype(bf)
    ka[:, :128] = key
    ka[:, 128:] = neg[...]
    va[:, :128] = val
    va[:, 128:] = jnp.ones((T, 128), bf)
    qa[:, 128:] = onehot[...]
    for h in range(2):
        sel = (lane // 64) == h
        qa[:, :128] = jnp.where(sel, qs, jnp.zeros_like(qs))
        for b in range(T // block):
            r = slice(b * block, (b + 1) * block)
            s = nt(qa[r, :], ka[...])
            m = jnp.max(s, axis=1, keepdims=True)
            e = jnp.exp(s - m).astype(bf)
            o = nn(e, va[...])
            tot = o[:, 128:]
            c = o[:, :128] / tot
            l = m + jnp.log(tot)
            ctx_o[r, :] = c if h == 0 else jnp.where(sel, c, ctx_o[r, :])
            lse_o[r, :] = jnp.where(lane == 2 * pair + h, l, lse_o[r, :])


def attend(tok, w, bias, onehot, neg, block=256):
    full = lambda s: pl.BlockSpec(s, lambda i: (0,) * len(s))
    col = pl.BlockSpec((T, 128), lambda i: (0, i))
    return pl.pallas_call(
        functools.partial(attend_kernel, block),
        grid=(PAIRS,),
        in_specs=[
            full((T, D)), pl.BlockSpec((D, W3), lambda i: (0, i)), pl.BlockSpec((1, W3), lambda i: (0, i)),
            full((T, 128)), full((T, 128)),
        ],
        out_specs=[col, col, col, col, full((T, 128))],
        out_shape=[S((T, D), bf)] * 3 + [S((T, D), f32), S((T, 128), f32)],
        scratch_shapes=[pltpu.VMEM((T, 256), bf)] * 3,
        compiler_params=pltpu.CompilerParams(vmem_limit_bytes=60 * MIB),
        name="attend",
    )(tok, w, bias, onehot, neg)


def split3(x):
    hi = x.astype(bf).astype(f32)
    mid = (x - hi).astype(bf).astype(f32)
    return hi, mid, x - hi - mid


class Back:
    def __init__(self, block, onehot, neg, qa, ka, va, da, kT, dqT, dka, dva):
        self.block, self.onehot, self.neg = block, onehot, neg
        self.refs = (qa, ka, va, da, kT, dqT, dka, dva)
        self.lane = lax.broadcasted_iota(jnp.int32, (1, 128), 1)

    def start(self):
        qa, ka, va, da, kT, dqT, dka, dva = self.refs
        minus = jnp.where((self.lane >= 16) & (self.lane < 19), -1.0, 0.0)
        ka[:, 128:] = (self.neg[...].astype(f32) + minus).astype(bf)
        va[:, 128:] = jnp.broadcast_to(minus, (T, 128)).astype(bf)

    def pair(self, pair, q, key, val, d, ctx, lse, tick):
        lane, block = self.lane, self.block
        qa, ka, va, da, kT, dqT, dka, dva = self.refs
        qs = (q.astype(f32) * HD ** (-0.5)).astype(bf)
        ka[:, :128] = key
        va[:, :128] = val
        kT[...] = key.T
        prod = d.astype(f32) * ctx

        def extra(base, parts):
            for j, part in enumerate(parts):
                base = jnp.where(lane == 16 + j, part, base)
            return base.astype(bf)

        for h in range(2):
            sel = (lane // 64) == h
            inner = jnp.sum(jnp.where(sel, prod, 0.0), axis=1, keepdims=True)
            lsum = jnp.sum(jnp.where(lane == 2 * pair + h, lse, 0.0), axis=1, keepdims=True)
            qa[:, :128] = jnp.where(sel, qs, jnp.zeros_like(qs))
            qa[:, 128:] = extra(self.onehot[...].astype(f32), split3(lsum))
            da[:, :128] = jnp.where(sel, d, jnp.zeros_like(d))
            da[:, 128:] = extra(jnp.zeros((T, 128), f32), split3(inner))
            for b in range(T // block):
                r = slice(b * block, (b + 1) * block)
                pt = jnp.exp(nt(ka[...], qa[r, :]))
                dpt = nt(va[...], da[r, :])
                ds = (pt * dpt).astype(bf)
                x = nn(pt.astype(bf), da[r, :128])
                y = nn(ds, qa[r, :128])
                dqT[h * 64 : (h + 1) * 64, r] = nn(kT[h * 64 : (h + 1) * 64, :], ds)
                if h == 0 and b == 0:
                    dva[...] = x
                    dka[...] = y
                else:
                    dva[...] += x
                    dka[...] += y
                tick()
        dv = dva[...].astype(bf)
        dk = dka[...].astype(bf)
        dq = (dqT[...].T * HD ** (-0.5)).astype(bf)
        return dq, dk, dv


BACK_SCRATCH = (
    [pltpu.VMEM((T, 256), bf)] * 4 + [pltpu.VMEM((128, T), bf), pltpu.VMEM((128, T), f32)] + [pltpu.VMEM((T, 128), f32)] * 2
)


def attend_back_kernel(
    block, tok, w, dh1, q_i, k_i, v_i, dctx_i, ctx_i, lse, onehot, neg, g_o, ig_o, vg_o, *scratch,
):
    tokT, ig = scratch[-2:]
    step = pl.program_id(0)
    back = Back(block, onehot, neg, *scratch[:-2])

    @pl.when(step == 0)
    def _():
        tokT[...] = tok[...].T
        ig[...] = dh1[...]

    back.start()
    dq, dk, dv = back.pair(step, q_i[...], k_i[...], v_i[...], dctx_i[...], ctx_i[...], lse[...], lambda: None)
    vg_o[...] = jnp.zeros_like(vg_o)
    vg_o[0:1, :] = colsum(dq.astype(f32))
    vg_o[1:2, :] = colsum(dv.astype(f32))
    cat = jnp.concatenate([dq, dk, dv], axis=1)
    g_o[...] = nn(tokT[...], cat).astype(bf)
    ig[...] += nt(cat, w[...])

    @pl.when(step == PAIRS - 1)
    def _():
        ig_o[...] = ig[...].astype(bf)


def attend_back(tok, w, dh1, q, k, v, dctx, ctx, lse, onehot, neg, block=512):
    full = lambda s: pl.BlockSpec(s, lambda i: (0,) * len(s))
    col = pl.BlockSpec((T, 128), lambda i: (0, i))
    return pl.pallas_call(
        functools.partial(attend_back_kernel, block),
        grid=(PAIRS,),
        in_specs=[
            full((T, D)), pl.BlockSpec((D, W3), lambda i: (0, i)), full((T, D)),
            col, col, col, col, col, full((T, 128)), full((T, 128)), full((T, 128)),
        ],
        out_specs=[pl.BlockSpec((D, W3), lambda i: (0, i)), full((T, D)), pl.BlockSpec((16, 128), lambda i: (0, i))],
        out_shape=[S((D, 3 * D), bf), S((T, D), bf), S((16, D), f32)],
        scratch_shapes=BACK_SCRATCH + [pltpu.VMEM((D, T), bf), pltpu.VMEM((T, D), f32)],
        compiler_params=pltpu.CompilerParams(vmem_limit_bytes=60 * MIB),
        name="attend_back",
    )(tok, w, dh1, q, k, v, dctx, ctx, lse, onehot, neg)


def fold(x):
    rows, width = x.shape
    x = x * x
    tot = jnp.zeros((8, 128), f32)
    for i in range(rows // 8):
        for j in range(width // 128):
            tot = tot + x[i * 8 : (i + 1) * 8, j * 128 : (j + 1) * 128]
    return tot


def add_rows(dst, row0, src, rows):
    step = 96 if rows % 96 == 0 else rows

    def body(i, carry):
        d = pl.ds(pl.multiple_of(row0 + i * step, 16), step)
        s = pl.ds(pl.multiple_of(i * step, 16), step)
        dst[d, :] = (dst[d, :].astype(f32) + src[s, :].astype(f32)).astype(bf)
        return carry

    lax.fori_loop(0, rows // step, body, 0)


OFF = (2, 4, 6)


class Reduce:
    def __init__(self, p, gs, gr, s_vec):
        self.p, self.gs, self.gr, self.s_vec = p, gs, gr, s_vec
        self.sent = []
        self.squares = jnp.zeros((8, 128), f32)

    def go(self, src, dst, n, j, peer):
        c = rcopy(src, dst, self.gs.at[n, j], self.gr.at[n, j], peer)
        c.start()
        self.sent.append(c)
        return c

    def go_x(self, src, dst, ssem, rsem, peer):
        c = rcopy(src, dst, ssem, rsem, peer)
        c.start()
        self.sent.append(c)
        return c

    def send_first(self, part):
        n, rc, acc, give, ready, rs, r2, r1, rz, fin = part
        return self.go(give, rs, n, 0, self.p.sib)

    def slots(self, chunks, issue):
        p, n = self.p, len(chunks)
        cS, cP, cQ, cZ = {}, {}, {}, {}
        for s in range(n + OFF[2]):
            i = s
            if i < n:
                cP[i] = []
                for part, first in zip(chunks[i], issue(i)):
                    num, rc, acc, give, ready, rs, r2, r1, rz, fin = part
                    if ready is not None:
                        ready.wait()
                    first.wait_recv()
                    add_rows(acc, 0, rs, 16 * rc)
                    cP[i].append((
                        self.go(acc.at[band(4 * rc, p.dp2), :], r2.at[0], num, 1, p.n2),
                        self.go(acc.at[band(4 * rc, p.dp3), :], r2.at[1], num, 2, p.n2),
                    ))
            i = s - OFF[0]
            if 0 <= i < n:
                cQ[i] = []
                for part, (near, cross) in zip(chunks[i], cP[i]):
                    num, rc, acc, give, ready, rs, r2, r1, rz, fin = part
                    cross.wait_recv()
                    add_rows(acc, p.dp1 * 4 * rc, r2.at[1], 4 * rc)
                    cQ[i].append(self.go(acc.at[band(4 * rc, p.dp1), :], r1, num, 3, p.n1))
                    near.wait_recv()
                    add_rows(acc, p.dp * 4 * rc, r2.at[0], 4 * rc)
            i = s - OFF[1]
            if 0 <= i < n:
                cZ[i] = []
                for part, q in zip(chunks[i], cQ[i]):
                    num, rc, acc, give, ready, rs, r2, r1, rz, fin = part
                    q.wait_recv()
                    add_rows(acc, p.dp * 4 * rc, r1, 4 * rc)
                    cZ[i].append([
                        self.go(acc.at[band(rc, p.dp * 4 + (p.z + j + 1) % 4), :], rz.at[j], num, 4 + j, p.zp[j]) for j in range(3)
                    ])
            i = s - OFF[2]
            if 0 <= i < n:
                for part, zs in zip(chunks[i], cZ[i]):
                    num, rc, acc, give, ready, rs, r2, r1, rz, fin = part
                    for c in zs:
                        c.wait_recv()
                    own = acc[band(rc, p.dp * 4 + p.z), :].astype(f32)
                    for j in range(3):
                        own = own + rz[j].astype(f32)
                    if fin is None:
                        own = jnp.where(p.k == 0, own[:24], own[24:])
                        self.s_vec[...] = own
                    else:
                        fin[...] = own
                    self.squares = self.squares + fold(own)
            yield s + 1


def backward_kernel(
    block, tok_h, wqkv_h, dh1_h, q_h, k_h, v_h, dctx_h, ctx_h, lse, onehot, neg, vg_i, gwo, gwi, gw2,
    ig_h, s_qkv, s_out, s_in, s_down, s_vec, total,
    tok, wq, ig, q, k_, v, dctx, ctx, gq, gvt, vg,
    qa, ka, va, da, kT, dqT, dka, dva, tokT,
    acc_a, rs_a, r2_a, r1_a, rz_a, acc_d, rs_d, r2_d, r1_d, rz_d, acc_v, rs_v, r2_v, r1_v, rz_v,
    fin_a, fin_d, rx_a, rx_d, tile, nb1, nb2, gs, gr, ls, xs, xr, ns, nr, ps, ts,
):
    p = Place()
    k = p.k
    far = 1 - k
    order = (0, 3, 1, 4, 2, 5)
    cols = lambda pair: slice(pair * 128, (pair + 1) * 128)
    early = [pltpu.make_async_copy(tok_h, tok, ts.at[0])]
    pairs = {}
    for pair in order:
        moves = ((q_h, q), (k_h, k_), (v_h, v), (dctx_h, dctx), (ctx_h, ctx))
        pairs[pair] = [
            pltpu.make_async_copy(src.at[:, cols(pair)], dst.at[:, cols(pair)], ps.at[n, pair]) for n, (src, dst) in enumerate(moves)
        ]
    late = [pltpu.make_async_copy(wqkv_h, wq, ts.at[1]), pltpu.make_async_copy(dh1_h, ig, ts.at[2])]
    for c in early + pairs[0] + pairs[3]:
        c.start()
    enter(p.others + p.zp)
    red = Reduce(p, gs, gr, s_vec)

    chunks = []
    for t in range(3):
        load = pltpu.make_async_copy(gw2.at[:, half(128, 3 * k + t)], acc_d.at[t], ls.at[t])
        load.start()
        chunks.append([(
            t, 192, acc_d.at[t], gw2.at[:, half(128, 3 * far + t)], load, rs_d.at[t], r2_d.at[t], r1_d.at[t], rz_d.at[t], fin_d.at[t],
        )])
    spots = lambda a: (rs_a.at[a], r2_a.at[a], r1_a.at[a], rz_a.at[a], fin_a.at[a])
    for t in range(5):
        ref, start = (gwi, lambda c: t + 4 * c) if t < 4 else (gwo, lambda c: c)
        load = pltpu.make_async_copy(ref.at[:, half(W3, start(k))], acc_a.at[t], ls.at[3 + t])
        load.start()
        chunks.append([(3 + t, 48, acc_a.at[t], ref.at[:, half(W3, start(far))], load) + spots(t)])
    firsts = {i: [red.send_first(part) for part in chunks[i]] for i in range(8)}
    for t in range(3):
        chunks.append([(8 + t, 48, gq.at[t, k], gq.at[t, far], None) + spots(5 + t)])
    chunks[10].append((11, 48, acc_v, gvt, None, rs_v, r2_v, r1_v, rz_v, None))
    sequence = (0, 1, 2, 3, 8, 4, 5, 6, 9, 7, 10)
    ordered = [chunks[i] for i in sequence]
    ready = set(range(8))

    def issue(s):
        assert sequence[s] in ready
        return firsts[sequence[s]]

    slots = red.slots(ordered, issue)
    place = [0]

    def step():
        place[0] = next(slots)

    for pair in order[2:]:
        for c in pairs[pair]:
            c.start()
    for c in late:
        c.start()
    early[0].wait()
    tokT[...] = tok[...].T
    back = Back(block, onehot, neg, qa, ka, va, da, kT, dqT, dka, dva)
    back.start()
    vg[...] = vg_i[...]
    ticks = [0]

    def tick():
        ticks[0] += 1
        if ticks[0] % 2 == 0 and place[0] < len(sequence) and sequence[place[0]] in ready:
            step()

    parts = {}
    for turn, pair in enumerate(order):
        cs = cols(pair)
        for c in pairs[pair]:
            c.wait()
        dq, dk, dv = back.pair(pair, q[:, cs], k_[:, cs], v[:, cs], dctx[:, cs], ctx[:, cs], lse[...], tick)
        q[:, cs] = dq
        k_[:, cs] = dk
        v[:, cs] = dv
        vg[0:1, cs] = colsum(dq.astype(f32))
        vg[1:2, cs] = colsum(dv.astype(f32))
        t, side = turn // 2, turn % 2
        for j, part in enumerate((dq, dk, dv)):
            gq[t, side, :, j * 128 : (j + 1) * 128] = nn(tokT[...], part).astype(bf)
        if side == 1:
            if t == 2:
                gvt[...] = jnp.concatenate([vg[...], jnp.zeros((112, D), f32)], axis=0).T.astype(bf)
                acc_v[...] = gvt[...]
            firsts[8 + t] = [red.send_first(part) for part in chunks[8 + t]]
            ready.add(8 + t)
    for c in late:
        c.wait()
    rows = [slice(b * 256, (b + 1) * 256) for b in range(4)]
    for r in rows:
        if place[0] < len(sequence) + OFF[2]:
            step()
        tot = ig[r, :]
        for pair in range(PAIRS):
            cs = cols(pair)
            cat = jnp.concatenate([q[r, cs], k_[r, cs], v[r, cs]], axis=1)
            tot = tot + nt(cat, wq[:, pair * W3 : (pair + 1) * W3])
        dctx[r, :] = tot.astype(bf)
    give = pltpu.make_async_copy(dctx, ig_h, ts.at[0])
    give.start()
    for c in slots:
        pass
    cX = []
    for a in range(8):
        cX.append(red.go_x(fin_a.at[a, pl.ds(pl.multiple_of(far * 24, 8), 24), :], rx_a.at[a], xs.at[a], xr.at[a], p.sib))
    for t in range(3):
        cX.append(red.go_x(fin_d.at[t, pl.ds(pl.multiple_of(far * 96, 8), 96), :], rx_d.at[t], xs.at[8 + t], xr.at[8 + t], p.sib))
    part = jnp.sum(jnp.sum(red.squares, axis=1, keepdims=True), axis=0, keepdims=True)
    tile[0] = jnp.broadcast_to(part, (8, 128))
    cN = [red.go_x(tile.at[0], nb1.at[j], ns.at[j], nr.at[j], p.zp[j]) for j in range(3)]
    for c in cN:
        c.wait_recv()
    zsum = jnp.zeros((8, 128), f32)
    for zz in range(4):
        term = tile[0]
        for j in range(3):
            term = jnp.where((p.z + 3 - j) % 4 == zz, nb1[j], term)
        zsum = zsum + term
    tile[1] = zsum
    cN = [red.go_x(tile.at[1], nb2.at[j], ns.at[3 + j], nr.at[3 + j], p.others[j]) for j in range(7)]
    my24 = pl.ds(pl.multiple_of(k * 24, 8), 24)
    my96 = pl.ds(pl.multiple_of(k * 96, 8), 96)
    for c in cX:
        c.wait_recv()
    for src, side in ((lambda a: fin_a[a, my24, :], k), (lambda a: rx_a[a], far)):
        for t in range(4):
            s_in[:, half(W3, t + 4 * side)] = src(t)
        s_out[:, half(W3, side)] = src(4)
        for t in range(3):
            term = src(5 + t)
            for j in range(3):
                s_qkv[j, :, half(128, 3 * side + t)] = term[:, j * 128 : (j + 1) * 128]
    for t in range(3):
        s_down[:, half(128, 3 * k + t)] = fin_d[t, my96, :]
        s_down[:, half(128, 3 * far + t)] = rx_d[t]
    for c in cN:
        c.wait_recv()
    msum = jnp.zeros((8, 128), f32)
    for mm in range(8):
        term = tile[1]
        for j in range(7):
            term = jnp.where((p.m + 7 - j) % 8 == mm, nb2[j], term)
        msum = msum + term
    total[...] = msum
    for c in red.sent:
        c.wait_send()
    give.wait()


def backward(tok, wqkv, dh1, q, k, v, dctx, ctx, lse, onehot, neg, vg, gwo, gwi, gw2, block=512):
    vb = lambda *shape: pltpu.VMEM(shape, bf)
    vf = lambda *shape: pltpu.VMEM(shape, f32)
    dma = lambda *shape: pltpu.SemaphoreType.DMA(shape)
    landing = lambda lead, rows, w: [
        vb(*lead, rows, w), vb(*lead, 2, rows // 4, w), vb(*lead, rows // 4, w), vb(*lead, 3, rows // 16, w)
    ]
    return pl.pallas_call(
        functools.partial(backward_kernel, block),
        in_specs=[ANY] * 8 + [VM] * 4 + [ANY] * 3,
        out_specs=[ANY] + [VM] * 6,
        out_shape=[
            S((T, D), bf), S((3, 24, D), f32), S((24, D), f32), S((24, FF), f32), S((96, D), f32), S((24, 128), f32), S((8, 128), f32),
        ],
        scratch_shapes=[
            vb(T, D), vb(D, 3 * D), vf(T, D), vb(T, D), vb(T, D), vb(T, D), vb(T, D), vf(T, D), vb(3, 2, D, W3), vb(D, 128), vf(16, D),
        ]
        + BACK_SCRATCH + [vb(D, T)]
        + [vb(5, D, W3)] + landing((8,), D, W3) + [vb(3, FF, 128)] + landing((3,), FF, 128) + [vb(D, 128)] + landing((), D, 128)
        + [
            vf(8, 48, W3), vf(3, 192, 128), vf(8, 24, W3), vf(3, 96, 128), vf(2, 8, 128), vf(3, 8, 128), vf(7, 8, 128),
            dma(12, 7), dma(12, 7), dma(8), dma(11), dma(11), dma(10), dma(10), dma(5, 6), dma(3),
        ],
        compiler_params=pltpu.CompilerParams(collective_id=1, has_side_effects=True, vmem_limit_bytes=62 * MIB),
        name="backward",
    )(tok, wqkv, dh1, q, k, v, dctx, ctx, lse, onehot, neg, vg, gwo, gwi, gw2)


def gelu_parts(x):
    e = jnp.exp(x * x * (-0.5))
    t = 1.0 / (1.0 + (0.3275911 * 0.7071067811865476) * jnp.abs(x))
    poly = 0.5 * 1.061405429
    for a in (-1.453152027, 1.421413741, -0.284496736, 0.254829592):
        poly = 0.5 * a + t * poly
    tail = t * poly * e
    return jnp.where(x >= 0, 1.0 - tail, tail), e * 0.3989422804014327


def norm_forward(h):
    c = h - jnp.mean(h, axis=1, keepdims=True)
    r = lax.rsqrt(jnp.mean(c * c, axis=1, keepdims=True) + norm_epsilon)
    return c * r, r


def norm_backward(dy, xh, r, g):
    dx = dy * g
    return r * (dx - jnp.mean(dx, axis=1, keepdims=True) - xh * jnp.mean(dx * xh, axis=1, keepdims=True))


def ffn_kernel(
    block, tok, ctx, cot, vec, wo_h, wi_h, w2_h, out_o, dh1_o, dctx_o, vg_o, gwo_h, gwi_h, gw2_h,
    wo, wi, w2, cb, x1b, hb, gp, dfb, dhp, dab, stage, tr, insem, outsem,
):
    loads = [
        pltpu.make_async_copy(wo_h, wo, insem.at[0]),
        pltpu.make_async_copy(wi_h, wi, insem.at[1]),
        pltpu.make_async_copy(w2_h, w2, insem.at[2]),
    ]
    for c in loads:
        c.start()
    vg_o[...] = jnp.zeros_like(vg_o)
    row = lambda i: vec[i : i + 1, :]
    for c in loads:
        c.wait()

    def one_block(b, carry):
        r = pl.ds(pl.multiple_of(b * block, block), block)
        c = ctx[r, :].astype(bf)
        cb[r, :] = c
        xh1, r1 = norm_forward(tok[r, :].astype(f32) + (nn(c, wo[...]) + row(2)))
        x1 = xh1 * row(4) + row(5)
        xb = x1.astype(bf)
        x1b[r, :] = xb
        acc = x1 + row(3)
        for j in range(4):
            cs = slice(j * D, (j + 1) * D)
            hp = nn(xb, wi[:, cs]) + row(8 + j)
            big, dense = gelu_parts(hp)
            h = (hp * big).astype(bf)
            hb[r, cs] = h
            gp[:, cs] = big + hp * dense
            acc = acc + nn(h, w2[cs, :])
        xh2, r2 = norm_forward(acc)
        out_o[r, :] = (xh2 * row(6) + row(7)).astype(bf)
        dy = cot[r, :].astype(f32)
        vg_o[6:7, :] += colsum(dy * xh2)
        vg_o[7:8, :] += colsum(dy)
        dh2 = norm_backward(dy, xh2, r2, row(6))
        df = dh2.astype(bf)
        dfb[r, :] = df
        vg_o[3:4, :] += colsum(df.astype(f32))
        dx1 = dh2
        for j in range(4):
            cs = slice(j * D, (j + 1) * D)
            dh = (gp[:, cs] * nt(df, w2[cs, :])).astype(bf)
            dhp[r, cs] = dh
            vg_o[8 + j : 9 + j, :] += colsum(dh.astype(f32))
            dx1 = dx1 + nt(dh, wi[:, cs])
        vg_o[4:5, :] += colsum(dx1 * xh1)
        vg_o[5:6, :] += colsum(dx1)
        dh1 = norm_backward(dx1, xh1, r1, row(4))
        dh1_o[r, :] = dh1
        da = dh1.astype(bf)
        dab[r, :] = da
        vg_o[2:3, :] += colsum(da.astype(f32))
        dctx_o[r, :] = nt(da, wo[...]).astype(bf)
        return carry

    lax.fori_loop(0, T // block, one_block, 0)
    outs = []

    def emit(val, dst):
        i = len(outs)
        if i >= 2:
            outs[i - 2].wait()
        stage[i % 2] = val.astype(bf)
        c = pltpu.make_async_copy(stage.at[i % 2], dst, outsem.at[i % 2])
        c.start()
        outs.append(c)

    for j in range(4):
        cs = slice(j * D, (j + 1) * D)
        emit(tn(hb[:, cs], dfb[...]), gw2_h.at[cs, :])
    tr[...] = x1b[...].T
    for j in range(4):
        cs = slice(j * D, (j + 1) * D)
        emit(nn(tr[...], dhp[:, cs]), gwi_h.at[:, cs])
    emit(tn(cb[...], dab[...]), gwo_h)
    outs[7].wait()
    outs[8].wait()


def feed_forward(tok, ctx, cot, vec, wo, wi, w2, block=256):
    return pl.pallas_call(
        functools.partial(ffn_kernel, block),
        in_specs=[VM] * 4 + [ANY] * 3,
        out_specs=[VM] * 4 + [ANY] * 3,
        out_shape=[
            S((T, D), bf), S((T, D), f32), S((T, D), bf), S((16, D), f32), S((D, D), bf), S((D, FF), bf), S((FF, D), bf),
        ],
        scratch_shapes=[
            pltpu.VMEM((D, D), bf), pltpu.VMEM((D, FF), bf), pltpu.VMEM((FF, D), bf), pltpu.VMEM((T, D), bf),
            pltpu.VMEM((T, D), bf), pltpu.VMEM((T, FF), bf), pltpu.VMEM((block, FF), f32), pltpu.VMEM((T, D), bf),
            pltpu.VMEM((T, FF), bf), pltpu.VMEM((T, D), bf), pltpu.VMEM((2, D, D), bf), pltpu.VMEM((D, T), bf),
            pltpu.SemaphoreType.DMA((3,)), pltpu.SemaphoreType.DMA((2,)),
        ],
        compiler_params=pltpu.CompilerParams(vmem_limit_bytes=60 * MIB),
        name="feed_forward",
    )(tok, ctx, cot, vec, wo, wi, w2)


def adam_step(weight, gradient, first_old, second_old, decay_rate, step_rate):
    first_new = moment_decay * first_old + (1.0 - moment_decay) * gradient
    second_new = square_decay * second_old + (1.0 - square_decay) * gradient * gradient
    first_hat = first_new / (1.0 - moment_decay**STEP)
    second_hat = second_new / (1.0 - square_decay**STEP)
    weight_new = weight - step_rate * (first_hat / (jnp.sqrt(second_hat) + adam_epsilon) + decay_rate * weight)
    return (weight_new, first_new, second_new)


def update_kernel(total, *refs):
    hbm, outs, scratch = refs[0:21], refs[21:38], refs[38:]
    bufs, sem = scratch[:20], scratch[20]
    ig_in, w, g, m, u = hbm[0], bufs[0:5], bufs[5:10], bufs[10:15], bufs[15:20]
    ig_out, norm_o, new, first, second = outs[0], outs[1], outs[2:7], outs[7:12], outs[12:17]
    through = pltpu.make_async_copy(ig_in, ig_out, sem.at[20])
    through.start()
    loads = [pltpu.make_async_copy(hbm[1 + i], bufs[i], sem.at[i]) for i in range(20)]
    for c in loads:
        c.start()
    norm = jnp.sqrt(total[...])
    norm_o[...] = norm
    factor = jnp.minimum(1.0, clip_limit / (norm + 1e-06))[0:1, 0:1]
    for c in loads:
        c.wait()
    for i in range(4):
        n, f, s = adam_step(w[i][...], factor * g[i][...], m[i][...], u[i][...], weight_decay, learn_rate)
        new[i][...] = n
        first[i][...] = f
        second[i][...] = s
    wide = jnp.concatenate([g[4][...], jnp.zeros((104, 128), f32)], axis=0).T[:12, :24]
    n, f, s = adam_step(w[4][...], factor * wide, m[4][...], u[4][...], 0.0, vector_rate)
    new[4][...] = n
    first[4][...] = f
    second[4][...] = s
    through.wait()


def update(total, input_grad, weights, grads, firsts, seconds):
    shapes = [S(w.shape, f32) for w in weights]
    arrays = (*weights, *grads, *firsts, *seconds)
    return pl.pallas_call(
        update_kernel,
        in_specs=[VM] + [ANY] * 21,
        out_specs=[VM] * 17,
        out_shape=[S(input_grad.shape, bf), S((8, 128), f32)] + shapes * 3,
        scratch_shapes=[pltpu.VMEM(a.shape, f32) for a in arrays] + [pltpu.SemaphoreType.DMA((21,))],
        compiler_params=pltpu.CompilerParams(vmem_limit_bytes=60 * MIB),
        name="clip_and_update",
    )(total, input_grad, *arrays)


def segment_ids(lengths):
    bounds = jnp.cumsum(lengths, axis=-1)
    places = jnp.arange(T, dtype=jnp.int32)
    return jnp.sum((places[:, None] >= bounds[None, :]).astype(jnp.int32), axis=-1)


def pairs_last(a):
    return a.reshape(3, D, PAIRS, 128).transpose(1, 2, 0, 3).reshape(D, 3 * D)


def per_device(
    small, tokens, cotangent, lengths, qkv_weight, out_weight, in_weight, down_weight, vectors,
    qkv_first, out_first, in_first, down_first, vec_first, qkv_second, out_second, in_second, down_second, vec_second,
):
    weights = (qkv_weight, out_weight, in_weight, down_weight, vectors)
    firsts = (qkv_first, out_first, in_first, down_first, vec_first)
    seconds = (qkv_second, out_second, in_second, down_second, vec_second)
    axes = ("dp", "fsdp")
    seg = segment_ids(lengths[0])
    lane = jnp.arange(128)
    match = seg[:, None] == lane[None, :]
    onehot = match.astype(bf)
    neg = jnp.where(match | (lane >= lengths.shape[1])[None, :], 0.0, -1e30).astype(bf)
    if small:
        wqkv, wo, wi, w2, vec, q, k, v, ctx, lse = forward(tokens, onehot, neg, weights)
        result, dh1, dctx, vg, gwo, gwi, gw2 = feed_forward(tokens, ctx, cotangent, vec[:16], wo, wi, w2)
        ig, *grads, total = backward(tokens, wqkv, dh1, q, k, v, dctx, ctx, lse, onehot, neg, vg, gwo, gwi, gw2)
        updated = update(total, ig, weights, grads, firsts, seconds)
        return (result, updated[0], updated[1][0, 0], *updated[2:])
    gather = lambda a, axis: lax.all_gather(a.astype(bf), axes, axis=axis, tiled=True)
    wqkv = pairs_last(gather(qkv_weight, 1))
    wo, wi, w2 = gather(out_weight, 0), gather(in_weight, 0), gather(down_weight, 0)
    vec = jnp.concatenate([gather(vectors, 1).astype(f32), jnp.zeros((4, D), f32)], axis=0)
    bias = jnp.stack([vec[0], jnp.zeros_like(vec[0]), vec[1]]).reshape(3, PAIRS, 128).transpose(1, 0, 2).reshape(1, 3 * D)
    q, k, v, ctx, lse = attend(tokens, wqkv, bias, onehot, neg)
    result, dh1, dctx, vg, gwo, gwi, gw2 = feed_forward(tokens, ctx, cotangent, vec, wo, wi, w2)
    gqkv, input_grad, vg_qv = attend_back(tokens, wqkv, dh1, q, k, v, dctx, ctx, lse, onehot, neg)
    vg = vg + vg_qv
    scatter = lambda a, axis: lax.psum_scatter(a.astype(f32), axes, scatter_dimension=axis, tiled=True)
    gqkv = gqkv.reshape(D, PAIRS, 3, 128).transpose(2, 0, 1, 3).reshape(3, D, D)
    grads = (scatter(gqkv, 1), scatter(gwo, 0), scatter(gwi, 0), scatter(gw2, 0), scatter(vg[:12], 1))
    grad_norm = jnp.sqrt(lax.psum(sum(jnp.sum(g * g) for g in grads), axes))
    factor = jnp.minimum(1.0, clip_limit / (grad_norm + 1e-06))
    updated = []
    for i in range(5):
        rates = (0.0, vector_rate) if i == 4 else (weight_decay, learn_rate)
        updated.append(adam_step(weights[i], factor * grads[i], firsts[i], seconds[i], *rates))
    return (result, input_grad, grad_norm, *[u[j] for j in range(3) for u in updated])


def solution(mesh):
    rows = P(("dp", "fsdp"), None)
    deep = P(None, ("dp", "fsdp"), None)
    wide = P(None, ("dp", "fsdp"))
    group = (deep, rows, rows, rows, wide)
    small = mesh.shape["dp"] == 4 and mesh.shape["fsdp"] == 8
    return jax.shard_map(
        functools.partial(per_device, small),
        mesh=mesh,
        in_specs=(rows, rows, rows) + group * 3,
        out_specs=(rows, rows, P()) + group * 3,
        check_vma=False,
    )
```

```python
import functools

import jax
import jax.numpy as jnp
from jax import lax
from jax.experimental import pallas as pl
from jax.experimental.pallas import tpu as pltpu
from jax.sharding import PartitionSpec as P

D = 768
H = 12
HD = 64
FF = 3072
T = 1024
STEP = 10
PAIRS = H // 2
W3 = 384

moment_decay = 0.9
square_decay = 0.999
learn_rate = 0.02
vector_rate = 0.15
weight_decay = 0.01
adam_epsilon = 1e-08
clip_limit = 1.0
norm_epsilon = 1e-05

bf = jnp.bfloat16
f32 = jnp.float32
MESH = pl.DeviceIdType.MESH
VM = pl.BlockSpec(memory_space=pltpu.VMEM)
ANY = pl.BlockSpec(memory_space=pl.ANY)
MIB = 2**20


def S(shape, dtype):
    return jax.ShapeDtypeStruct(shape, dtype)


def nn(a, b):
    return lax.dot_general(a, b, (((1,), (0,)), ((), ())), preferred_element_type=f32)


def nt(a, b):
    return lax.dot_general(a, b, (((1,), (1,)), ((), ())), preferred_element_type=f32)


def tn(a, b):
    return lax.dot_general(a, b, (((0,), (0,)), ((), ())), preferred_element_type=f32)


def colsum(x):
    return jnp.sum(x, axis=0, keepdims=True)


class Place:
    def __init__(self):
        self.dp = lax.axis_index("dp")
        self.fs = lax.axis_index("fsdp")
        self.z = self.fs // 2
        self.k = self.fs % 2
        dp, k = self.dp, self.k
        xn = dp + 1 - 2 * (dp % 2)
        yn = (dp + 2) % 4
        self.dp1 = xn * (1 - k) + yn * k
        self.dp2 = yn * (1 - k) + xn * k
        self.dp3 = 3 - dp
        self.n1 = (self.dp1, self.fs)
        self.n2 = (self.dp2, self.fs)
        self.sib = (dp, self.z * 2 + 1 - k)
        self.zp = [(dp, ((self.z + i) % 4) * 2 + k) for i in (1, 2, 3)]
        self.m = dp * 2 + k
        self.others = []
        for j in range(1, 8):
            other = (self.m + j) % 8
            self.others.append((other // 2, self.z * 2 + other % 2))


def enter(peers):
    barrier = pltpu.get_barrier_semaphore()
    for peer in peers:
        pl.semaphore_signal(barrier, inc=1, device_id=peer, device_id_type=MESH)
    pl.semaphore_wait(barrier, len(peers))


def rcopy(src, dst, ssem, rsem, peer):
    return pltpu.make_async_remote_copy(src, dst, ssem, rsem, device_id=peer, device_id_type=MESH)


def half(w, c):
    return pl.ds(pl.multiple_of(c * w, 128), w)


def band(rows, index):
    return pl.ds(pl.multiple_of(rows * index, 16), rows)


def masks(lengths, onehot, neg):
    lane = lax.broadcasted_iota(jnp.int32, (1, 128), 1)
    first = jnp.full((1, 128), T, jnp.int32)
    after = jnp.full((1, 128), T, jnp.int32)
    total = jnp.int32(0)
    count = lengths.shape[1]
    for j in range(count):
        first = jnp.where(lane == j, total, first)
        total = total + lengths[0, j]
        after = jnp.where(lane == j, total, after)
    row = lax.broadcasted_iota(jnp.int32, (T, 128), 0)
    own = (row >= first) & (row < after)
    onehot[...] = jnp.where(own, 1.0, 0.0).astype(bf)
    neg[...] = jnp.where(own | (lane >= count), 0.0, -1e30).astype(bf)


PACE_FORWARD = 5.2
PACE_BACKWARD = 4.2


class Gather:
    def __init__(self, p, chunks, gs, gr):
        self.p, self.chunks, self.gs, self.gr = p, chunks, gs, gr
        self.sent = []

    def go(self, part, j, rows, peer):
        n, ref, rc, cols, swap = part
        view = ref.at[rows, cols]
        c = rcopy(view, view, self.gs.at[n, j], self.gr.at[n, j], peer)
        c.start()
        self.sent.append(c)
        return c

    def first(self, i):
        p = self.p
        out = []
        for part in self.chunks[i]:
            rc = part[2]
            out.append([self.go(part, j, band(rc, p.dp * 4 + p.z), p.zp[j]) for j in range(3)])
        return out

    def slots(self, ahead):
        p, n = self.p, len(self.chunks)
        zc, c1, c2, c3, c4 = {}, {}, {}, {}, {}

        def more(i):
            if i < n:
                zc[i] = self.first(i)

        def links(i):
            if 0 <= i < n:
                c1[i], c2[i] = [], []
                for q, part in enumerate(self.chunks[i]):
                    for c in zc[i][q]:
                        c.wait_recv()
                    c1[i].append(self.go(part, 3, band(4 * part[2], p.dp), p.n1))
                    c2[i].append(self.go(part, 4, band(4 * part[2], p.dp), p.n2))

        def cross(i):
            if 0 <= i < n:
                c3[i] = []
                for q, part in enumerate(self.chunks[i]):
                    c1[i][q].wait_recv()
                    c3[i].append(self.go(part, 5, band(4 * part[2], p.dp1), p.n2))

        def swap(i):
            if 0 <= i < n:
                c4[i] = []
                for q, part in enumerate(self.chunks[i]):
                    c2[i][q].wait_recv()
                    c3[i][q].wait_recv()
                    if part[4]:
                        c4[i].append(self.go(part, 6, pl.ds(0, 16 * part[2]), p.sib))

        def take(i):
            if 0 <= i < n:
                for c in c4[i]:
                    c.wait_recv()

        for i in range(min(ahead, n)):
            zc[i] = self.first(i)
        yield -1
        links(0)
        cross(0)
        links(1)
        swap(0)
        links(2)
        more(ahead)
        take(0)
        cross(1)
        links(3)
        more(ahead + 1)
        yield 0
        for t in range(1, n + 2):
            more(t + ahead + 1)
            links(t + 3)
            cross(t + 1)
            if t != 2:
                swap(max(t - 1, 1))
            if t == 2 or t > 3:
                take(max(t - 2, 1))
            yield max(t - 2, min(t - 1, 1))
        for c in self.sent:
            c.wait_send()
        yield n


def forward_kernel(
    block, tok_h, lengths, qkv, out, inw, down, vec,
    wqkv_h, wo_h, wi_h, w2, vrow, q_h, k_h, v_h, ctx_h, low_h, lse, hb_h, gp_h, xh_h, sd, xb_h,
    tok, wq, vt, qs_, ks_, vs_, ctx, low, qa, ka, va, onehot, neg,
    m_qkv, m_out, m_in, m_down, m_vec, x_qkv, x_out, x_in, x_down, x_vec, myvec,
    own_down, wo, wi, hb, gp, xh, xb, xs, xr, gs, gr, ls, os, fs,
):
    p = Place()
    k = p.k
    far = 1 - k
    loads = [
        pltpu.make_async_copy(vec, m_vec, ls.at[4]),
        pltpu.make_async_copy(qkv.at[:, :, half(W3, k)], m_qkv, ls.at[0]),
        pltpu.make_async_copy(out.at[:, half(W3, k)], m_out, ls.at[1]),
        pltpu.make_async_copy(inw.at[:, half(4 * W3, k)], m_in, ls.at[2]),
        pltpu.make_async_copy(down.at[:, half(W3, k)], m_down, ls.at[3]),
        pltpu.make_async_copy(tok_h, tok, ls.at[5]),
    ]
    for c in loads:
        c.start()
    enter([p.sib, p.n1, p.n2] + p.zp)
    swaps = [
        rcopy(qkv.at[:, :, half(W3, far)], x_qkv, xs.at[0], xr.at[0], p.sib),
        rcopy(out.at[:, half(W3, far)], x_out, xs.at[1], xr.at[1], p.sib),
        rcopy(inw.at[:, half(4 * W3, far)], x_in, xs.at[2], xr.at[2], p.sib),
        rcopy(down.at[:, half(W3, far)], x_down, xs.at[3], xr.at[3], p.sib),
        rcopy(myvec, x_vec, xs.at[4], xr.at[4], p.sib),
    ]
    for c in swaps[:4]:
        c.start()
    loads[0].wait()
    pad = jnp.concatenate([m_vec[...], jnp.zeros((128 - 12, 24), f32)], axis=0)
    myvec[...] = jnp.concatenate([pad, jnp.zeros((128, 104), f32)], axis=1).T[:24, :]
    swaps[4].start()

    def both(mine, other):
        lo = jnp.where(k == 0, mine, other)
        hi = jnp.where(k == 0, other, mine)
        return jnp.concatenate([lo, hi], axis=0).astype(bf)

    chip = p.dp * 4 + p.z
    loads[1].wait()
    swaps[0].wait_recv()
    for j in range(3):
        mat = both(m_qkv[j], x_qkv[j])
        for t in range(3):
            wq[band(48, chip), pl.ds(pl.multiple_of((3 * k + t) * W3 + j * 128, 128), 128)] = mat[:, t * 128 : (t + 1) * 128]
    swaps[4].wait_recv()
    vt[band(48, chip), :] = both(myvec[...], x_vec[...])

    chunks = []
    for t in range(3):
        chunks.append([(len(chunks), wq, 48, half(W3, t + 3 * k), True)])
    chunks.append([(len(chunks), wo, 48, half(W3, k), True)])
    for t in range(4):
        chunks.append([(len(chunks), wi, 48, half(W3, t + 4 * k), True)])
    for t in range(3):
        chunks.append([(len(chunks), w2, 192, half(128, 3 * k + t), True)])
    chunks[0].append((11, vt, 48, pl.ds(0, 128), False))
    gather = Gather(p, chunks, gs, gr)
    slots = gather.slots(3)
    done = [next(slots)]
    for i in range(3):
        loads[2 + i].wait()
        swaps[1 + i].wait_recv()
    wo[band(48, chip), half(W3, k)] = both(m_out[...], x_out[...])
    wi[band(48, chip), half(4 * W3, k)] = both(m_in[...], x_in[...])
    own_down[...] = both(m_down[...], x_down[...])
    local = pltpu.make_async_copy(own_down, w2.at[band(192, chip), half(W3, k)], ls.at[3])
    local.start()
    local.wait()
    loads[5].wait()
    masks(lengths, onehot, neg)

    def upto(i):
        while done[0] < i:
            done[0] = next(slots, len(chunks))

    spent = [0.0]

    def spend(us):
        spent[0] += us
        if spent[0] >= PACE_FORWARD and done[0] < len(chunks) - 1:
            spent[0] -= PACE_FORWARD
            done[0] = next(slots)

    upto(0)
    vrow[...] = vt[...].astype(f32).T
    lane = lax.broadcasted_iota(jnp.int32, (1, 128), 1)
    ka[:, 128:] = neg[...]
    va[:, 128:] = jnp.ones((T, 128), bf)
    qa[:, 128:] = onehot[...]
    outs = []
    for turn, pair in enumerate((0, 3, 1, 4, 2, 5)):
        upto(turn // 2)
        spend(0.8)
        cs = slice(pair * 128, (pair + 1) * 128)
        y = nn(tok[...], wq[:, pair * W3 : (pair + 1) * W3])
        q = (y[:, :128] + vrow[0:1, cs]).astype(bf)
        key = y[:, 128:256].astype(bf)
        val = (y[:, 256:] + vrow[1:2, cs]).astype(bf)
        qs_[:, cs] = q
        ks_[:, cs] = key
        vs_[:, cs] = val
        for n, (src, dst) in enumerate(((qs_, q_h), (ks_, k_h), (vs_, v_h))):
            outs.append(pltpu.make_async_copy(src.at[:, cs], dst.at[:, cs], os.at[n, pair]))
            outs[-1].start()
        qs = (q.astype(f32) * HD ** (-0.5)).astype(bf)
        ka[:, :128] = key
        va[:, :128] = val
        for h in range(2):
            sel = (lane // 64) == h
            qa[:, :128] = jnp.where(sel, qs, jnp.zeros_like(qs))
            for b in range(T // block):
                r = slice(b * block, (b + 1) * block)
                s = nt(qa[r, :], ka[...])
                m = jnp.max(s, axis=1, keepdims=True)
                e = jnp.exp(s - m).astype(bf)
                o = nn(e, va[...])
                tot = o[:, 128:]
                c = o[:, :128] / tot
                l = m + jnp.log(tot)
                ctx[r, cs] = c if h == 0 else jnp.where(sel, c, ctx[r, cs])
                lse[r, :] = l if turn + h == 0 else jnp.where(lane == 2 * pair + h, l, lse[r, :])
                spend(0.55)
        low[:, cs] = ctx[:, cs].astype(bf)
        for n, (src, dst) in enumerate(((ctx, ctx_h), (low, low_h))):
            outs.append(pltpu.make_async_copy(src.at[:, cs], dst.at[:, cs], os.at[3 + n, pair]))
            outs[-1].start()
    def give(src, dst, sem):
        outs.append(pltpu.make_async_copy(src, dst, sem))
        outs[-1].start()

    give(wq, wqkv_h, ls.at[0])
    row = lambda i: vrow[i : i + 1, :]
    rows = [slice(b * 256, (b + 1) * 256) for b in range(4)]
    upto(3)
    for r in rows:
        spend(0.7)
        xhat, rd = norm_forward(tok[r, :].astype(f32) + (nn(low[r, :], wo[...]) + row(2)))
        xh[r, :] = xhat
        sd[r, :] = jnp.broadcast_to(rd, (256, 128))
        xb[r, :] = (xhat * row(4) + row(5)).astype(bf)
    give(wo, wo_h, ls.at[1])
    give(xh, xh_h, ls.at[2])
    give(xb, xb_h, ls.at[3])
    for j in (0, 2, 1, 3):
        upto(5 if j % 2 == 0 else 7)
        cs = slice(j * D, (j + 1) * D)
        for r in rows:
            hp = nn(xb[r, :], wi[:, cs]) + row(8 + j)
            big, dense = gelu_parts(hp)
            hb[r, cs] = (hp * big).astype(bf)
            gp[r, cs] = big + hp * dense
            spend(0.7)
        give(hb.at[:, cs], hb_h.at[:, cs], fs.at[0, j])
        give(gp.at[:, cs], gp_h.at[:, cs], fs.at[1, j])
    give(wi, wi_h, ls.at[4])
    for c in slots:
        pass
    for c in swaps:
        c.wait_send()
    for c in outs:
        c.wait()


SMEM = pl.BlockSpec(memory_space=pltpu.SMEM)


def forward(tok, lengths, weights, block=256):
    vb = lambda *shape: pltpu.VMEM(shape, bf)
    vf = lambda *shape: pltpu.VMEM(shape, f32)
    dma = lambda *shape: pltpu.SemaphoreType.DMA(shape)
    return pl.pallas_call(
        functools.partial(forward_kernel, block),
        in_specs=[ANY, SMEM] + [ANY] * 5,
        out_specs=[ANY] * 4 + [VM] + [ANY] * 5 + [VM] + [ANY] * 3 + [VM] + [ANY],
        out_shape=[S((D, 3 * D), bf), S((D, D), bf), S((D, FF), bf), S((FF, D), bf), S((128, D), f32)]
        + [S((T, D), bf)] * 3 + [S((T, D), f32), S((T, D), bf), S((T, 128), f32)]
        + [S((T, FF), bf), S((T, FF), f32), S((T, D), f32), S((T, 128), f32), S((T, D), bf)],
        scratch_shapes=[
            vb(T, D), vb(D, 3 * D), vb(D, 128), vb(T, D), vb(T, D), vb(T, D), vf(T, D), vb(T, D), vb(T, 256), vb(T, 256), vb(T, 256),
            vb(T, 128), vb(T, 128),
            vf(3, 24, W3), vf(24, W3), vf(24, 4 * W3), vf(96, W3), vf(12, 24),
            vf(3, 24, W3), vf(24, W3), vf(24, 4 * W3), vf(96, W3), vf(24, 128), vf(24, 128),
            vb(192, W3), vb(D, D), vb(D, FF), vb(T, FF), vf(T, FF), vf(T, D), vb(T, D),
            dma(5), dma(5), dma(12, 7), dma(12, 7), dma(6), dma(5, 6), dma(2, 4),
        ],
        compiler_params=pltpu.CompilerParams(collective_id=0, has_side_effects=True, vmem_limit_bytes=60 * MIB),
        name="forward",
    )(tok, lengths, *weights)


def attend_kernel(block, tok, w, bias, onehot, neg, q_o, k_o, v_o, ctx_o, lse_o, qa, ka, va):
    lane = lax.broadcasted_iota(jnp.int32, (1, 128), 1)
    pair = pl.program_id(0)
    y = nn(tok[...], w[...]) + bias[...]
    q = y[:, :128].astype(bf)
    key = y[:, 128:256].astype(bf)
    val = y[:, 256:].astype(bf)
    q_o[...] = q
    k_o[...] = key
    v_o[...] = val
    qs = (q.astype(f32) * HD ** (-0.5)).astype(bf)
    ka[:, :128] = key
    ka[:, 128:] = neg[...]
    va[:, :128] = val
    va[:, 128:] = jnp.ones((T, 128), bf)
    qa[:, 128:] = onehot[...]
    for h in range(2):
        sel = (lane // 64) == h
        qa[:, :128] = jnp.where(sel, qs, jnp.zeros_like(qs))
        for b in range(T // block):
            r = slice(b * block, (b + 1) * block)
            s = nt(qa[r, :], ka[...])
            m = jnp.max(s, axis=1, keepdims=True)
            e = jnp.exp(s - m).astype(bf)
            o = nn(e, va[...])
            tot = o[:, 128:]
            c = o[:, :128] / tot
            l = m + jnp.log(tot)
            ctx_o[r, :] = c if h == 0 else jnp.where(sel, c, ctx_o[r, :])
            lse_o[r, :] = jnp.where(lane == 2 * pair + h, l, lse_o[r, :])


def attend(tok, w, bias, onehot, neg, block=256):
    full = lambda s: pl.BlockSpec(s, lambda i: (0,) * len(s))
    col = pl.BlockSpec((T, 128), lambda i: (0, i))
    return pl.pallas_call(
        functools.partial(attend_kernel, block),
        grid=(PAIRS,),
        in_specs=[
            full((T, D)), pl.BlockSpec((D, W3), lambda i: (0, i)), pl.BlockSpec((1, W3), lambda i: (0, i)),
            full((T, 128)), full((T, 128)),
        ],
        out_specs=[col, col, col, col, full((T, 128))],
        out_shape=[S((T, D), bf)] * 3 + [S((T, D), f32), S((T, 128), f32)],
        scratch_shapes=[pltpu.VMEM((T, 256), bf)] * 3,
        compiler_params=pltpu.CompilerParams(vmem_limit_bytes=60 * MIB),
        name="attend",
    )(tok, w, bias, onehot, neg)


def split3(x):
    hi = x.astype(bf).astype(f32)
    mid = (x - hi).astype(bf).astype(f32)
    return hi, mid, x - hi - mid


class Back:
    def __init__(self, block, onehot, neg, qa, ka, va, da, kT, dqT, dka, dva):
        self.block, self.onehot, self.neg = block, onehot, neg
        self.refs = (qa, ka, va, da, kT, dqT, dka, dva)
        self.lane = lax.broadcasted_iota(jnp.int32, (1, 128), 1)

    def start(self):
        qa, ka, va, da, kT, dqT, dka, dva = self.refs
        minus = jnp.where((self.lane >= 16) & (self.lane < 19), -1.0, 0.0)
        ka[:, 128:] = (self.neg[...].astype(f32) + minus).astype(bf)
        va[:, 128:] = jnp.broadcast_to(minus, (T, 128)).astype(bf)

    def pair(self, pair, q, key, val, d, ctx, lse, tick):
        lane, block = self.lane, self.block
        qa, ka, va, da, kT, dqT, dka, dva = self.refs
        qs = (q.astype(f32) * HD ** (-0.5)).astype(bf)
        ka[:, :128] = key
        va[:, :128] = val
        kT[...] = key.T
        prod = d.astype(f32) * ctx

        def extra(base, parts):
            for j, part in enumerate(parts):
                base = jnp.where(lane == 16 + j, part, base)
            return base.astype(bf)

        for h in range(2):
            sel = (lane // 64) == h
            inner = jnp.sum(jnp.where(sel, prod, 0.0), axis=1, keepdims=True)
            lsum = jnp.sum(jnp.where(lane == 2 * pair + h, lse, 0.0), axis=1, keepdims=True)
            qa[:, :128] = jnp.where(sel, qs, jnp.zeros_like(qs))
            qa[:, 128:] = extra(self.onehot[...].astype(f32), split3(lsum))
            da[:, :128] = jnp.where(sel, d, jnp.zeros_like(d))
            da[:, 128:] = extra(jnp.zeros((T, 128), f32), split3(inner))
            for b in range(T // block):
                r = slice(b * block, (b + 1) * block)
                pt = jnp.exp(nt(ka[...], qa[r, :]))
                dpt = nt(va[...], da[r, :])
                ds = (pt * dpt).astype(bf)
                x = nn(pt.astype(bf), da[r, :128])
                y = nn(ds, qa[r, :128])
                dqT[h * 64 : (h + 1) * 64, r] = nn(kT[h * 64 : (h + 1) * 64, :], ds)
                if h == 0 and b == 0:
                    dva[...] = x
                    dka[...] = y
                else:
                    dva[...] += x
                    dka[...] += y
                tick()
        dv = dva[...].astype(bf)
        dk = dka[...].astype(bf)
        dq = (dqT[...].T * HD ** (-0.5)).astype(bf)
        return dq, dk, dv


BACK_SCRATCH = (
    [pltpu.VMEM((T, 256), bf)] * 4 + [pltpu.VMEM((128, T), bf), pltpu.VMEM((128, T), f32)] + [pltpu.VMEM((T, 128), f32)] * 2
)


def attend_back_kernel(
    block, tok, w, dh1, q_i, k_i, v_i, dctx_i, ctx_i, lse, onehot, neg, g_o, ig_o, vg_o, *scratch,
):
    tokT, ig = scratch[-2:]
    step = pl.program_id(0)
    back = Back(block, onehot, neg, *scratch[:-2])

    @pl.when(step == 0)
    def _():
        tokT[...] = tok[...].T
        ig[...] = dh1[...]

    back.start()
    dq, dk, dv = back.pair(step, q_i[...], k_i[...], v_i[...], dctx_i[...], ctx_i[...], lse[...], lambda: None)
    vg_o[...] = jnp.zeros_like(vg_o)
    vg_o[0:1, :] = colsum(dq.astype(f32))
    vg_o[1:2, :] = colsum(dv.astype(f32))
    cat = jnp.concatenate([dq, dk, dv], axis=1)
    g_o[...] = nn(tokT[...], cat).astype(bf)
    ig[...] += nt(cat, w[...])

    @pl.when(step == PAIRS - 1)
    def _():
        ig_o[...] = ig[...].astype(bf)


def attend_back(tok, w, dh1, q, k, v, dctx, ctx, lse, onehot, neg, block=512):
    full = lambda s: pl.BlockSpec(s, lambda i: (0,) * len(s))
    col = pl.BlockSpec((T, 128), lambda i: (0, i))
    return pl.pallas_call(
        functools.partial(attend_back_kernel, block),
        grid=(PAIRS,),
        in_specs=[
            full((T, D)), pl.BlockSpec((D, W3), lambda i: (0, i)), full((T, D)),
            col, col, col, col, col, full((T, 128)), full((T, 128)), full((T, 128)),
        ],
        out_specs=[pl.BlockSpec((D, W3), lambda i: (0, i)), full((T, D)), pl.BlockSpec((16, 128), lambda i: (0, i))],
        out_shape=[S((D, 3 * D), bf), S((T, D), bf), S((16, D), f32)],
        scratch_shapes=BACK_SCRATCH + [pltpu.VMEM((D, T), bf), pltpu.VMEM((T, D), f32)],
        compiler_params=pltpu.CompilerParams(vmem_limit_bytes=60 * MIB),
        name="attend_back",
    )(tok, w, dh1, q, k, v, dctx, ctx, lse, onehot, neg)


def fold(x):
    rows, width = x.shape
    x = x * x
    tot = jnp.zeros((8, 128), f32)
    for i in range(rows // 8):
        for j in range(width // 128):
            tot = tot + x[i * 8 : (i + 1) * 8, j * 128 : (j + 1) * 128]
    return tot


def add_rows(dst, row0, src, rows):
    step = 96 if rows % 96 == 0 else rows

    def body(i, carry):
        d = pl.ds(pl.multiple_of(row0 + i * step, 16), step)
        s = pl.ds(pl.multiple_of(i * step, 16), step)
        dst[d, :] = (dst[d, :].astype(f32) + src[s, :].astype(f32)).astype(bf)
        return carry

    lax.fori_loop(0, rows // step, body, 0)


OFF = (2, 4, 6)


class Reduce:
    def __init__(self, p, gs, gr, s_vec):
        self.p, self.gs, self.gr, self.s_vec = p, gs, gr, s_vec
        self.sent = []
        self.squares = jnp.zeros((8, 128), f32)

    def go(self, src, dst, n, j, peer):
        c = rcopy(src, dst, self.gs.at[n, j], self.gr.at[n, j], peer)
        c.start()
        self.sent.append(c)
        return c

    def go_x(self, src, dst, ssem, rsem, peer):
        c = rcopy(src, dst, ssem, rsem, peer)
        c.start()
        self.sent.append(c)
        return c

    def send_first(self, part):
        n, rc, acc, give, ready, rs, r2, r1, rz, fin = part
        return self.go(give, rs, n, 0, self.p.sib)

    def slots(self, chunks, issue):
        p, n = self.p, len(chunks)
        cS, cP, cQ, cZ = {}, {}, {}, {}
        for s in range(n + OFF[2]):
            i = s
            if i < n:
                cP[i] = []
                for part, first in zip(chunks[i], issue(i)):
                    num, rc, acc, give, ready, rs, r2, r1, rz, fin = part
                    if ready is not None:
                        ready.wait()
                    first.wait_recv()
                    add_rows(acc, 0, rs, 16 * rc)
                    cP[i].append((
                        self.go(acc.at[band(4 * rc, p.dp2), :], r2.at[0], num, 1, p.n2),
                        self.go(acc.at[band(4 * rc, p.dp3), :], r2.at[1], num, 2, p.n2),
                    ))
            i = s - OFF[0]
            if 0 <= i < n:
                cQ[i] = []
                for part, (near, cross) in zip(chunks[i], cP[i]):
                    num, rc, acc, give, ready, rs, r2, r1, rz, fin = part
                    cross.wait_recv()
                    add_rows(acc, p.dp1 * 4 * rc, r2.at[1], 4 * rc)
                    cQ[i].append(self.go(acc.at[band(4 * rc, p.dp1), :], r1, num, 3, p.n1))
                    near.wait_recv()
                    add_rows(acc, p.dp * 4 * rc, r2.at[0], 4 * rc)
            i = s - OFF[1]
            if 0 <= i < n:
                cZ[i] = []
                for part, q in zip(chunks[i], cQ[i]):
                    num, rc, acc, give, ready, rs, r2, r1, rz, fin = part
                    q.wait_recv()
                    add_rows(acc, p.dp * 4 * rc, r1, 4 * rc)
                    cZ[i].append([
                        self.go(acc.at[band(rc, p.dp * 4 + (p.z + j + 1) % 4), :], rz.at[j], num, 4 + j, p.zp[j]) for j in range(3)
                    ])
            i = s - OFF[2]
            if 0 <= i < n:
                for part, zs in zip(chunks[i], cZ[i]):
                    num, rc, acc, give, ready, rs, r2, r1, rz, fin = part
                    for c in zs:
                        c.wait_recv()
                    own = acc[band(rc, p.dp * 4 + p.z), :].astype(f32)
                    for j in range(3):
                        own = own + rz[j].astype(f32)
                    if fin is None:
                        own = jnp.where(p.k == 0, own[:24], own[24:])
                        self.s_vec[...] = own
                    else:
                        fin[...] = own
                    self.squares = self.squares + fold(own)
            yield s + 1


def backward_kernel(
    block, lengths, tok_h, wqkv_h, dh1_h, q_h, k_h, v_h, dctx_h, ctx_h, lse, vg_i, gwo, gwi, gw2,
    ig_h, s_qkv, s_out, s_in, s_down, s_vec, total,
    onehot, neg, tok, wq, ig, q, k_, v, dctx, ctx, gq, gvt, vg,
    qa, ka, va, da, kT, dqT, dka, dva, tokT,
    acc_a, rs_a, r2_a, r1_a, rz_a, acc_d, rs_d, r2_d, r1_d, rz_d, acc_v, rs_v, r2_v, r1_v, rz_v,
    fin_a, fin_d, rx_a, rx_d, tile, nb1, nb2, gs, gr, ls, xs, xr, ns, nr, ps, ts,
):
    p = Place()
    k = p.k
    far = 1 - k
    order = (0, 3, 1, 4, 2, 5)
    cols = lambda pair: slice(pair * 128, (pair + 1) * 128)
    early = [pltpu.make_async_copy(tok_h, tok, ts.at[0])]
    pairs = {}
    for pair in order:
        moves = ((q_h, q), (k_h, k_), (v_h, v), (dctx_h, dctx), (ctx_h, ctx))
        pairs[pair] = [
            pltpu.make_async_copy(src.at[:, cols(pair)], dst.at[:, cols(pair)], ps.at[n, pair]) for n, (src, dst) in enumerate(moves)
        ]
    late = [pltpu.make_async_copy(wqkv_h, wq, ts.at[1]), pltpu.make_async_copy(dh1_h, ig, ts.at[2])]
    for c in early + pairs[0] + pairs[3]:
        c.start()
    enter(p.others + p.zp)
    red = Reduce(p, gs, gr, s_vec)

    chunks = []
    for t in range(3):
        load = pltpu.make_async_copy(gw2.at[:, half(128, 3 * k + t)], acc_d.at[t], ls.at[t])
        load.start()
        chunks.append([(
            t, 192, acc_d.at[t], gw2.at[:, half(128, 3 * far + t)], load, rs_d.at[t], r2_d.at[t], r1_d.at[t], rz_d.at[t], fin_d.at[t],
        )])
    spots = lambda a: (rs_a.at[a], r2_a.at[a], r1_a.at[a], rz_a.at[a], fin_a.at[a])
    for t in range(5):
        ref, start = (gwi, lambda c: t + 4 * c) if t < 4 else (gwo, lambda c: c)
        load = pltpu.make_async_copy(ref.at[:, half(W3, start(k))], acc_a.at[t], ls.at[3 + t])
        load.start()
        chunks.append([(3 + t, 48, acc_a.at[t], ref.at[:, half(W3, start(far))], load) + spots(t)])
    firsts = {i: [red.send_first(part) for part in chunks[i]] for i in range(8)}
    for t in range(3):
        chunks.append([(8 + t, 48, gq.at[t, k], gq.at[t, far], None) + spots(5 + t)])
    chunks[10].append((11, 48, acc_v, gvt, None, rs_v, r2_v, r1_v, rz_v, None))
    sequence = (0, 1, 2, 3, 8, 4, 5, 6, 9, 7, 10)
    ordered = [chunks[i] for i in sequence]
    ready = set(range(8))

    def issue(s):
        assert sequence[s] in ready
        return firsts[sequence[s]]

    slots = red.slots(ordered, issue)
    place = [0]

    def step():
        place[0] = next(slots)

    for pair in order[2:]:
        for c in pairs[pair]:
            c.start()
    for c in late:
        c.start()
    early[0].wait()
    tokT[...] = tok[...].T
    back = Back(block, onehot, neg, qa, ka, va, da, kT, dqT, dka, dva)
    masks(lengths, onehot, neg)
    back.start()
    vg[...] = vg_i[...]
    spent = [0.0]

    def tick(us=1.65):
        spent[0] += us
        if spent[0] >= PACE_BACKWARD and place[0] < len(sequence) and sequence[place[0]] in ready:
            spent[0] -= PACE_BACKWARD
            step()

    parts = {}
    for turn, pair in enumerate(order):
        cs = cols(pair)
        for c in pairs[pair]:
            c.wait()
        dq, dk, dv = back.pair(pair, q[:, cs], k_[:, cs], v[:, cs], dctx[:, cs], ctx[:, cs], lse[...], tick)
        q[:, cs] = dq
        k_[:, cs] = dk
        v[:, cs] = dv
        vg[0:1, cs] = colsum(dq.astype(f32))
        vg[1:2, cs] = colsum(dv.astype(f32))
        t, side = turn // 2, turn % 2
        for j, part in enumerate((dq, dk, dv)):
            gq[t, side, :, j * 128 : (j + 1) * 128] = nn(tokT[...], part).astype(bf)
        tick(0.8)
        if side == 1:
            if t == 2:
                gvt[...] = jnp.concatenate([vg[...], jnp.zeros((112, D), f32)], axis=0).T.astype(bf)
                acc_v[...] = gvt[...]
            firsts[8 + t] = [red.send_first(part) for part in chunks[8 + t]]
            ready.add(8 + t)
    for c in late:
        c.wait()
    rows = [slice(b * 256, (b + 1) * 256) for b in range(4)]
    for r in rows:
        if place[0] < len(sequence) + OFF[2]:
            step()
        tot = ig[r, :]
        for pair in range(PAIRS):
            cs = cols(pair)
            cat = jnp.concatenate([q[r, cs], k_[r, cs], v[r, cs]], axis=1)
            tot = tot + nt(cat, wq[:, pair * W3 : (pair + 1) * W3])
        dctx[r, :] = tot.astype(bf)
    give = pltpu.make_async_copy(dctx, ig_h, ts.at[0])
    give.start()
    for c in slots:
        pass
    cX = []
    for a in range(8):
        cX.append(red.go_x(fin_a.at[a, pl.ds(pl.multiple_of(far * 24, 8), 24), :], rx_a.at[a], xs.at[a], xr.at[a], p.sib))
    for t in range(3):
        cX.append(red.go_x(fin_d.at[t, pl.ds(pl.multiple_of(far * 96, 8), 96), :], rx_d.at[t], xs.at[8 + t], xr.at[8 + t], p.sib))
    part = jnp.sum(jnp.sum(red.squares, axis=1, keepdims=True), axis=0, keepdims=True)
    tile[0] = jnp.broadcast_to(part, (8, 128))
    cN = [red.go_x(tile.at[0], nb1.at[j], ns.at[j], nr.at[j], p.zp[j]) for j in range(3)]
    for c in cN:
        c.wait_recv()
    zsum = jnp.zeros((8, 128), f32)
    for zz in range(4):
        term = tile[0]
        for j in range(3):
            term = jnp.where((p.z + 3 - j) % 4 == zz, nb1[j], term)
        zsum = zsum + term
    tile[1] = zsum
    cN = [red.go_x(tile.at[1], nb2.at[j], ns.at[3 + j], nr.at[3 + j], p.others[j]) for j in range(7)]
    my24 = pl.ds(pl.multiple_of(k * 24, 8), 24)
    for c in cX:
        c.wait_recv()
    for src, side in ((lambda a: fin_a[a, my24, :], k), (lambda a: rx_a[a], far)):
        for t in range(4):
            s_in[:, half(W3, t + 4 * side)] = src(t)
        s_out[:, half(W3, side)] = src(4)
        for t in range(3):
            term = src(5 + t)
            for j in range(3):
                s_qkv[j, :, half(128, 3 * side + t)] = term[:, j * 128 : (j + 1) * 128]
    my96 = pl.ds(pl.multiple_of(k * 96, 8), 96)
    for t in range(3):
        s_down[:, half(128, 3 * k + t)] = fin_d[t, my96, :]
        s_down[:, half(128, 3 * far + t)] = rx_d[t]
    for c in cN:
        c.wait_recv()
    msum = jnp.zeros((8, 128), f32)
    for mm in range(8):
        term = tile[1]
        for j in range(7):
            term = jnp.where((p.m + 7 - j) % 8 == mm, nb2[j], term)
        msum = msum + term
    total[...] = msum
    for c in red.sent:
        c.wait_send()
    give.wait()


def landing(lead, rows, w):
    shapes = ((rows, w), (2, rows // 4, w), (rows // 4, w), (3, rows // 16, w))
    return [pltpu.VMEM(lead + shape, bf) for shape in shapes]


def backward(lengths, tok, wqkv, dh1, q, k, v, dctx, ctx, lse, vg, gwo, gwi, gw2, block=512):
    vb = lambda *shape: pltpu.VMEM(shape, bf)
    vf = lambda *shape: pltpu.VMEM(shape, f32)
    dma = lambda *shape: pltpu.SemaphoreType.DMA(shape)
    return pl.pallas_call(
        functools.partial(backward_kernel, block),
        in_specs=[SMEM] + [ANY] * 8 + [VM] * 2 + [ANY] * 3,
        out_specs=[ANY] + [VM] * 6,
        out_shape=[S((T, D), bf), S((3, 24, D), f32), S((24, D), f32), S((24, FF), f32), S((96, D), f32), S((24, 128), f32), S((8, 128), f32)],
        scratch_shapes=[
            vb(T, 128), vb(T, 128),
            vb(T, D), vb(D, 3 * D), vf(T, D), vb(T, D), vb(T, D), vb(T, D), vb(T, D), vf(T, D), vb(3, 2, D, W3), vb(D, 128), vf(16, D),
        ]
        + BACK_SCRATCH + [vb(D, T)]
        + [vb(5, D, W3)] + landing((8,), D, W3) + [vb(3, FF, 128)] + landing((3,), FF, 128) + [vb(D, 128)] + landing((), D, 128)
        + [
            vf(8, 48, W3), vf(3, 192, 128), vf(8, 24, W3), vf(3, 96, 128), vf(2, 8, 128), vf(3, 8, 128), vf(7, 8, 128),
            dma(12, 7), dma(12, 7), dma(8), dma(11), dma(11), dma(10), dma(10), dma(5, 6), dma(3),
        ],
        compiler_params=pltpu.CompilerParams(collective_id=1, has_side_effects=True, vmem_limit_bytes=62 * MIB),
        name="backward",
    )(lengths, tok, wqkv, dh1, q, k, v, dctx, ctx, lse, vg, gwo, gwi, gw2)


def gelu_parts(x):
    e = jnp.exp(x * x * (-0.5))
    t = 1.0 / (1.0 + (0.3275911 * 0.7071067811865476) * jnp.abs(x))
    poly = 0.5 * 1.061405429
    for a in (-1.453152027, 1.421413741, -0.284496736, 0.254829592):
        poly = 0.5 * a + t * poly
    tail = t * poly * e
    return jnp.where(x >= 0, 1.0 - tail, tail), e * 0.3989422804014327


def norm_forward(h):
    c = h - jnp.mean(h, axis=1, keepdims=True)
    r = lax.rsqrt(jnp.mean(c * c, axis=1, keepdims=True) + norm_epsilon)
    return c * r, r


def norm_backward(dy, xh, r, g):
    dx = dy * g
    return r * (dx - jnp.mean(dx, axis=1, keepdims=True) - xh * jnp.mean(dx * xh, axis=1, keepdims=True))


def ffn_kernel(
    block, tok, ctx, cot, vec, wo_h, wi_h, w2_h, out_o, dh1_o, dctx_o, vg_o, gwo_h, gwi_h, gw2_h,
    wo, wi, w2, cb, x1b, hb, gp, dfb, dhp, dab, stage, tr, insem, outsem,
):
    loads = [
        pltpu.make_async_copy(wo_h, wo, insem.at[0]),
        pltpu.make_async_copy(wi_h, wi, insem.at[1]),
        pltpu.make_async_copy(w2_h, w2, insem.at[2]),
    ]
    for c in loads:
        c.start()
    vg_o[...] = jnp.zeros_like(vg_o)
    row = lambda i: vec[i : i + 1, :]
    for c in loads:
        c.wait()

    def one_block(b, carry):
        r = pl.ds(pl.multiple_of(b * block, block), block)
        c = ctx[r, :].astype(bf)
        cb[r, :] = c
        xh1, r1 = norm_forward(tok[r, :].astype(f32) + (nn(c, wo[...]) + row(2)))
        x1 = xh1 * row(4) + row(5)
        xb = x1.astype(bf)
        x1b[r, :] = xb
        acc = x1 + row(3)
        for j in range(4):
            cs = slice(j * D, (j + 1) * D)
            hp = nn(xb, wi[:, cs]) + row(8 + j)
            big, dense = gelu_parts(hp)
            h = (hp * big).astype(bf)
            hb[r, cs] = h
            gp[:, cs] = big + hp * dense
            acc = acc + nn(h, w2[cs, :])
        xh2, r2 = norm_forward(acc)
        out_o[r, :] = (xh2 * row(6) + row(7)).astype(bf)
        dy = cot[r, :].astype(f32)
        vg_o[6:7, :] += colsum(dy * xh2)
        vg_o[7:8, :] += colsum(dy)
        dh2 = norm_backward(dy, xh2, r2, row(6))
        df = dh2.astype(bf)
        dfb[r, :] = df
        vg_o[3:4, :] += colsum(df.astype(f32))
        dx1 = dh2
        for j in range(4):
            cs = slice(j * D, (j + 1) * D)
            dh = (gp[:, cs] * nt(df, w2[cs, :])).astype(bf)
            dhp[r, cs] = dh
            vg_o[8 + j : 9 + j, :] += colsum(dh.astype(f32))
            dx1 = dx1 + nt(dh, wi[:, cs])
        vg_o[4:5, :] += colsum(dx1 * xh1)
        vg_o[5:6, :] += colsum(dx1)
        dh1 = norm_backward(dx1, xh1, r1, row(4))
        dh1_o[r, :] = dh1
        da = dh1.astype(bf)
        dab[r, :] = da
        vg_o[2:3, :] += colsum(da.astype(f32))
        dctx_o[r, :] = nt(da, wo[...]).astype(bf)
        return carry

    lax.fori_loop(0, T // block, one_block, 0)
    outs = []

    def emit(val, dst):
        i = len(outs)
        if i >= 2:
            outs[i - 2].wait()
        stage[i % 2] = val.astype(bf)
        c = pltpu.make_async_copy(stage.at[i % 2], dst, outsem.at[i % 2])
        c.start()
        outs.append(c)

    for j in range(4):
        cs = slice(j * D, (j + 1) * D)
        emit(tn(hb[:, cs], dfb[...]), gw2_h.at[cs, :])
    tr[...] = x1b[...].T
    for j in range(4):
        cs = slice(j * D, (j + 1) * D)
        emit(nn(tr[...], dhp[:, cs]), gwi_h.at[:, cs])
    emit(tn(cb[...], dab[...]), gwo_h)
    outs[7].wait()
    outs[8].wait()


def feed_forward(tok, ctx, cot, vec, wo, wi, w2, block=256):
    return pl.pallas_call(
        functools.partial(ffn_kernel, block),
        in_specs=[VM] * 4 + [ANY] * 3,
        out_specs=[VM] * 4 + [ANY] * 3,
        out_shape=[
            S((T, D), bf), S((T, D), f32), S((T, D), bf), S((16, D), f32), S((D, D), bf), S((D, FF), bf), S((FF, D), bf),
        ],
        scratch_shapes=[
            pltpu.VMEM((D, D), bf), pltpu.VMEM((D, FF), bf), pltpu.VMEM((FF, D), bf), pltpu.VMEM((T, D), bf),
            pltpu.VMEM((T, D), bf), pltpu.VMEM((T, FF), bf), pltpu.VMEM((block, FF), f32), pltpu.VMEM((T, D), bf),
            pltpu.VMEM((T, FF), bf), pltpu.VMEM((T, D), bf), pltpu.VMEM((2, D, D), bf), pltpu.VMEM((D, T), bf),
            pltpu.SemaphoreType.DMA((3,)), pltpu.SemaphoreType.DMA((2,)),
        ],
        compiler_params=pltpu.CompilerParams(vmem_limit_bytes=60 * MIB),
        name="feed_forward",
    )(tok, ctx, cot, vec, wo, wi, w2)


def middle_kernel(
    block, low_h, cot_h, vec_h, wo_h, wi_h, w2_h, hb_h, gp_h, xh_h, sd, xb_h, out_h, dh1_h, dctx_h, vg, gwo_h, gwi_h, gw2_h,
    vec, wo, wi, w2, cb, out, cot, xh1, x1b, hb, gp, hT, dfb, dh, dab, turned, go, ls, os,
):
    moves = (
        (w2_h, w2), (hb_h, hb), (xh_h, xh1), (vec_h, vec), (cot_h, cot), (gp_h, gp), (wi_h, wi), (wo_h, wo), (xb_h, x1b), (low_h, cb),
    )
    loads = [pltpu.make_async_copy(src, dst, ls.at[i]) for i, (src, dst) in enumerate(moves)]
    for c in loads:
        c.start()
    vg[...] = jnp.zeros_like(vg)
    row = lambda i: vec[i : i + 1, :]
    rows = [slice(b * block, (b + 1) * block) for b in range(T // block)]
    quarter = [slice(j * D, (j + 1) * D) for j in range(4)]
    outs = []

    def give(src, dst):
        outs.append(pltpu.make_async_copy(src, dst, os.at[len(outs)]))
        outs[-1].start()

    for c in loads[:5]:
        c.wait()
    for r in rows:
        acc = xh1[r, :] * row(4) + row(5) + (nn(hb[r, :], w2[...]) + row(3))
        xh2, r2d = norm_forward(acc)
        out[r, :] = (xh2 * row(6) + row(7)).astype(bf)
        dy = cot[r, :].astype(f32)
        vg[6:7, :] += colsum(dy * xh2)
        vg[7:8, :] += colsum(dy)
        dh2 = norm_backward(dy, xh2, r2d, row(6))
        dh[r, :] = dh2
        df = dh2.astype(bf)
        dfb[r, :] = df
        vg[3:4, :] += colsum(df.astype(f32))
    give(out, out_h)
    for cs in quarter:
        hT[cs, :] = hb[:, cs].T
    for c in loads[5:]:
        c.wait()
    for r in rows:
        df = dfb[r, :]
        for j, cs in enumerate(quarter):
            low = (gp[r, cs] * nt(df, w2[cs, :])).astype(bf)
            hb[r, cs] = low
            vg[8 + j : 9 + j, :] += colsum(low.astype(f32))
        dx1 = dh[r, :] + nt(hb[r, :], wi[...])
        xh = xh1[r, :]
        vg[4:5, :] += colsum(dx1 * xh)
        vg[5:6, :] += colsum(dx1)
        dh1 = norm_backward(dx1, xh, sd[r, 0:1], row(4))
        dh[r, :] = dh1
        da = dh1.astype(bf)
        dab[r, :] = da
        vg[2:3, :] += colsum(da.astype(f32))
        cot[r, :] = nt(da, wo[...]).astype(bf)
    give(dh, dh1_h)
    give(cot, dctx_h)
    for cs in quarter:
        w2[cs, :] = nn(hT[cs, :], dfb[...]).astype(bf)
        give(w2.at[cs, :], gw2_h.at[cs, :])
    turned[...] = x1b[...].T
    for cs in quarter:
        wi[:, cs] = nn(turned[...], hb[:, cs]).astype(bf)
        give(wi.at[:, cs], gwi_h.at[:, cs])
    turned[...] = cb[...].T
    go[...] = nn(turned[...], dab[...]).astype(bf)
    give(go, gwo_h)
    for c in outs:
        c.wait()


def middle(low, cot, vec, wo, wi, w2, hb, gp, xh, sd, xb, block=256):
    vb = lambda *shape: pltpu.VMEM(shape, bf)
    vf = lambda *shape: pltpu.VMEM(shape, f32)
    dma = lambda *shape: pltpu.SemaphoreType.DMA(shape)
    return pl.pallas_call(
        functools.partial(middle_kernel, block),
        in_specs=[ANY] * 9 + [VM] + [ANY],
        out_specs=[ANY] * 3 + [VM] + [ANY] * 3,
        out_shape=[
            S((T, D), bf), S((T, D), f32), S((T, D), bf), S((16, D), f32), S((D, D), bf), S((D, FF), bf), S((FF, D), bf),
        ],
        scratch_shapes=[
            vf(128, D), vb(D, D), vb(D, FF), vb(FF, D), vb(T, D), vb(T, D), vb(T, D), vf(T, D), vb(T, D),
            vb(T, FF), vf(T, FF), vb(FF, T), vb(T, D), vf(T, D), vb(T, D), vb(D, T), vb(D, D), dma(10), dma(12),
        ],
        compiler_params=pltpu.CompilerParams(vmem_limit_bytes=62 * MIB),
        name="middle",
    )(low, cot, vec, wo, wi, w2, hb, gp, xh, sd, xb)


def adam_step(weight, gradient, first_old, second_old, decay_rate, step_rate):
    first_new = moment_decay * first_old + (1.0 - moment_decay) * gradient
    second_new = square_decay * second_old + (1.0 - square_decay) * gradient * gradient
    first_hat = first_new / (1.0 - moment_decay**STEP)
    second_hat = second_new / (1.0 - square_decay**STEP)
    weight_new = weight - step_rate * (first_hat / (jnp.sqrt(second_hat) + adam_epsilon) + decay_rate * weight)
    return (weight_new, first_new, second_new)


def update_kernel(total, *refs):
    hbm, outs, scratch = refs[0:21], refs[21:38], refs[38:]
    bufs, sem = scratch[:20], scratch[20]
    ig_in, w, g, m, u = hbm[0], bufs[0:5], bufs[5:10], bufs[10:15], bufs[15:20]
    ig_out, norm_o, new, first, second = outs[0], outs[1], outs[2:7], outs[7:12], outs[12:17]
    through = pltpu.make_async_copy(ig_in, ig_out, sem.at[20])
    through.start()
    loads = [pltpu.make_async_copy(hbm[1 + i], bufs[i], sem.at[i]) for i in range(20)]
    for c in loads:
        c.start()
    norm = jnp.sqrt(total[...])
    norm_o[0, 0] = norm[0, 0]
    factor = jnp.minimum(1.0, clip_limit / (norm + 1e-06))[0:1, 0:1]
    for c in loads:
        c.wait()
    for i in range(4):
        n, f, s = adam_step(w[i][...], factor * g[i][...], m[i][...], u[i][...], weight_decay, learn_rate)
        new[i][...] = n
        first[i][...] = f
        second[i][...] = s
    wide = jnp.concatenate([g[4][...], jnp.zeros((104, 128), f32)], axis=0).T[:12, :24]
    n, f, s = adam_step(w[4][...], factor * wide, m[4][...], u[4][...], 0.0, vector_rate)
    new[4][...] = n
    first[4][...] = f
    second[4][...] = s
    through.wait()


def update(total, input_grad, weights, grads, firsts, seconds):
    shapes = [S(w.shape, f32) for w in weights]
    arrays = (*weights, *grads, *firsts, *seconds)
    return pl.pallas_call(
        update_kernel,
        in_specs=[VM] + [ANY] * 21,
        out_specs=[VM, SMEM] + [VM] * 15,
        out_shape=[S(input_grad.shape, bf), S((1, 1), f32)] + shapes * 3,
        scratch_shapes=[pltpu.VMEM(a.shape, f32) for a in arrays] + [pltpu.SemaphoreType.DMA((21,))],
        compiler_params=pltpu.CompilerParams(vmem_limit_bytes=60 * MIB),
        name="clip_and_update",
    )(total, input_grad, *arrays)


def segment_ids(lengths):
    bounds = jnp.cumsum(lengths, axis=-1)
    places = jnp.arange(T, dtype=jnp.int32)
    return jnp.sum((places[:, None] >= bounds[None, :]).astype(jnp.int32), axis=-1)


def pairs_last(a):
    return a.reshape(3, D, PAIRS, 128).transpose(1, 2, 0, 3).reshape(D, 3 * D)


def per_device(
    small, tokens, cotangent, lengths, qkv_weight, out_weight, in_weight, down_weight, vectors,
    qkv_first, out_first, in_first, down_first, vec_first, qkv_second, out_second, in_second, down_second, vec_second,
):
    weights = (qkv_weight, out_weight, in_weight, down_weight, vectors)
    firsts = (qkv_first, out_first, in_first, down_first, vec_first)
    seconds = (qkv_second, out_second, in_second, down_second, vec_second)
    axes = ("dp", "fsdp")
    if small:
        wqkv, wo, wi, w2, vec, q, k, v, ctx, low, lse, *kept = forward(tokens, lengths, weights)
        result, dh1, dctx, vg, gwo, gwi, gw2 = middle(low, cotangent, vec, wo, wi, w2, *kept)
        ig, *grads, total = backward(lengths, tokens, wqkv, dh1, q, k, v, dctx, ctx, lse, vg, gwo, gwi, gw2)
        updated = update(total, ig, weights, grads, firsts, seconds)
        return (result, updated[0], updated[1].reshape(()), *updated[2:])
    seg = segment_ids(lengths[0])
    lane = jnp.arange(128)
    match = seg[:, None] == lane[None, :]
    onehot = match.astype(bf)
    neg = jnp.where(match | (lane >= lengths.shape[1])[None, :], 0.0, -1e30).astype(bf)
    gather = lambda a, axis: lax.all_gather(a.astype(bf), axes, axis=axis, tiled=True)
    wqkv = pairs_last(gather(qkv_weight, 1))
    wo, wi, w2 = gather(out_weight, 0), gather(in_weight, 0), gather(down_weight, 0)
    vec = jnp.concatenate([gather(vectors, 1).astype(f32), jnp.zeros((4, D), f32)], axis=0)
    bias = jnp.stack([vec[0], jnp.zeros_like(vec[0]), vec[1]]).reshape(3, PAIRS, 128).transpose(1, 0, 2).reshape(1, 3 * D)
    q, k, v, ctx, lse = attend(tokens, wqkv, bias, onehot, neg)
    result, dh1, dctx, vg, gwo, gwi, gw2 = feed_forward(tokens, ctx, cotangent, vec, wo, wi, w2)
    gqkv, input_grad, vg_qv = attend_back(tokens, wqkv, dh1, q, k, v, dctx, ctx, lse, onehot, neg)
    vg = vg + vg_qv
    scatter = lambda a, axis: lax.psum_scatter(a.astype(f32), axes, scatter_dimension=axis, tiled=True)
    gqkv = gqkv.reshape(D, PAIRS, 3, 128).transpose(2, 0, 1, 3).reshape(3, D, D)
    grads = (scatter(gqkv, 1), scatter(gwo, 0), scatter(gwi, 0), scatter(gw2, 0), scatter(vg[:12], 1))
    grad_norm = jnp.sqrt(lax.psum(sum(jnp.sum(g * g) for g in grads), axes))
    factor = jnp.minimum(1.0, clip_limit / (grad_norm + 1e-06))
    updated = []
    for i in range(5):
        rates = (0.0, vector_rate) if i == 4 else (weight_decay, learn_rate)
        updated.append(adam_step(weights[i], factor * grads[i], firsts[i], seconds[i], *rates))
    return (result, input_grad, grad_norm, *[u[j] for j in range(3) for u in updated])


def solution(mesh):
    rows = P(("dp", "fsdp"), None)
    deep = P(None, ("dp", "fsdp"), None)
    wide = P(None, ("dp", "fsdp"))
    group = (deep, rows, rows, rows, wide)
    small = mesh.shape["dp"] == 4 and mesh.shape["fsdp"] == 8
    return jax.shard_map(
        functools.partial(per_device, small),
        mesh=mesh,
        in_specs=(rows, rows, rows) + group * 3,
        out_specs=(rows, rows, P()) + group * 3,
        check_vma=False,
    )
```

```python
import functools

import jax
import jax.numpy as jnp
from jax import lax
from jax.experimental import pallas as pl
from jax.experimental.pallas import tpu as pltpu
from jax.sharding import PartitionSpec as P

D = 768
H = 12
HD = 64
FF = 3072
T = 1024
STEP = 10
PAIRS = H // 2
W3 = 384

moment_decay = 0.9
square_decay = 0.999
learn_rate = 0.02
vector_rate = 0.15
weight_decay = 0.01
adam_epsilon = 1e-08
clip_limit = 1.0
norm_epsilon = 1e-05

bf = jnp.bfloat16
f32 = jnp.float32
MESH = pl.DeviceIdType.MESH
VM = pl.BlockSpec(memory_space=pltpu.VMEM)
ANY = pl.BlockSpec(memory_space=pl.ANY)
MIB = 2**20


def S(shape, dtype):
    return jax.ShapeDtypeStruct(shape, dtype)


def nn(a, b):
    return lax.dot_general(a, b, (((1,), (0,)), ((), ())), preferred_element_type=f32)


def nt(a, b):
    return lax.dot_general(a, b, (((1,), (1,)), ((), ())), preferred_element_type=f32)


def tn(a, b):
    return lax.dot_general(a, b, (((0,), (0,)), ((), ())), preferred_element_type=f32)


def colsum(x):
    return jnp.sum(x, axis=0, keepdims=True)


class Place:
    def __init__(self):
        self.dp = lax.axis_index("dp")
        self.fs = lax.axis_index("fsdp")
        self.z = self.fs // 2
        self.k = self.fs % 2
        dp, k = self.dp, self.k
        xn = dp + 1 - 2 * (dp % 2)
        yn = (dp + 2) % 4
        self.dp1 = xn * (1 - k) + yn * k
        self.dp2 = yn * (1 - k) + xn * k
        self.dp3 = 3 - dp
        self.n1 = (self.dp1, self.fs)
        self.n2 = (self.dp2, self.fs)
        self.sib = (dp, self.z * 2 + 1 - k)
        self.zp = [(dp, ((self.z + i) % 4) * 2 + k) for i in (1, 2, 3)]
        self.m = dp * 2 + k
        self.others = []
        for j in range(1, 8):
            other = (self.m + j) % 8
            self.others.append((other // 2, self.z * 2 + other % 2))


def enter(peers):
    barrier = pltpu.get_barrier_semaphore()
    for peer in peers:
        pl.semaphore_signal(barrier, inc=1, device_id=peer, device_id_type=MESH)
    pl.semaphore_wait(barrier, len(peers))


def rcopy(src, dst, ssem, rsem, peer):
    return pltpu.make_async_remote_copy(src, dst, ssem, rsem, device_id=peer, device_id_type=MESH)


def half(w, c):
    return pl.ds(pl.multiple_of(c * w, 128), w)


def band(rows, index):
    return pl.ds(pl.multiple_of(rows * index, 16), rows)


def masks(lengths, onehot, neg):
    lane = lax.broadcasted_iota(jnp.int32, (1, 128), 1)
    first = jnp.full((1, 128), T, jnp.int32)
    after = jnp.full((1, 128), T, jnp.int32)
    total = jnp.int32(0)
    count = lengths.shape[1]
    for j in range(count):
        first = jnp.where(lane == j, total, first)
        total = total + lengths[0, j]
        after = jnp.where(lane == j, total, after)
    row = lax.broadcasted_iota(jnp.int32, (T, 128), 0)
    own = (row >= first) & (row < after)
    onehot[...] = jnp.where(own, 1.0, 0.0).astype(bf)
    neg[...] = jnp.where(own | (lane >= count), 0.0, -1e30).astype(bf)


PACE_FORWARD = 6.0
PACE_BACKWARD = 6.5


ORDER = (0, 3, 1, 4, 2, 5)


MIXED = (4, 7, 10)


class Gather:
    def __init__(self, p, chunks, gs, gr):
        self.p, self.chunks, self.gs, self.gr = p, chunks, gs, gr
        self.sent = []

    def go(self, part, j, rows, peer):
        n, ref, rc, cols, swap, mixed = part
        view = ref.at[rows, cols]
        c = rcopy(view, view, self.gs.at[n, j], self.gr.at[n, j], peer)
        c.start()
        self.sent.append(c)
        return c

    def slots(self, ahead):
        p, n = self.p, len(self.chunks)
        c0, c1, c2, c3, c4 = {}, {}, {}, {}, {}

        def more(i):
            if i < n:
                c0[i] = []
                for part in self.chunks[i]:
                    own = band(part[2], p.dp * 4 + p.z)
                    c0[i].append([self.go(part, 3, own, p.n1)] if part[5] else [self.go(part, j, own, p.zp[j]) for j in range(3)])

        def links(i):
            if 0 <= i < n:
                c1[i], c2[i] = [], []
                for q, part in enumerate(self.chunks[i]):
                    rc = part[2]
                    for c in c0[i][q]:
                        c.wait_recv()
                    if part[5]:
                        c1[i].append([
                            self.go(part, j + 7 * h, band(rc, d * 4 + p.z), p.zp[j]) for j in range(3) for h, d in enumerate((p.dp, p.dp1))
                        ])
                    else:
                        c1[i].append([self.go(part, 3, band(4 * rc, p.dp), p.n1)])
                        c2[i].append(self.go(part, 4, band(4 * rc, p.dp), p.n2))

        def cross(i):
            if 0 <= i < n:
                c3[i] = []
                for q, part in enumerate(self.chunks[i]):
                    for c in c1[i][q]:
                        c.wait_recv()
                    if part[5]:
                        c2[i].append(self.go(part, 4, band(4 * part[2], p.dp), p.n2))
                    c3[i].append(self.go(part, 5, band(4 * part[2], p.dp1), p.n2))

        def swap(i):
            if 0 <= i < n:
                c4[i] = []
                for q, part in enumerate(self.chunks[i]):
                    c2[i][q].wait_recv()
                    c3[i][q].wait_recv()
                    if part[4]:
                        c4[i].append(self.go(part, 6, pl.ds(0, 16 * part[2]), p.sib))

        def take(i):
            if 0 <= i < n:
                for c in c4[i]:
                    c.wait_recv()

        for i in range(3):
            more(i)
        yield -1
        for i in range(3, ahead):
            more(i)
        links(0)
        cross(0)
        links(1)
        swap(0)
        links(2)
        more(ahead)
        take(0)
        cross(1)
        links(3)
        more(ahead + 1)
        yield 0
        for t in range(1, n + 2):
            more(t + ahead + 1)
            links(t + 3)
            cross(t + 1)
            if t != 2:
                swap(max(t - 1, 1))
            if t == 2 or t > 3:
                take(max(t - 2, 1))
            yield max(t - 2, min(t - 1, 1))
        for c in self.sent:
            c.wait_send()
        yield n


def forward_kernel(
    block, tok_h, lengths, qkv, out, inw, down, vec,
    wqkv_h, wo_h, wi_h, w2, vrow, qkv_h, ctx_h, lse, hb_h, gp_h, xh_h, sd, tokT_h, lowT_h, xbT_h, hbT_h,
    tok, wq, vt, qkvs, ctx, low, qa, ka, va, onehot, neg,
    m_qkv, m_out, m_in, m_down, m_vec, x_qkv, x_out, x_in, x_down, x_vec, myvec,
    own_down, wo, wi, hb, gp, xh, xb, hbT, turned, xs, xr, gs, gr, ls, os, fs,
):
    p = Place()
    k = p.k
    far = 1 - k
    loads = [
        pltpu.make_async_copy(vec, m_vec, ls.at[4]),
        pltpu.make_async_copy(qkv.at[:, :, half(W3, k)], m_qkv, ls.at[0]),
        pltpu.make_async_copy(out.at[:, half(W3, k)], m_out, ls.at[1]),
        pltpu.make_async_copy(inw.at[:, half(4 * W3, k)], m_in, ls.at[2]),
        pltpu.make_async_copy(down.at[:, half(W3, k)], m_down, ls.at[3]),
        pltpu.make_async_copy(tok_h, tok, ls.at[5]),
    ]
    for c in loads:
        c.start()
    enter([p.sib, p.n1, p.n2] + p.zp)
    swaps = [
        rcopy(qkv.at[:, :, half(W3, far)], x_qkv, xs.at[0], xr.at[0], p.sib),
        rcopy(out.at[:, half(W3, far)], x_out, xs.at[1], xr.at[1], p.sib),
        rcopy(inw.at[:, half(4 * W3, far)], x_in, xs.at[2], xr.at[2], p.sib),
        rcopy(down.at[:, half(W3, far)], x_down, xs.at[3], xr.at[3], p.sib),
        rcopy(myvec, x_vec, xs.at[4], xr.at[4], p.sib),
    ]
    for c in swaps[:4]:
        c.start()
    loads[0].wait()
    pad = jnp.concatenate([m_vec[...], jnp.zeros((128 - 12, 24), f32)], axis=0)
    myvec[...] = jnp.concatenate([pad, jnp.zeros((128, 104), f32)], axis=1).T[:24, :]
    swaps[4].start()

    def both(mine, other):
        lo = jnp.where(k == 0, mine, other)
        hi = jnp.where(k == 0, other, mine)
        return jnp.concatenate([lo, hi], axis=0).astype(bf)

    chip = p.dp * 4 + p.z
    loads[1].wait()
    swaps[0].wait_recv()
    for j in range(3):
        mat = both(m_qkv[j], x_qkv[j])
        for t in range(3):
            wq[band(48, chip), pl.ds(pl.multiple_of((2 * t + k) * W3 + j * 128, 128), 128)] = mat[:, t * 128 : (t + 1) * 128]
    swaps[4].wait_recv()
    vt[band(48, chip), :] = both(myvec[...], x_vec[...])

    chunks = []
    places = [(wq, 48, half(W3, 2 * t + k)) for t in range(3)] + [(wo, 48, half(W3, k))]
    places += [(wi, 48, half(W3, t + 4 * k)) for t in range(4)]
    places += [(w2, 192, half(128, 3 * k + t)) for t in range(3)]
    for ref, rc, cs in places:
        chunks.append([(len(chunks), ref, rc, cs, True, len(chunks) in MIXED)])
    chunks[0].append((11, vt, 48, pl.ds(0, 128), False, False))
    gather = Gather(p, chunks, gs, gr)
    slots = gather.slots(5)
    done = [next(slots)]
    for i in range(3):
        loads[2 + i].wait()
        swaps[1 + i].wait_recv()
    wo[band(48, chip), half(W3, k)] = both(m_out[...], x_out[...])
    wi[band(48, chip), half(4 * W3, k)] = both(m_in[...], x_in[...])
    own_down[...] = both(m_down[...], x_down[...])
    local = pltpu.make_async_copy(own_down, w2.at[band(192, chip), half(W3, k)], ls.at[3])
    local.start()
    local.wait()
    loads[5].wait()
    masks(lengths, onehot, neg)
    outs = []

    def give(src, dst, sem):
        outs.append(pltpu.make_async_copy(src, dst, sem))
        outs[-1].start()

    turned[0] = tok[...].T
    give(turned.at[0], tokT_h, ls.at[6])

    def upto(i):
        while done[0] < i:
            done[0] = next(slots, len(chunks))

    spent = [0.0]

    def spend(us):
        spent[0] += us
        if spent[0] >= PACE_FORWARD and done[0] < len(chunks) - 1:
            spent[0] -= PACE_FORWARD
            done[0] = next(slots)

    upto(0)
    vrow[...] = vt[...].astype(f32).T
    lane = lax.broadcasted_iota(jnp.int32, (1, 128), 1)
    ka[:, 128:] = neg[...]
    va[:, 128:] = jnp.ones((T, 128), bf)
    qa[:, 128:] = onehot[...]
    for turn, pair in enumerate(ORDER):
        upto(turn // 2)
        spend(0.8)
        cs = slice(pair * 128, (pair + 1) * 128)
        y = nn(tok[...], wq[:, turn * W3 : (turn + 1) * W3])
        q = (y[:, :128] + vrow[0:1, cs]).astype(bf)
        key = y[:, 128:256].astype(bf)
        val = (y[:, 256:] + vrow[1:2, cs]).astype(bf)
        us = slice(turn * W3, (turn + 1) * W3)
        for j, part in enumerate((q, key, val)):
            qkvs[:, turn * W3 + j * 128 : turn * W3 + (j + 1) * 128] = part
        give(qkvs.at[:, us], qkv_h.at[:, us], os.at[0, pair])
        qs = (q.astype(f32) * HD ** (-0.5)).astype(bf)
        ka[:, :128] = key
        va[:, :128] = val
        for h in range(2):
            sel = (lane // 64) == h
            qa[:, :128] = jnp.where(sel, qs, jnp.zeros_like(qs))
            for b in range(T // block):
                r = slice(b * block, (b + 1) * block)
                s = nt(qa[r, :], ka[...])
                m = jnp.max(s, axis=1, keepdims=True)
                e = jnp.exp(s - m).astype(bf)
                o = nn(e, va[...])
                tot = o[:, 128:]
                c = o[:, :128] / tot
                l = m + jnp.log(tot)
                ctx[r, cs] = c if h == 0 else jnp.where(sel, c, ctx[r, cs])
                lse[r, :] = l if turn + h == 0 else jnp.where(lane == 2 * pair + h, l, lse[r, :])
                spend(0.55)
        low[:, cs] = ctx[:, cs].astype(bf)
        give(ctx.at[:, cs], ctx_h.at[:, cs], os.at[1, pair])
    give(wq, wqkv_h, ls.at[0])
    row = lambda i: vrow[i : i + 1, :]
    rows = [slice(b * 256, (b + 1) * 256) for b in range(4)]
    turned[1] = low[...].T
    give(turned.at[1], lowT_h, ls.at[4])
    spend(1.5)
    upto(3)
    for r in rows:
        spend(0.7)
        xhat, rd = norm_forward(tok[r, :].astype(f32) + (nn(low[r, :], wo[...]) + row(2)))
        xh[r, :] = xhat
        sd[r, :] = jnp.broadcast_to(rd, (256, 128))
        xb[r, :] = (xhat * row(4) + row(5)).astype(bf)
    give(wo, wo_h, ls.at[1])
    give(xh, xh_h, ls.at[2])
    turned[2] = xb[...].T
    give(turned.at[2], xbT_h, ls.at[3])
    spend(1.5)
    for j in (0, 2, 1, 3):
        upto(5 if j % 2 == 0 else 7)
        cs = slice(j * D, (j + 1) * D)
        for r in rows:
            hp = nn(xb[r, :], wi[:, cs]) + row(8 + j)
            big, dense = gelu_parts(hp)
            hb[r, cs] = (hp * big).astype(bf)
            gp[r, cs] = big + hp * dense
            spend(0.7)
        give(hb.at[:, cs], hb_h.at[:, cs], fs.at[0, j])
        give(gp.at[:, cs], gp_h.at[:, cs], fs.at[1, j])
        hbT[cs, :] = hb[:, cs].T
        give(hbT.at[cs, :], hbT_h.at[cs, :], fs.at[2, j])
        spend(1.5)
    give(wi, wi_h, ls.at[5])
    for c in slots:
        pass
    for c in swaps:
        c.wait_send()
    for c in outs:
        c.wait()


SMEM = pl.BlockSpec(memory_space=pltpu.SMEM)


def forward(tok, lengths, weights, block=256):
    vb = lambda *shape: pltpu.VMEM(shape, bf)
    vf = lambda *shape: pltpu.VMEM(shape, f32)
    dma = lambda *shape: pltpu.SemaphoreType.DMA(shape)
    return pl.pallas_call(
        functools.partial(forward_kernel, block),
        in_specs=[ANY, SMEM] + [ANY] * 5,
        out_specs=[ANY] * 4 + [VM] + [ANY] * 2 + [VM] + [ANY] * 3 + [VM] + [ANY] * 4,
        out_shape=[S((D, 3 * D), bf), S((D, D), bf), S((D, FF), bf), S((FF, D), bf), S((128, D), f32)]
        + [S((T, 3 * D), bf), S((T, D), f32), S((T, 128), f32)]
        + [S((T, FF), bf), S((T, FF), f32), S((T, D), f32), S((T, 128), f32)]
        + [S((D, T), bf)] * 3 + [S((FF, T), bf)],
        scratch_shapes=[
            vb(T, D), vb(D, 3 * D), vb(D, 128), vb(T, 3 * D), vf(T, D), vb(T, D), vb(T, 256), vb(T, 256), vb(T, 256),
            vb(T, 128), vb(T, 128),
            vf(3, 24, W3), vf(24, W3), vf(24, 4 * W3), vf(96, W3), vf(12, 24),
            vf(3, 24, W3), vf(24, W3), vf(24, 4 * W3), vf(96, W3), vf(24, 128), vf(24, 128),
            vb(192, W3), vb(D, D), vb(D, FF), vb(T, FF), vf(T, FF), vf(T, D), vb(T, D), vb(FF, T), vb(3, D, T),
            dma(5), dma(5), dma(12, 10), dma(12, 10), dma(7), dma(2, 6), dma(3, 4),
        ],
        compiler_params=pltpu.CompilerParams(collective_id=0, has_side_effects=True, vmem_limit_bytes=60 * MIB),
        name="forward",
    )(tok, lengths, *weights)


def attend_kernel(block, tok, w, bias, onehot, neg, q_o, k_o, v_o, ctx_o, lse_o, qa, ka, va):
    lane = lax.broadcasted_iota(jnp.int32, (1, 128), 1)
    pair = pl.program_id(0)
    y = nn(tok[...], w[...]) + bias[...]
    q = y[:, :128].astype(bf)
    key = y[:, 128:256].astype(bf)
    val = y[:, 256:].astype(bf)
    q_o[...] = q
    k_o[...] = key
    v_o[...] = val
    qs = (q.astype(f32) * HD ** (-0.5)).astype(bf)
    ka[:, :128] = key
    ka[:, 128:] = neg[...]
    va[:, :128] = val
    va[:, 128:] = jnp.ones((T, 128), bf)
    qa[:, 128:] = onehot[...]
    for h in range(2):
        sel = (lane // 64) == h
        qa[:, :128] = jnp.where(sel, qs, jnp.zeros_like(qs))
        for b in range(T // block):
            r = slice(b * block, (b + 1) * block)
            s = nt(qa[r, :], ka[...])
            m = jnp.max(s, axis=1, keepdims=True)
            e = jnp.exp(s - m).astype(bf)
            o = nn(e, va[...])
            tot = o[:, 128:]
            c = o[:, :128] / tot
            l = m + jnp.log(tot)
            ctx_o[r, :] = c if h == 0 else jnp.where(sel, c, ctx_o[r, :])
            lse_o[r, :] = jnp.where(lane == 2 * pair + h, l, lse_o[r, :])


def attend(tok, w, bias, onehot, neg, block=256):
    full = lambda s: pl.BlockSpec(s, lambda i: (0,) * len(s))
    col = pl.BlockSpec((T, 128), lambda i: (0, i))
    return pl.pallas_call(
        functools.partial(attend_kernel, block),
        grid=(PAIRS,),
        in_specs=[
            full((T, D)), pl.BlockSpec((D, W3), lambda i: (0, i)), pl.BlockSpec((1, W3), lambda i: (0, i)),
            full((T, 128)), full((T, 128)),
        ],
        out_specs=[col, col, col, col, full((T, 128))],
        out_shape=[S((T, D), bf)] * 3 + [S((T, D), f32), S((T, 128), f32)],
        scratch_shapes=[pltpu.VMEM((T, 256), bf)] * 3,
        compiler_params=pltpu.CompilerParams(vmem_limit_bytes=60 * MIB),
        name="attend",
    )(tok, w, bias, onehot, neg)


def split3(x):
    hi = x.astype(bf).astype(f32)
    mid = (x - hi).astype(bf).astype(f32)
    return hi, mid, x - hi - mid


class Back:
    def __init__(self, block, onehot, neg, qa, ka, va, da, kT, dqT, dka, dva):
        self.block, self.onehot, self.neg = block, onehot, neg
        self.refs = (qa, ka, va, da, kT, dqT, dka, dva)
        self.lane = lax.broadcasted_iota(jnp.int32, (1, 128), 1)

    def start(self):
        qa, ka, va, da, kT, dqT, dka, dva = self.refs
        minus = jnp.where((self.lane >= 16) & (self.lane < 19), -1.0, 0.0)
        ka[:, 128:] = (self.neg[...].astype(f32) + minus).astype(bf)
        va[:, 128:] = jnp.broadcast_to(minus, (T, 128)).astype(bf)

    def pair(self, pair, q, key, val, d, ctx, lse, tick):
        lane, block = self.lane, self.block
        qa, ka, va, da, kT, dqT, dka, dva = self.refs
        qs = (q.astype(f32) * HD ** (-0.5)).astype(bf)
        ka[:, :128] = key
        va[:, :128] = val
        kT[...] = key.T
        prod = d.astype(f32) * ctx

        def extra(base, parts):
            for j, part in enumerate(parts):
                base = jnp.where(lane == 16 + j, part, base)
            return base.astype(bf)

        for h in range(2):
            sel = (lane // 64) == h
            inner = jnp.sum(jnp.where(sel, prod, 0.0), axis=1, keepdims=True)
            lsum = jnp.sum(jnp.where(lane == 2 * pair + h, lse, 0.0), axis=1, keepdims=True)
            qa[:, :128] = jnp.where(sel, qs, jnp.zeros_like(qs))
            qa[:, 128:] = extra(self.onehot[...].astype(f32), split3(lsum))
            da[:, :128] = jnp.where(sel, d, jnp.zeros_like(d))
            da[:, 128:] = extra(jnp.zeros((T, 128), f32), split3(inner))
            for b in range(T // block):
                r = slice(b * block, (b + 1) * block)
                pt = jnp.exp(nt(ka[...], qa[r, :]))
                dpt = nt(va[...], da[r, :])
                ds = (pt * dpt).astype(bf)
                x = nn(pt.astype(bf), da[r, :128])
                y = nn(ds, qa[r, :128])
                dqT[h * 64 : (h + 1) * 64, r] = nn(kT[h * 64 : (h + 1) * 64, :], ds)
                if h == 0 and b == 0:
                    dva[...] = x
                    dka[...] = y
                else:
                    dva[...] += x
                    dka[...] += y
                tick()
        dv = dva[...].astype(bf)
        dk = dka[...].astype(bf)
        dq = (dqT[...].T * HD ** (-0.5)).astype(bf)
        return dq, dk, dv


BACK_SCRATCH = (
    [pltpu.VMEM((T, 256), bf)] * 4 + [pltpu.VMEM((128, T), bf), pltpu.VMEM((128, T), f32)] + [pltpu.VMEM((T, 128), f32)] * 2
)


def attend_back_kernel(
    block, tok, w, dh1, q_i, k_i, v_i, dctx_i, ctx_i, lse, onehot, neg, g_o, ig_o, vg_o, *scratch,
):
    tokT, ig = scratch[-2:]
    step = pl.program_id(0)
    back = Back(block, onehot, neg, *scratch[:-2])

    @pl.when(step == 0)
    def _():
        tokT[...] = tok[...].T
        ig[...] = dh1[...]

    back.start()
    dq, dk, dv = back.pair(step, q_i[...], k_i[...], v_i[...], dctx_i[...], ctx_i[...], lse[...], lambda: None)
    vg_o[...] = jnp.zeros_like(vg_o)
    vg_o[0:1, :] = colsum(dq.astype(f32))
    vg_o[1:2, :] = colsum(dv.astype(f32))
    cat = jnp.concatenate([dq, dk, dv], axis=1)
    g_o[...] = nn(tokT[...], cat).astype(bf)
    ig[...] += nt(cat, w[...])

    @pl.when(step == PAIRS - 1)
    def _():
        ig_o[...] = ig[...].astype(bf)


def attend_back(tok, w, dh1, q, k, v, dctx, ctx, lse, onehot, neg, block=512):
    full = lambda s: pl.BlockSpec(s, lambda i: (0,) * len(s))
    col = pl.BlockSpec((T, 128), lambda i: (0, i))
    return pl.pallas_call(
        functools.partial(attend_back_kernel, block),
        grid=(PAIRS,),
        in_specs=[
            full((T, D)), pl.BlockSpec((D, W3), lambda i: (0, i)), full((T, D)),
            col, col, col, col, col, full((T, 128)), full((T, 128)), full((T, 128)),
        ],
        out_specs=[pl.BlockSpec((D, W3), lambda i: (0, i)), full((T, D)), pl.BlockSpec((16, 128), lambda i: (0, i))],
        out_shape=[S((D, 3 * D), bf), S((T, D), bf), S((16, D), f32)],
        scratch_shapes=BACK_SCRATCH + [pltpu.VMEM((D, T), bf), pltpu.VMEM((T, D), f32)],
        compiler_params=pltpu.CompilerParams(vmem_limit_bytes=60 * MIB),
        name="attend_back",
    )(tok, w, dh1, q, k, v, dctx, ctx, lse, onehot, neg)


def fold(x):
    rows, width = x.shape
    x = x * x
    tot = jnp.zeros((8, 128), f32)
    for i in range(rows // 8):
        for j in range(width // 128):
            tot = tot + x[i * 8 : (i + 1) * 8, j * 128 : (j + 1) * 128]
    return tot


def add_rows(dst, row0, src, rows):
    step = min(rows, 384 if src.shape[-1] == W3 else 1024)
    assert rows % step == 0

    def body(i, carry):
        d = pl.ds(pl.multiple_of(row0 + i * step, 16), step)
        s = pl.ds(pl.multiple_of(i * step, 16), step)
        dst[d, :] = (dst[d, :].astype(f32) + src[s, :].astype(f32)).astype(bf)
        return carry

    lax.fori_loop(0, rows // step, body, 0)


OFF = (2, 3, 5)


class Copies:
    def __init__(self, copies):
        self.copies = copies

    def start(self):
        for c in self.copies:
            c.start()

    def wait(self):
        for c in self.copies:
            c.wait()


class Reduce:
    def __init__(self, p, gs, gr, s_vec):
        self.p, self.gs, self.gr, self.s_vec = p, gs, gr, s_vec
        self.sent = []
        self.squares = jnp.zeros((8, 128), f32)

    def go(self, src, dst, n, j, peer):
        c = rcopy(src, dst, self.gs.at[n, j], self.gr.at[n, j], peer)
        c.start()
        self.sent.append(c)
        return c

    def go_x(self, src, dst, ssem, rsem, peer):
        c = rcopy(src, dst, ssem, rsem, peer)
        c.start()
        self.sent.append(c)
        return c

    def send_first(self, part):
        n, rc, acc, give, ready, rs, r2, r1, rz, fin = part
        return self.go(give, rs, n, 0, self.p.sib)

    def slots(self, chunks, issue):
        p, n = self.p, len(chunks)
        cS, cP, cQ, cZ = {}, {}, {}, {}
        for s in range(n + OFF[2]):
            i = s
            if i < n:
                cP[i] = []
                for part, first in zip(chunks[i], issue(i)):
                    num, rc, acc, give, ready, rs, r2, r1, rz, fin = part
                    if give is None:
                        cP[i].append((None, None))
                        continue
                    if ready is not None:
                        ready.wait()
                    first.wait_recv()
                    add_rows(acc, 0, rs, 16 * rc)
                    over = self.go(acc.at[band(4 * rc, p.dp3), :], r2.at[1], num, 2, p.n2)
                    cP[i].append((self.go(acc.at[band(4 * rc, p.dp2), :], r2.at[0], num, 1, p.n2), over))
            i = s - OFF[0]
            if 0 <= i < n:
                cQ[i] = []
                for part, (near, cross) in zip(chunks[i], cP[i]):
                    num, rc, acc, give, ready, rs, r2, r1, rz, fin = part
                    if give is None:
                        ready.wait()
                    else:
                        cross.wait_recv()
                        add_rows(acc, p.dp1 * 4 * rc, r2.at[1], 4 * rc)
                    cQ[i].append(self.go(acc.at[band(4 * rc, p.dp1), :], r1, num, 3, p.n1))
                    if give is not None:
                        near.wait_recv()
                        add_rows(acc, p.dp * 4 * rc, r2.at[0], 4 * rc)
            i = s - OFF[1]
            if 0 <= i < n:
                cZ[i] = []
                for part, q in zip(chunks[i], cQ[i]):
                    num, rc, acc, give, ready, rs, r2, r1, rz, fin = part
                    q.wait_recv()
                    add_rows(acc, p.dp * 4 * rc, r1, 4 * rc)
                    cZ[i].append([
                        self.go(acc.at[band(rc, p.dp * 4 + (p.z + j + 1) % 4), :], rz.at[j], num, 4 + j, p.zp[j]) for j in range(3)
                    ])
            i = s - OFF[2]
            if 0 <= i < n:
                for part, zs in zip(chunks[i], cZ[i]):
                    num, rc, acc, give, ready, rs, r2, r1, rz, fin = part
                    for c in zs:
                        c.wait_recv()
                    own = acc[band(rc, p.dp * 4 + p.z), :].astype(f32)
                    for j in range(3):
                        own = own + rz[j].astype(f32)
                    if fin is None:
                        own = jnp.where(p.k == 0, own[:24], own[24:])
                        self.s_vec[...] = own
                    else:
                        fin[...] = own
                    self.squares = self.squares + fold(own)
            yield s + 1


def backward_kernel(
    block, lengths, tokT_h, wqkv_h, dh1_h, qkv_h, dctx_h, ctx_h, lse, vg_i, gwo, gwi, acc_h,
    ig_h, s_qkv, s_out, s_in, s_down, s_vec, total,
    onehot, neg, wq, ig, qkv, dctx, ctx, gq, gvt, vg,
    qa, ka, va, da, kT, dqT, dka, dva, tokT,
    acc_a, rs_a, r2_a, r1_a, rz_a, acc_d, r1_d, rz_d, acc_v, rs_v, r2_v, r1_v, rz_v,
    fin_a, fin_d, rx_a, rx_d, tile, nb1, nb2, gs, gr, ls, xs, xr, ns, nr, ps, ts, ds,
):
    p = Place()
    k = p.k
    far = 1 - k
    turns = lambda turn, count=1: slice(turn * W3, (turn + count) * W3)
    cols = lambda pair: slice(pair * 128, (pair + 1) * 128)
    early = [pltpu.make_async_copy(tokT_h, tokT, ts.at[0])]
    pairs = {}
    for turn, pair in enumerate(ORDER):
        moves = ((qkv_h, qkv, turns(turn)), (dctx_h, dctx, cols(pair)), (ctx_h, ctx, cols(pair)))
        pairs[pair] = [
            pltpu.make_async_copy(src.at[:, cs], dst.at[:, cs], ps.at[n, pair]) for n, (src, dst, cs) in enumerate(moves)
        ]
    late = [pltpu.make_async_copy(wqkv_h, wq, ts.at[1]), pltpu.make_async_copy(dh1_h, ig, ts.at[2])]
    for c in pairs[0]:
        c.start()
    enter(p.others + p.zp)
    red = Reduce(p, gs, gr, s_vec)

    chunks = []
    for t in range(3):
        loads = Copies([
            pltpu.make_async_copy(acc_h.at[t, band(D, dp), :], acc_d.at[t, band(D, dp), :], ds.at[t, n]) for n, dp in enumerate((p.dp, p.dp1))
        ])
        chunks.append([(t, 192, acc_d.at[t], None, loads, None, None, r1_d.at[t], rz_d.at[t], fin_d.at[t])])
    spots = lambda a: (rs_a.at[a], r2_a.at[a], r1_a.at[a], rz_a.at[a], fin_a.at[a])
    for t in range(5):
        ref, start = (gwi, lambda c: t + 4 * c) if t < 4 else (gwo, lambda c: c)
        load = pltpu.make_async_copy(ref.at[:, half(W3, start(k))], acc_a.at[t], ls.at[t])
        chunks.append([(3 + t, 48, acc_a.at[t], ref.at[:, half(W3, start(far))], load) + spots(t)])
    firsts = {}

    def begin(i):
        if i not in firsts:
            for part in chunks[i]:
                if part[4] is not None:
                    part[4].start()
            firsts[i] = [None if part[3] is None else red.send_first(part) for part in chunks[i]]

    for t in range(3):
        chunks.append([(8 + t, 48, gq.at[t, k], gq.at[t, far], None) + spots(5 + t)])
    chunks[10].append((11, 48, acc_v, gvt, None, rs_v, r2_v, r1_v, rz_v, None))
    for t in range(3):
        chunks[3 + t] += chunks[t]
    sequence = (3, 4, 5, 8, 6, 7, 9, 10)
    ordered = [chunks[i] for i in sequence]
    ready = set(range(3, 8))

    def issue(s):
        for i in sequence[s : s + 3]:
            if i in ready:
                begin(i)
        return firsts[sequence[s]]

    begin(sequence[0])
    begin(sequence[1])

    for c in pairs[3] + early:
        c.start()
    slots = red.slots(ordered, issue)
    place = [0]

    def step():
        place[0] = next(slots, 100)

    back = Back(block, onehot, neg, qa, ka, va, da, kT, dqT, dka, dva)
    masks(lengths, onehot, neg)
    back.start()
    vg[...] = vg_i[...]
    spent = [0.0]
    step()

    def tick(us=1.65):
        spent[0] += us
        if spent[0] >= PACE_BACKWARD and place[0] < len(sequence) and sequence[place[0]] in ready:
            spent[0] -= PACE_BACKWARD
            step()

    for turn, pair in enumerate(ORDER):
        cs = cols(pair)
        for c in pairs[pair]:
            c.wait()
        soon = pairs[ORDER[turn + 2]] if turn + 2 < PAIRS else []
        for c in soon + (late if turn == 2 else []):
            c.start()
        q, key, val = [qkv[:, turn * W3 + j * 128 : turn * W3 + (j + 1) * 128] for j in range(3)]
        dq, dk, dv = back.pair(pair, q, key, val, dctx[:, cs], ctx[:, cs], lse[...], tick)
        for j, part in enumerate((dq, dk, dv)):
            qkv[:, turn * W3 + j * 128 : turn * W3 + (j + 1) * 128] = part
        vg[0:1, cs] = colsum(dq.astype(f32))
        vg[1:2, cs] = colsum(dv.astype(f32))
        t, side = turn // 2, turn % 2
        if turn == 1:
            early[0].wait()
        if side == 1:
            g = nn(tokT[...], qkv[:, turns(2 * t, 2)])
            gq[t, 0] = g[:, :W3].astype(bf)
            gq[t, 1] = g[:, W3:].astype(bf)
            tick(1.6)
        if side == 1:
            if t == 2:
                gvt[...] = jnp.concatenate([vg[...], jnp.zeros((112, D), f32)], axis=0).T.astype(bf)
                acc_v[...] = gvt[...]
            begin(8 + t)
            ready.add(8 + t)
    while place[0] < len(sequence) - 1:
        step()
    for c in late:
        c.wait()
    for b in range(4):
        r = slice(b * 256, (b + 1) * 256)
        if b >= 2:
            step()
        dctx[r, :] = (ig[r, :] + nt(qkv[r, :], wq[...])).astype(bf)
    give = pltpu.make_async_copy(dctx, ig_h, ts.at[0])
    give.start()
    for c in slots:
        pass
    cX = []
    for a in range(8):
        cX.append(red.go_x(fin_a.at[a, pl.ds(pl.multiple_of(far * 24, 8), 24), :], rx_a.at[a], xs.at[a], xr.at[a], p.sib))
    for t in range(3):
        cX.append(red.go_x(fin_d.at[t, pl.ds(pl.multiple_of(far * 96, 8), 96), :], rx_d.at[t], xs.at[8 + t], xr.at[8 + t], p.sib))
    part = jnp.sum(jnp.sum(red.squares, axis=1, keepdims=True), axis=0, keepdims=True)
    tile[0] = jnp.broadcast_to(part, (8, 128))
    cN = [red.go_x(tile.at[0], nb1.at[j], ns.at[j], nr.at[j], p.zp[j]) for j in range(3)]
    for c in cN:
        c.wait_recv()
    zsum = jnp.zeros((8, 128), f32)
    for zz in range(4):
        term = tile[0]
        for j in range(3):
            term = jnp.where((p.z + 3 - j) % 4 == zz, nb1[j], term)
        zsum = zsum + term
    tile[1] = zsum
    cN = [red.go_x(tile.at[1], nb2.at[j], ns.at[3 + j], nr.at[3 + j], p.others[j]) for j in range(7)]
    my24 = pl.ds(pl.multiple_of(k * 24, 8), 24)
    for c in cX:
        c.wait_recv()
    for src, side in ((lambda a: fin_a[a, my24, :], k), (lambda a: rx_a[a], far)):
        for t in range(4):
            s_in[:, half(W3, t + 4 * side)] = src(t)
        s_out[:, half(W3, side)] = src(4)
        for t in range(3):
            term = src(5 + t)
            for j in range(3):
                s_qkv[j, :, half(128, 3 * side + t)] = term[:, j * 128 : (j + 1) * 128]
    my96 = pl.ds(pl.multiple_of(k * 96, 8), 96)
    for t in range(3):
        s_down[:, half(128, 3 * k + t)] = fin_d[t, my96, :]
        s_down[:, half(128, 3 * far + t)] = rx_d[t]
    for c in cN:
        c.wait_recv()
    msum = jnp.zeros((8, 128), f32)
    for mm in range(8):
        term = tile[1]
        for j in range(7):
            term = jnp.where((p.m + 7 - j) % 8 == mm, nb2[j], term)
        msum = msum + term
    total[...] = msum
    for c in red.sent:
        c.wait_send()
    give.wait()


def landing(lead, rows, w):
    shapes = ((rows, w), (2, rows // 4, w), (rows // 4, w), (3, rows // 16, w))
    return [pltpu.VMEM(lead + shape, bf) for shape in shapes]


def backward(lengths, tokT, wqkv, dh1, qkv, dctx, ctx, lse, vg, gwo, gwi, acc, block=512):
    vb = lambda *shape: pltpu.VMEM(shape, bf)
    vf = lambda *shape: pltpu.VMEM(shape, f32)
    dma = lambda *shape: pltpu.SemaphoreType.DMA(shape)
    return pl.pallas_call(
        functools.partial(backward_kernel, block),
        in_specs=[SMEM] + [ANY] * 6 + [VM] * 2 + [ANY] * 3,
        out_specs=[ANY] + [VM] * 6,
        out_shape=[S((T, D), bf), S((3, 24, D), f32), S((24, D), f32), S((24, FF), f32), S((96, D), f32), S((24, 128), f32), S((8, 128), f32)],
        scratch_shapes=[
            vb(T, 128), vb(T, 128),
            vb(D, 3 * D), vf(T, D), vb(T, 3 * D), vb(T, D), vf(T, D), vb(3, 2, D, W3), vb(D, 128), vf(16, D),
        ]
        + BACK_SCRATCH + [vb(D, T)]
        + [vb(5, D, W3)] + landing((8,), D, W3) + [vb(3, FF, 128)] + landing((3,), FF, 128)[2:] + [vb(D, 128)] + landing((), D, 128)
        + [
            vf(8, 48, W3), vf(3, 192, 128), vf(8, 24, W3), vf(3, 96, 128), vf(2, 8, 128), vf(3, 8, 128), vf(7, 8, 128),
            dma(12, 7), dma(12, 7), dma(8), dma(11), dma(11), dma(10), dma(10), dma(3, 6), dma(3), dma(3, 2),
        ],
        compiler_params=pltpu.CompilerParams(collective_id=1, has_side_effects=True, vmem_limit_bytes=62 * MIB),
        name="backward",
    )(lengths, tokT, wqkv, dh1, qkv, dctx, ctx, lse, vg, gwo, gwi, acc)


def gelu_parts(x):
    e = jnp.exp(x * x * (-0.5))
    t = 1.0 / (1.0 + (0.3275911 * 0.7071067811865476) * jnp.abs(x))
    poly = 0.5 * 1.061405429
    for a in (-1.453152027, 1.421413741, -0.284496736, 0.254829592):
        poly = 0.5 * a + t * poly
    tail = t * poly * e
    return jnp.where(x >= 0, 1.0 - tail, tail), e * 0.3989422804014327


def norm_forward(h):
    c = h - jnp.mean(h, axis=1, keepdims=True)
    r = lax.rsqrt(jnp.mean(c * c, axis=1, keepdims=True) + norm_epsilon)
    return c * r, r


def norm_backward(dy, xh, r, g):
    dx = dy * g
    return r * (dx - jnp.mean(dx, axis=1, keepdims=True) - xh * jnp.mean(dx * xh, axis=1, keepdims=True))


def ffn_kernel(
    block, tok, ctx, cot, vec, wo_h, wi_h, w2_h, out_o, dh1_o, dctx_o, vg_o, gwo_h, gwi_h, gw2_h,
    wo, wi, w2, cb, x1b, hb, gp, dfb, dhp, dab, stage, tr, insem, outsem,
):
    loads = [
        pltpu.make_async_copy(wo_h, wo, insem.at[0]),
        pltpu.make_async_copy(wi_h, wi, insem.at[1]),
        pltpu.make_async_copy(w2_h, w2, insem.at[2]),
    ]
    for c in loads:
        c.start()
    vg_o[...] = jnp.zeros_like(vg_o)
    row = lambda i: vec[i : i + 1, :]
    for c in loads:
        c.wait()

    def one_block(b, carry):
        r = pl.ds(pl.multiple_of(b * block, block), block)
        c = ctx[r, :].astype(bf)
        cb[r, :] = c
        xh1, r1 = norm_forward(tok[r, :].astype(f32) + (nn(c, wo[...]) + row(2)))
        x1 = xh1 * row(4) + row(5)
        xb = x1.astype(bf)
        x1b[r, :] = xb
        acc = x1 + row(3)
        for j in range(4):
            cs = slice(j * D, (j + 1) * D)
            hp = nn(xb, wi[:, cs]) + row(8 + j)
            big, dense = gelu_parts(hp)
            h = (hp * big).astype(bf)
            hb[r, cs] = h
            gp[:, cs] = big + hp * dense
            acc = acc + nn(h, w2[cs, :])
        xh2, r2 = norm_forward(acc)
        out_o[r, :] = (xh2 * row(6) + row(7)).astype(bf)
        dy = cot[r, :].astype(f32)
        vg_o[6:7, :] += colsum(dy * xh2)
        vg_o[7:8, :] += colsum(dy)
        dh2 = norm_backward(dy, xh2, r2, row(6))
        df = dh2.astype(bf)
        dfb[r, :] = df
        vg_o[3:4, :] += colsum(df.astype(f32))
        dx1 = dh2
        for j in range(4):
            cs = slice(j * D, (j + 1) * D)
            dh = (gp[:, cs] * nt(df, w2[cs, :])).astype(bf)
            dhp[r, cs] = dh
            vg_o[8 + j : 9 + j, :] += colsum(dh.astype(f32))
            dx1 = dx1 + nt(dh, wi[:, cs])
        vg_o[4:5, :] += colsum(dx1 * xh1)
        vg_o[5:6, :] += colsum(dx1)
        dh1 = norm_backward(dx1, xh1, r1, row(4))
        dh1_o[r, :] = dh1
        da = dh1.astype(bf)
        dab[r, :] = da
        vg_o[2:3, :] += colsum(da.astype(f32))
        dctx_o[r, :] = nt(da, wo[...]).astype(bf)
        return carry

    lax.fori_loop(0, T // block, one_block, 0)
    outs = []

    def emit(val, dst):
        i = len(outs)
        if i >= 2:
            outs[i - 2].wait()
        stage[i % 2] = val.astype(bf)
        c = pltpu.make_async_copy(stage.at[i % 2], dst, outsem.at[i % 2])
        c.start()
        outs.append(c)

    for j in range(4):
        cs = slice(j * D, (j + 1) * D)
        emit(tn(hb[:, cs], dfb[...]), gw2_h.at[cs, :])
    tr[...] = x1b[...].T
    for j in range(4):
        cs = slice(j * D, (j + 1) * D)
        emit(nn(tr[...], dhp[:, cs]), gwi_h.at[:, cs])
    emit(tn(cb[...], dab[...]), gwo_h)
    outs[7].wait()
    outs[8].wait()


def feed_forward(tok, ctx, cot, vec, wo, wi, w2, block=256):
    return pl.pallas_call(
        functools.partial(ffn_kernel, block),
        in_specs=[VM] * 4 + [ANY] * 3,
        out_specs=[VM] * 4 + [ANY] * 3,
        out_shape=[
            S((T, D), bf), S((T, D), f32), S((T, D), bf), S((16, D), f32), S((D, D), bf), S((D, FF), bf), S((FF, D), bf),
        ],
        scratch_shapes=[
            pltpu.VMEM((D, D), bf), pltpu.VMEM((D, FF), bf), pltpu.VMEM((FF, D), bf), pltpu.VMEM((T, D), bf),
            pltpu.VMEM((T, D), bf), pltpu.VMEM((T, FF), bf), pltpu.VMEM((block, FF), f32), pltpu.VMEM((T, D), bf),
            pltpu.VMEM((T, FF), bf), pltpu.VMEM((T, D), bf), pltpu.VMEM((2, D, D), bf), pltpu.VMEM((D, T), bf),
            pltpu.SemaphoreType.DMA((3,)), pltpu.SemaphoreType.DMA((2,)),
        ],
        compiler_params=pltpu.CompilerParams(vmem_limit_bytes=60 * MIB),
        name="feed_forward",
    )(tok, ctx, cot, vec, wo, wi, w2)


def middle_kernel(
    block, cot_h, vec_h, wo_h, wi_h, w2_h, hb_h, gp_h, xh_h, sd, hbT_h, xbT_h, lowT_h, out_h, dh1_h, dctx_h, vg, gwo_h, gwi_h, acc_h,
    vec, wo, wi, w2, out, cot, xh1, hb, gp, hT, dfb, dh, da, gw2, rs, r2, ls, os, xs, xr, gs,
):
    p = Place()
    k = p.k
    far = 1 - k
    top, low_part = slice(0, T // 2), slice(T // 2, T)
    xbT, lowT, go = hT.at[0:D, :], hT.at[D : 2 * D, :], hT.at[2 * D : 3 * D, 0:D]
    moves = [(w2_h, w2), (vec_h, vec)]
    for part in (top, low_part):
        moves += [(src.at[part, :], dst.at[part, :]) for src, dst in ((hb_h, hb), (xh_h, xh1), (cot_h, cot))]
    moves += [(hbT_h, hT), (gp_h, gp), (wi_h, wi), (wo_h, wo), (xbT_h, xbT), (lowT_h, lowT)]
    loads = [pltpu.make_async_copy(src, dst, ls.at[i]) for i, (src, dst) in enumerate(moves)]

    def start(first, last):
        for c in loads[first:last]:
            c.start()

    def arrive(first, last):
        for c in loads[first:last]:
            c.wait()

    start(0, 5)
    enter([p.sib, p.n2])
    vg[...] = jnp.zeros_like(vg)
    row = lambda i: vec[i : i + 1, :]
    rows = [slice(b * block, (b + 1) * block) for b in range(T // block)]
    quarter = [slice(j * D, (j + 1) * D) for j in range(4)]
    outs = []

    def give(src, dst):
        outs.append(pltpu.make_async_copy(src, dst, os.at[len(outs)]))
        outs[-1].start()

    arrive(0, 5)
    start(5, 12)
    for r in rows:
        if r.start == T // 2:
            arrive(5, 8)
        acc = xh1[r, :] * row(4) + row(5) + (nn(hb[r, :], w2[...]) + row(3))
        xh2, r2d = norm_forward(acc)
        out[r, :] = (xh2 * row(6) + row(7)).astype(bf)
        dy = cot[r, :].astype(f32)
        vg[6:7, :] += colsum(dy * xh2)
        vg[7:8, :] += colsum(dy)
        dh2 = norm_backward(dy, xh2, r2d, row(6))
        dh[r, :] = dh2
        df = dh2.astype(bf)
        dfb[r, :] = df
        vg[3:4, :] += colsum(df.astype(f32))
    give(out, out_h)
    arrive(8, 9)
    sent, swaps, near, cross = [], [], [], []

    def go_to(src, dst, t, j, peer):
        c = rcopy(src, dst, xs.at[t, j], xr.at[t, j], peer)
        c.start()
        sent.append(c)
        return c

    for t in range(3):
        both = jnp.concatenate([dfb[:, t * 128 : (t + 1) * 128], dfb[:, (t + 3) * 128 : (t + 4) * 128]], axis=1)
        for cs in quarter:
            g = nn(hT[cs, :], both).astype(bf)
            gw2[t, 0, cs, :] = g[:, :128]
            gw2[t, 1, cs, :] = g[:, 128:]
        swaps.append(go_to(gw2.at[t, far], rs.at[t], t, 0, p.sib))

    def over(t):
        mine = gw2.at[t, k]
        swaps[t].wait_recv()
        add_rows(mine, 0, rs.at[t], FF)
        cross.append(go_to(mine.at[band(D, p.dp3), :], r2.at[t, 1], t, 1, p.n2))
        near.append(go_to(mine.at[band(D, p.dp2), :], r2.at[t, 0], t, 2, p.n2))

    def back(t):
        mine = gw2.at[t, k]
        for n, (c, dp) in enumerate(((near[t], p.dp), (cross[t], p.dp1))):
            c.wait_recv()
            add_rows(mine, dp * D, r2.at[t, n], D)
            outs.append(pltpu.make_async_copy(mine.at[band(D, dp), :], acc_h.at[t, band(D, dp), :], gs.at[t, n]))
            outs[-1].start()

    arrive(9, 12)
    start(12, 14)
    for b, r in enumerate(rows):
        if b < 3:
            over(b)
        else:
            back(0)
        df = dfb[r, :]
        for j, cs in enumerate(quarter):
            low = (gp[r, cs] * nt(df, w2[cs, :])).astype(bf)
            hb[r, cs] = low
            vg[8 + j : 9 + j, :] += colsum(low.astype(f32))
        dx1 = dh[r, :] + nt(hb[r, :], wi[...])
        xh = xh1[r, :]
        vg[4:5, :] += colsum(dx1 * xh)
        vg[5:6, :] += colsum(dx1)
        dh1 = norm_backward(dx1, xh, sd[r, 0:1], row(4))
        dh[r, :] = dh1
        low = dh1.astype(bf)
        da[r, :] = low
        vg[2:3, :] += colsum(low.astype(f32))
        cot[r, :] = nt(low, wo[...]).astype(bf)
    give(dh, dh1_h)
    give(cot, dctx_h)
    back(1)
    back(2)
    arrive(12, 14)
    for cs in quarter:
        wi[:, cs] = nn(xbT[...], hb[:, cs]).astype(bf)
    give(wi, gwi_h)
    go[...] = nn(lowT[...], da[...]).astype(bf)
    give(go, gwo_h)
    for c in sent:
        c.wait_send()
    for c in outs:
        c.wait()


def middle(cot, vec, wo, wi, w2, hb, gp, xh, sd, hbT, xbT, lowT, block=256):
    vb = lambda *shape: pltpu.VMEM(shape, bf)
    vf = lambda *shape: pltpu.VMEM(shape, f32)
    dma = lambda *shape: pltpu.SemaphoreType.DMA(shape)
    return pl.pallas_call(
        functools.partial(middle_kernel, block),
        in_specs=[ANY] * 8 + [VM] + [ANY] * 3,
        out_specs=[ANY] * 3 + [VM] + [ANY] * 3,
        out_shape=[
            S((T, D), bf), S((T, D), f32), S((T, D), bf), S((16, D), f32), S((D, D), bf), S((D, FF), bf), S((3, FF, 128), bf),
        ],
        scratch_shapes=[
            vf(128, D), vb(D, D), vb(D, FF), vb(FF, D), vb(T, D), vb(T, D), vf(T, D),
            vb(T, FF), vf(T, FF), vb(FF, T), vb(T, D), vf(T, D), vb(T, D),
            vb(3, 2, FF, 128), vb(3, FF, 128), vb(3, 2, D, 128), dma(14), dma(11), dma(3, 3), dma(3, 3), dma(3, 2),
        ],
        compiler_params=pltpu.CompilerParams(collective_id=2, has_side_effects=True, vmem_limit_bytes=62 * MIB),
        name="middle",
    )(cot, vec, wo, wi, w2, hb, gp, xh, sd, hbT, xbT, lowT)


def adam_step(weight, gradient, first_old, second_old, decay_rate, step_rate):
    first_new = moment_decay * first_old + (1.0 - moment_decay) * gradient
    second_new = square_decay * second_old + (1.0 - square_decay) * gradient * gradient
    first_hat = first_new / (1.0 - moment_decay**STEP)
    second_hat = second_new / (1.0 - square_decay**STEP)
    weight_new = weight - step_rate * (first_hat / (jnp.sqrt(second_hat) + adam_epsilon) + decay_rate * weight)
    return (weight_new, first_new, second_new)


def update_kernel(total, ig_h, *refs):
    hbm, outs, bufs, sem, osem = refs[0:20], refs[20:37], refs[37:58], refs[58], refs[59]
    ig_o, norm_o, new_h = outs[0], outs[1], outs[2:17]
    g, w, m, u, ig = bufs[0:5], bufs[5:10], bufs[10:15], bufs[15:20], bufs[20]
    order = [i + 5 * j for i in (2, 3, 0, 1, 4) for j in range(4)]
    loads = {i: pltpu.make_async_copy(hbm[i], bufs[i], sem.at[i]) for i in order}
    through = pltpu.make_async_copy(ig_h, ig, sem.at[20])
    for i in order:
        loads[i].start()
    through.start()
    norm = jnp.sqrt(total[...])
    norm_o[0, 0] = norm[0, 0]
    factor = jnp.minimum(1.0, clip_limit / (norm + 1e-06))[0:1, 0:1]
    gone = []

    def give(src, dst):
        gone.append(pltpu.make_async_copy(src, dst, osem.at[len(gone)]))
        gone[-1].start()

    for i in (2, 3, 0, 1, 4):
        for j in range(4):
            loads[i + 5 * j].wait()
        if i < 4:
            new = adam_step(w[i][...], factor * g[i][...], m[i][...], u[i][...], weight_decay, learn_rate)
        else:
            wide = jnp.concatenate([g[4][...], jnp.zeros((104, 128), f32)], axis=0).T[:12, :24]
            new = adam_step(w[4][...], factor * wide, m[4][...], u[4][...], 0.0, vector_rate)
        for j, (place, val) in enumerate(zip((w, m, u), new)):
            place[i][...] = val
            give(place[i], new_h[i + 5 * j])
        if i == 2:
            through.wait()
            give(ig, ig_o)
    for c in gone:
        c.wait()


def update(total, input_grad, weights, grads, firsts, seconds):
    arrays = (*grads, *weights, *firsts, *seconds)
    shapes = [S(w.shape, f32) for w in weights]
    return pl.pallas_call(
        update_kernel,
        in_specs=[VM] + [ANY] * 21,
        out_specs=[ANY, SMEM] + [ANY] * 15,
        out_shape=[S(input_grad.shape, bf), S((1, 1), f32)] + shapes * 3,
        scratch_shapes=[pltpu.VMEM(a.shape, f32) for a in arrays]
        + [pltpu.VMEM(input_grad.shape, bf), pltpu.SemaphoreType.DMA((21,)), pltpu.SemaphoreType.DMA((16,))],
        compiler_params=pltpu.CompilerParams(vmem_limit_bytes=62 * MIB),
        name="clip_and_update",
    )(total, input_grad, *grads, *weights, *firsts, *seconds)


def segment_ids(lengths):
    bounds = jnp.cumsum(lengths, axis=-1)
    places = jnp.arange(T, dtype=jnp.int32)
    return jnp.sum((places[:, None] >= bounds[None, :]).astype(jnp.int32), axis=-1)


def pairs_last(a):
    return a.reshape(3, D, PAIRS, 128).transpose(1, 2, 0, 3).reshape(D, 3 * D)


def per_device(
    small, tokens, cotangent, lengths, qkv_weight, out_weight, in_weight, down_weight, vectors,
    qkv_first, out_first, in_first, down_first, vec_first, qkv_second, out_second, in_second, down_second, vec_second,
):
    weights = (qkv_weight, out_weight, in_weight, down_weight, vectors)
    firsts = (qkv_first, out_first, in_first, down_first, vec_first)
    seconds = (qkv_second, out_second, in_second, down_second, vec_second)
    axes = ("dp", "fsdp")
    if small:
        wqkv, wo, wi, w2, vec, qkv, ctx, lse, hb, gp, xh, sd, tokT, lowT, xbT, hbT = forward(tokens, lengths, weights)
        result, dh1, dctx, vg, gwo, gwi, acc = middle(cotangent, vec, wo, wi, w2, hb, gp, xh, sd, hbT, xbT, lowT)
        ig, *grads, total = backward(lengths, tokT, wqkv, dh1, qkv, dctx, ctx, lse, vg, gwo, gwi, acc)
        updated = update(total, ig, weights, grads, firsts, seconds)
        return (result, updated[0], updated[1].reshape(()), *updated[2:])
    seg = segment_ids(lengths[0])
    lane = jnp.arange(128)
    match = seg[:, None] == lane[None, :]
    onehot = match.astype(bf)
    neg = jnp.where(match | (lane >= lengths.shape[1])[None, :], 0.0, -1e30).astype(bf)
    gather = lambda a, axis: lax.all_gather(a.astype(bf), axes, axis=axis, tiled=True)
    wqkv = pairs_last(gather(qkv_weight, 1))
    wo, wi, w2 = gather(out_weight, 0), gather(in_weight, 0), gather(down_weight, 0)
    vec = jnp.concatenate([gather(vectors, 1).astype(f32), jnp.zeros((4, D), f32)], axis=0)
    bias = jnp.stack([vec[0], jnp.zeros_like(vec[0]), vec[1]]).reshape(3, PAIRS, 128).transpose(1, 0, 2).reshape(1, 3 * D)
    q, k, v, ctx, lse = attend(tokens, wqkv, bias, onehot, neg)
    result, dh1, dctx, vg, gwo, gwi, gw2 = feed_forward(tokens, ctx, cotangent, vec, wo, wi, w2)
    gqkv, input_grad, vg_qv = attend_back(tokens, wqkv, dh1, q, k, v, dctx, ctx, lse, onehot, neg)
    vg = vg + vg_qv
    scatter = lambda a, axis: lax.psum_scatter(a.astype(f32), axes, scatter_dimension=axis, tiled=True)
    gqkv = gqkv.reshape(D, PAIRS, 3, 128).transpose(2, 0, 1, 3).reshape(3, D, D)
    grads = (scatter(gqkv, 1), scatter(gwo, 0), scatter(gwi, 0), scatter(gw2, 0), scatter(vg[:12], 1))
    grad_norm = jnp.sqrt(lax.psum(sum(jnp.sum(g * g) for g in grads), axes))
    factor = jnp.minimum(1.0, clip_limit / (grad_norm + 1e-06))
    updated = []
    for i in range(5):
        rates = (0.0, vector_rate) if i == 4 else (weight_decay, learn_rate)
        updated.append(adam_step(weights[i], factor * grads[i], firsts[i], seconds[i], *rates))
    return (result, input_grad, grad_norm, *[u[j] for j in range(3) for u in updated])


def solution(mesh):
    rows = P(("dp", "fsdp"), None)
    deep = P(None, ("dp", "fsdp"), None)
    wide = P(None, ("dp", "fsdp"))
    group = (deep, rows, rows, rows, wide)
    small = mesh.shape["dp"] == 4 and mesh.shape["fsdp"] == 8
    return jax.shard_map(
        functools.partial(per_device, small),
        mesh=mesh,
        in_specs=(rows, rows, rows) + group * 3,
        out_specs=(rows, rows, P()) + group * 3,
        check_vma=False,
    )
```

```python
import functools

import jax
import jax.numpy as jnp
from jax import lax
from jax.experimental import pallas as pl
from jax.experimental.pallas import tpu as pltpu
from jax.sharding import PartitionSpec as P

D = 768
H = 12
HD = 64
FF = 3072
T = 1024
STEP = 10
PAIRS = H // 2
W3 = 384

moment_decay = 0.9
square_decay = 0.999
learn_rate = 0.02
vector_rate = 0.15
weight_decay = 0.01
adam_epsilon = 1e-08
clip_limit = 1.0
norm_epsilon = 1e-05

bf = jnp.bfloat16
f32 = jnp.float32
MESH = pl.DeviceIdType.MESH
VM = pl.BlockSpec(memory_space=pltpu.VMEM)
ANY = pl.BlockSpec(memory_space=pl.ANY)
MIB = 2**20


def S(shape, dtype):
    return jax.ShapeDtypeStruct(shape, dtype)


def nn(a, b):
    return lax.dot_general(a, b, (((1,), (0,)), ((), ())), preferred_element_type=f32)


def nt(a, b):
    return lax.dot_general(a, b, (((1,), (1,)), ((), ())), preferred_element_type=f32)


def tn(a, b):
    return lax.dot_general(a, b, (((0,), (0,)), ((), ())), preferred_element_type=f32)


def colsum(x):
    return jnp.sum(x, axis=0, keepdims=True)


class Place:
    def __init__(self):
        self.dp = lax.axis_index("dp")
        self.fs = lax.axis_index("fsdp")
        self.z = self.fs // 2
        self.k = self.fs % 2
        dp, k = self.dp, self.k
        xn = dp + 1 - 2 * (dp % 2)
        yn = (dp + 2) % 4
        self.dp1 = xn * (1 - k) + yn * k
        self.dp2 = yn * (1 - k) + xn * k
        self.dp3 = 3 - dp
        self.n1 = (self.dp1, self.fs)
        self.n2 = (self.dp2, self.fs)
        self.sib = (dp, self.z * 2 + 1 - k)
        self.zp = [(dp, ((self.z + i) % 4) * 2 + k) for i in (1, 2, 3)]
        self.m = dp * 2 + k
        self.others = []
        for j in range(1, 8):
            other = (self.m + j) % 8
            self.others.append((other // 2, self.z * 2 + other % 2))


def enter(peers):
    barrier = pltpu.get_barrier_semaphore()
    for peer in peers:
        pl.semaphore_signal(barrier, inc=1, device_id=peer, device_id_type=MESH)
    pl.semaphore_wait(barrier, len(peers))


def rcopy(src, dst, ssem, rsem, peer):
    return pltpu.make_async_remote_copy(src, dst, ssem, rsem, device_id=peer, device_id_type=MESH)


def half(w, c):
    return pl.ds(pl.multiple_of(c * w, 128), w)


def band(rows, index):
    return pl.ds(pl.multiple_of(rows * index, 16), rows)


def masks(lengths, onehot, neg):
    lane = lax.broadcasted_iota(jnp.int32, (1, 128), 1)
    first = jnp.full((1, 128), T, jnp.int32)
    after = jnp.full((1, 128), T, jnp.int32)
    total = jnp.int32(0)
    count = lengths.shape[1]
    for j in range(count):
        first = jnp.where(lane == j, total, first)
        total = total + lengths[0, j]
        after = jnp.where(lane == j, total, after)
    row = lax.broadcasted_iota(jnp.int32, (T, 128), 0)
    own = (row >= first) & (row < after)
    onehot[...] = jnp.where(own, 1.0, 0.0).astype(bf)
    neg[...] = jnp.where(own | (lane >= count), 0.0, -1e30).astype(bf)


PACE_FORWARD = 6.0
PACE_BACKWARD = 6.5


ORDER = (0, 3, 1, 4, 2, 5)


MIXED = (4, 7, 10)


class Gather:
    def __init__(self, p, chunks, gs, gr):
        self.p, self.chunks, self.gs, self.gr = p, chunks, gs, gr
        self.sent = []

    def go(self, part, j, rows, peer):
        n, ref, rc, cols, swap, mixed = part
        view = ref.at[rows, cols]
        c = rcopy(view, view, self.gs.at[n, j], self.gr.at[n, j], peer)
        c.start()
        self.sent.append(c)
        return c

    def slots(self, ahead):
        p, n = self.p, len(self.chunks)
        c0, c1, c2, c3, c4 = {}, {}, {}, {}, {}

        def more(i):
            if i < n:
                c0[i] = []
                for part in self.chunks[i]:
                    own = band(part[2], p.dp * 4 + p.z)
                    c0[i].append([self.go(part, 3, own, p.n1)] if part[5] else [self.go(part, j, own, p.zp[j]) for j in range(3)])

        def links(i):
            if 0 <= i < n:
                c1[i], c2[i] = [], []
                for q, part in enumerate(self.chunks[i]):
                    rc = part[2]
                    for c in c0[i][q]:
                        c.wait_recv()
                    if part[5]:
                        c1[i].append([
                            self.go(part, j + 7 * h, band(rc, d * 4 + p.z), p.zp[j]) for j in range(3) for h, d in enumerate((p.dp, p.dp1))
                        ])
                    else:
                        c1[i].append([self.go(part, 3, band(4 * rc, p.dp), p.n1)])
                        c2[i].append(self.go(part, 4, band(4 * rc, p.dp), p.n2))

        def cross(i):
            if 0 <= i < n:
                c3[i] = []
                for q, part in enumerate(self.chunks[i]):
                    for c in c1[i][q]:
                        c.wait_recv()
                    if part[5]:
                        c2[i].append(self.go(part, 4, band(4 * part[2], p.dp), p.n2))
                    c3[i].append(self.go(part, 5, band(4 * part[2], p.dp1), p.n2))

        def swap(i):
            if 0 <= i < n:
                c4[i] = []
                for q, part in enumerate(self.chunks[i]):
                    c2[i][q].wait_recv()
                    c3[i][q].wait_recv()
                    if part[4]:
                        c4[i].append(self.go(part, 6, pl.ds(0, 16 * part[2]), p.sib))

        def take(i):
            if 0 <= i < n:
                for c in c4[i]:
                    c.wait_recv()

        for i in range(3):
            more(i)
        yield -1
        for i in range(3, ahead):
            more(i)
        links(0)
        cross(0)
        links(1)
        swap(0)
        links(2)
        more(ahead)
        take(0)
        cross(1)
        links(3)
        more(ahead + 1)
        yield 0
        for t in range(1, n + 2):
            more(t + ahead + 1)
            links(t + 3)
            cross(t + 1)
            if t != 2:
                swap(max(t - 1, 1))
            if t == 2 or t > 3:
                take(max(t - 2, 1))
            yield max(t - 2, min(t - 1, 1))
        for c in self.sent:
            c.wait_send()
        yield n


def forward_kernel(
    block, tok_h, lengths, qkv, out, inw, down, vec,
    wqkv_h, wo_h, wi_h, w2, vrow, qkv_h, ctx_h, lse, hb_h, gp_h, xh_h, sd, tokT_h, lowT_h, xbT_h, hbT_h,
    tok, wq, vt, qkvs, ctx, low, qa, ka, va, onehot, neg,
    m_qkv, m_out, m_in, m_down, m_vec, x_qkv, x_out, x_in, x_down, x_vec, myvec,
    own_down, wo, wi, hb, gp, xh, xb, hbT, turned, xs, xr, gs, gr, ls, os, fs,
):
    p = Place()
    k = p.k
    far = 1 - k
    loads = [
        pltpu.make_async_copy(vec, m_vec, ls.at[4]),
        pltpu.make_async_copy(qkv.at[:, :, half(W3, k)], m_qkv, ls.at[0]),
        pltpu.make_async_copy(out.at[:, half(W3, k)], m_out, ls.at[1]),
        pltpu.make_async_copy(inw.at[:, half(4 * W3, k)], m_in, ls.at[2]),
        pltpu.make_async_copy(down.at[:, half(W3, k)], m_down, ls.at[3]),
        pltpu.make_async_copy(tok_h, tok, ls.at[5]),
    ]
    for c in loads:
        c.start()
    enter([p.sib, p.n1, p.n2] + p.zp)
    swaps = [
        rcopy(qkv.at[:, :, half(W3, far)], x_qkv, xs.at[0], xr.at[0], p.sib),
        rcopy(out.at[:, half(W3, far)], x_out, xs.at[1], xr.at[1], p.sib),
        rcopy(inw.at[:, half(4 * W3, far)], x_in, xs.at[2], xr.at[2], p.sib),
        rcopy(down.at[:, half(W3, far)], x_down, xs.at[3], xr.at[3], p.sib),
        rcopy(myvec, x_vec, xs.at[4], xr.at[4], p.sib),
    ]
    for c in swaps[:4]:
        c.start()
    loads[0].wait()
    pad = jnp.concatenate([m_vec[...], jnp.zeros((128 - 12, 24), f32)], axis=0)
    myvec[...] = jnp.concatenate([pad, jnp.zeros((128, 104), f32)], axis=1).T[:24, :]
    swaps[4].start()

    def both(mine, other):
        lo = jnp.where(k == 0, mine, other)
        hi = jnp.where(k == 0, other, mine)
        return jnp.concatenate([lo, hi], axis=0).astype(bf)

    chip = p.dp * 4 + p.z
    loads[1].wait()
    swaps[0].wait_recv()
    for j in range(3):
        mat = both(m_qkv[j], x_qkv[j])
        for t in range(3):
            wq[band(48, chip), pl.ds(pl.multiple_of((2 * t + k) * W3 + j * 128, 128), 128)] = mat[:, t * 128 : (t + 1) * 128]
    swaps[4].wait_recv()
    vt[band(48, chip), :] = both(myvec[...], x_vec[...])

    chunks = []
    places = [(wq, 48, half(W3, 2 * t + k)) for t in range(3)] + [(wo, 48, half(W3, k))]
    places += [(wi, 48, half(W3, t + 4 * k)) for t in range(4)]
    places += [(w2, 192, half(128, 3 * k + t)) for t in range(3)]
    for ref, rc, cs in places:
        chunks.append([(len(chunks), ref, rc, cs, True, len(chunks) in MIXED)])
    chunks[0].append((11, vt, 48, pl.ds(0, 128), False, False))
    gather = Gather(p, chunks, gs, gr)
    slots = gather.slots(5)
    done = [next(slots)]
    for i in range(3):
        loads[2 + i].wait()
        swaps[1 + i].wait_recv()
    wo[band(48, chip), half(W3, k)] = both(m_out[...], x_out[...])
    wi[band(48, chip), half(4 * W3, k)] = both(m_in[...], x_in[...])
    own_down[...] = both(m_down[...], x_down[...])
    local = pltpu.make_async_copy(own_down, w2.at[band(192, chip), half(W3, k)], ls.at[3])
    local.start()
    local.wait()
    loads[5].wait()
    masks(lengths, onehot, neg)
    outs = []

    def give(src, dst, sem):
        outs.append(pltpu.make_async_copy(src, dst, sem))
        outs[-1].start()

    turned[0] = tok[...].T
    give(turned.at[0], tokT_h, ls.at[6])

    def upto(i):
        while done[0] < i:
            done[0] = next(slots, len(chunks))

    spent = [0.0]

    def spend(us):
        spent[0] += us
        if spent[0] >= PACE_FORWARD and done[0] < len(chunks) - 1:
            spent[0] -= PACE_FORWARD
            done[0] = next(slots)

    upto(0)
    vrow[...] = vt[...].astype(f32).T
    lane = lax.broadcasted_iota(jnp.int32, (1, 128), 1)
    ka[:, 128:] = neg[...]
    va[:, 128:] = jnp.ones((T, 128), bf)
    qa[:, 128:] = onehot[...]
    for turn, pair in enumerate(ORDER):
        upto(turn // 2)
        spend(0.8)
        cs = slice(pair * 128, (pair + 1) * 128)
        y = nn(tok[...], wq[:, turn * W3 : (turn + 1) * W3])
        q = (y[:, :128] + vrow[0:1, cs]).astype(bf)
        key = y[:, 128:256].astype(bf)
        val = (y[:, 256:] + vrow[1:2, cs]).astype(bf)
        us = slice(turn * W3, (turn + 1) * W3)
        for j, part in enumerate((q, key, val)):
            qkvs[:, turn * W3 + j * 128 : turn * W3 + (j + 1) * 128] = part
        give(qkvs.at[:, us], qkv_h.at[:, us], os.at[0, pair])
        qs = (q.astype(f32) * HD ** (-0.5)).astype(bf)
        ka[:, :128] = key
        va[:, :128] = val
        for h in range(2):
            sel = (lane // 64) == h
            qa[:, :128] = jnp.where(sel, qs, jnp.zeros_like(qs))
            for b in range(T // block):
                r = slice(b * block, (b + 1) * block)
                s = nt(qa[r, :], ka[...])
                m = jnp.max(s, axis=1, keepdims=True)
                e = jnp.exp(s - m).astype(bf)
                o = nn(e, va[...])
                tot = o[:, 128:]
                c = o[:, :128] / tot
                l = m + jnp.log(tot)
                ctx[r, cs] = c if h == 0 else jnp.where(sel, c, ctx[r, cs])
                lse[r, :] = l if turn + h == 0 else jnp.where(lane == 2 * pair + h, l, lse[r, :])
                spend(0.55)
        low[:, cs] = ctx[:, cs].astype(bf)
        give(ctx.at[:, cs], ctx_h.at[:, cs], os.at[1, pair])
    give(wq, wqkv_h, ls.at[0])
    row = lambda i: vrow[i : i + 1, :]
    rows = [slice(b * 256, (b + 1) * 256) for b in range(4)]
    turned[1] = low[...].T
    give(turned.at[1], lowT_h, ls.at[4])
    spend(1.5)
    upto(3)
    for r in rows:
        spend(0.7)
        xhat, rd = norm_forward(tok[r, :].astype(f32) + (nn(low[r, :], wo[...]) + row(2)))
        xh[r, :] = xhat
        sd[r, :] = jnp.broadcast_to(rd, (256, 128))
        xb[r, :] = (xhat * row(4) + row(5)).astype(bf)
    give(wo, wo_h, ls.at[1])
    give(xh, xh_h, ls.at[2])
    turned[2] = xb[...].T
    give(turned.at[2], xbT_h, ls.at[3])
    spend(1.5)
    for j in (0, 2, 1, 3):
        upto(5 if j % 2 == 0 else 7)
        cs = slice(j * D, (j + 1) * D)
        for r in rows:
            hp = nn(xb[r, :], wi[:, cs]) + row(8 + j)
            big, dense = gelu_parts(hp)
            hb[r, cs] = (hp * big).astype(bf)
            gp[r, cs] = big + hp * dense
            spend(0.7)
        give(hb.at[:, cs], hb_h.at[:, cs], fs.at[0, j])
        give(gp.at[:, cs], gp_h.at[:, cs], fs.at[1, j])
        hbT[cs, :] = hb[:, cs].T
        give(hbT.at[cs, :], hbT_h.at[cs, :], fs.at[2, j])
        spend(1.5)
    give(wi, wi_h, ls.at[5])
    for c in slots:
        pass
    for c in swaps:
        c.wait_send()
    for c in outs:
        c.wait()


SMEM = pl.BlockSpec(memory_space=pltpu.SMEM)


def forward(tok, lengths, weights, block=256):
    vb = lambda *shape: pltpu.VMEM(shape, bf)
    vf = lambda *shape: pltpu.VMEM(shape, f32)
    dma = lambda *shape: pltpu.SemaphoreType.DMA(shape)
    return pl.pallas_call(
        functools.partial(forward_kernel, block),
        in_specs=[ANY, SMEM] + [ANY] * 5,
        out_specs=[ANY] * 4 + [VM] + [ANY] * 2 + [VM] + [ANY] * 3 + [VM] + [ANY] * 4,
        out_shape=[S((D, 3 * D), bf), S((D, D), bf), S((D, FF), bf), S((FF, D), bf), S((128, D), f32)]
        + [S((T, 3 * D), bf), S((T, D), f32), S((T, 128), f32)]
        + [S((T, FF), bf), S((T, FF), f32), S((T, D), f32), S((T, 128), f32)]
        + [S((D, T), bf)] * 3 + [S((FF, T), bf)],
        scratch_shapes=[
            vb(T, D), vb(D, 3 * D), vb(D, 128), vb(T, 3 * D), vf(T, D), vb(T, D), vb(T, 256), vb(T, 256), vb(T, 256),
            vb(T, 128), vb(T, 128),
            vf(3, 24, W3), vf(24, W3), vf(24, 4 * W3), vf(96, W3), vf(12, 24),
            vf(3, 24, W3), vf(24, W3), vf(24, 4 * W3), vf(96, W3), vf(24, 128), vf(24, 128),
            vb(192, W3), vb(D, D), vb(D, FF), vb(T, FF), vf(T, FF), vf(T, D), vb(T, D), vb(FF, T), vb(3, D, T),
            dma(5), dma(5), dma(12, 10), dma(12, 10), dma(7), dma(2, 6), dma(3, 4),
        ],
        compiler_params=pltpu.CompilerParams(collective_id=0, has_side_effects=True, vmem_limit_bytes=60 * MIB),
        name="forward",
    )(tok, lengths, *weights)


def attend_kernel(block, tok, w, bias, onehot, neg, q_o, k_o, v_o, ctx_o, lse_o, qa, ka, va):
    lane = lax.broadcasted_iota(jnp.int32, (1, 128), 1)
    pair = pl.program_id(0)
    y = nn(tok[...], w[...]) + bias[...]
    q = y[:, :128].astype(bf)
    key = y[:, 128:256].astype(bf)
    val = y[:, 256:].astype(bf)
    q_o[...] = q
    k_o[...] = key
    v_o[...] = val
    qs = (q.astype(f32) * HD ** (-0.5)).astype(bf)
    ka[:, :128] = key
    ka[:, 128:] = neg[...]
    va[:, :128] = val
    va[:, 128:] = jnp.ones((T, 128), bf)
    qa[:, 128:] = onehot[...]
    for h in range(2):
        sel = (lane // 64) == h
        qa[:, :128] = jnp.where(sel, qs, jnp.zeros_like(qs))
        for b in range(T // block):
            r = slice(b * block, (b + 1) * block)
            s = nt(qa[r, :], ka[...])
            m = jnp.max(s, axis=1, keepdims=True)
            e = jnp.exp(s - m).astype(bf)
            o = nn(e, va[...])
            tot = o[:, 128:]
            c = o[:, :128] / tot
            l = m + jnp.log(tot)
            ctx_o[r, :] = c if h == 0 else jnp.where(sel, c, ctx_o[r, :])
            lse_o[r, :] = jnp.where(lane == 2 * pair + h, l, lse_o[r, :])


def attend(tok, w, bias, onehot, neg, block=256):
    full = lambda s: pl.BlockSpec(s, lambda i: (0,) * len(s))
    col = pl.BlockSpec((T, 128), lambda i: (0, i))
    return pl.pallas_call(
        functools.partial(attend_kernel, block),
        grid=(PAIRS,),
        in_specs=[
            full((T, D)), pl.BlockSpec((D, W3), lambda i: (0, i)), pl.BlockSpec((1, W3), lambda i: (0, i)),
            full((T, 128)), full((T, 128)),
        ],
        out_specs=[col, col, col, col, full((T, 128))],
        out_shape=[S((T, D), bf)] * 3 + [S((T, D), f32), S((T, 128), f32)],
        scratch_shapes=[pltpu.VMEM((T, 256), bf)] * 3,
        compiler_params=pltpu.CompilerParams(vmem_limit_bytes=60 * MIB),
        name="attend",
    )(tok, w, bias, onehot, neg)


def split3(x):
    hi = x.astype(bf).astype(f32)
    mid = (x - hi).astype(bf).astype(f32)
    return hi, mid, x - hi - mid


class Back:
    def __init__(self, block, onehot, neg, qa, ka, va, da, kT, dqT, dka, dva):
        self.block, self.onehot, self.neg = block, onehot, neg
        self.refs = (qa, ka, va, da, kT, dqT, dka, dva)
        self.lane = lax.broadcasted_iota(jnp.int32, (1, 128), 1)

    def start(self):
        qa, ka, va, da, kT, dqT, dka, dva = self.refs
        minus = jnp.where((self.lane >= 16) & (self.lane < 19), -1.0, 0.0)
        ka[:, 128:] = (self.neg[...].astype(f32) + minus).astype(bf)
        va[:, 128:] = jnp.broadcast_to(minus, (T, 128)).astype(bf)

    def pair(self, pair, q, key, val, d, ctx, lse, tick):
        lane, block = self.lane, self.block
        qa, ka, va, da, kT, dqT, dka, dva = self.refs
        qs = (q.astype(f32) * HD ** (-0.5)).astype(bf)
        ka[:, :128] = key
        va[:, :128] = val
        kT[...] = key.T
        prod = d.astype(f32) * ctx

        def extra(base, parts):
            for j, part in enumerate(parts):
                base = jnp.where(lane == 16 + j, part, base)
            return base.astype(bf)

        for h in range(2):
            sel = (lane // 64) == h
            inner = jnp.sum(jnp.where(sel, prod, 0.0), axis=1, keepdims=True)
            lsum = jnp.sum(jnp.where(lane == 2 * pair + h, lse, 0.0), axis=1, keepdims=True)
            qa[:, :128] = jnp.where(sel, qs, jnp.zeros_like(qs))
            qa[:, 128:] = extra(self.onehot[...].astype(f32), split3(lsum))
            da[:, :128] = jnp.where(sel, d, jnp.zeros_like(d))
            da[:, 128:] = extra(jnp.zeros((T, 128), f32), split3(inner))
            for b in range(T // block):
                r = slice(b * block, (b + 1) * block)
                pt = jnp.exp(nt(ka[...], qa[r, :]))
                dpt = nt(va[...], da[r, :])
                ds = (pt * dpt).astype(bf)
                x = nn(pt.astype(bf), da[r, :128])
                y = nn(ds, qa[r, :128])
                dqT[h * 64 : (h + 1) * 64, r] = nn(kT[h * 64 : (h + 1) * 64, :], ds)
                if h == 0 and b == 0:
                    dva[...] = x
                    dka[...] = y
                else:
                    dva[...] += x
                    dka[...] += y
                tick()
        dv = dva[...].astype(bf)
        dk = dka[...].astype(bf)
        dq = (dqT[...].T * HD ** (-0.5)).astype(bf)
        return dq, dk, dv


BACK_SCRATCH = (
    [pltpu.VMEM((T, 256), bf)] * 4 + [pltpu.VMEM((128, T), bf), pltpu.VMEM((128, T), f32)] + [pltpu.VMEM((T, 128), f32)] * 2
)


def attend_back_kernel(
    block, tok, w, dh1, q_i, k_i, v_i, dctx_i, ctx_i, lse, onehot, neg, g_o, ig_o, vg_o, *scratch,
):
    tokT, ig = scratch[-2:]
    step = pl.program_id(0)
    back = Back(block, onehot, neg, *scratch[:-2])

    @pl.when(step == 0)
    def _():
        tokT[...] = tok[...].T
        ig[...] = dh1[...]

    back.start()
    dq, dk, dv = back.pair(step, q_i[...], k_i[...], v_i[...], dctx_i[...], ctx_i[...], lse[...], lambda: None)
    vg_o[...] = jnp.zeros_like(vg_o)
    vg_o[0:1, :] = colsum(dq.astype(f32))
    vg_o[1:2, :] = colsum(dv.astype(f32))
    cat = jnp.concatenate([dq, dk, dv], axis=1)
    g_o[...] = nn(tokT[...], cat).astype(bf)
    ig[...] += nt(cat, w[...])

    @pl.when(step == PAIRS - 1)
    def _():
        ig_o[...] = ig[...].astype(bf)


def attend_back(tok, w, dh1, q, k, v, dctx, ctx, lse, onehot, neg, block=512):
    full = lambda s: pl.BlockSpec(s, lambda i: (0,) * len(s))
    col = pl.BlockSpec((T, 128), lambda i: (0, i))
    return pl.pallas_call(
        functools.partial(attend_back_kernel, block),
        grid=(PAIRS,),
        in_specs=[
            full((T, D)), pl.BlockSpec((D, W3), lambda i: (0, i)), full((T, D)),
            col, col, col, col, col, full((T, 128)), full((T, 128)), full((T, 128)),
        ],
        out_specs=[pl.BlockSpec((D, W3), lambda i: (0, i)), full((T, D)), pl.BlockSpec((16, 128), lambda i: (0, i))],
        out_shape=[S((D, 3 * D), bf), S((T, D), bf), S((16, D), f32)],
        scratch_shapes=BACK_SCRATCH + [pltpu.VMEM((D, T), bf), pltpu.VMEM((T, D), f32)],
        compiler_params=pltpu.CompilerParams(vmem_limit_bytes=60 * MIB),
        name="attend_back",
    )(tok, w, dh1, q, k, v, dctx, ctx, lse, onehot, neg)


def fold(x):
    rows, width = x.shape
    x = x * x
    tot = jnp.zeros((8, 128), f32)
    for i in range(rows // 8):
        for j in range(width // 128):
            tot = tot + x[i * 8 : (i + 1) * 8, j * 128 : (j + 1) * 128]
    return tot


def add_rows(dst, row0, src, rows):
    step = min(rows, 384 if src.shape[-1] == W3 else 1024)
    assert rows % step == 0

    def body(i, carry):
        d = pl.ds(pl.multiple_of(row0 + i * step, 16), step)
        s = pl.ds(pl.multiple_of(i * step, 16), step)
        dst[d, :] = (dst[d, :].astype(f32) + src[s, :].astype(f32)).astype(bf)
        return carry

    lax.fori_loop(0, rows // step, body, 0)


OFF = (2, 3, 5)


class Copies:
    def __init__(self, copies):
        self.copies = copies

    def start(self):
        for c in self.copies:
            c.start()

    def wait(self):
        for c in self.copies:
            c.wait()


class Reduce:
    def __init__(self, p, gs, gr, s_vec):
        self.p, self.gs, self.gr, self.s_vec = p, gs, gr, s_vec
        self.sent = []
        self.squares = jnp.zeros((8, 128), f32)

    def go(self, src, dst, n, j, peer):
        c = rcopy(src, dst, self.gs.at[n, j], self.gr.at[n, j], peer)
        c.start()
        self.sent.append(c)
        return c

    def go_x(self, src, dst, ssem, rsem, peer):
        c = rcopy(src, dst, ssem, rsem, peer)
        c.start()
        self.sent.append(c)
        return c

    def send_first(self, part):
        n, rc, acc, give, ready, rs, r2, r1, rz, fin = part
        return self.go(give, rs, n, 0, self.p.sib)

    def slots(self, chunks, issue):
        p, n = self.p, len(chunks)
        cS, cP, cQ, cZ = {}, {}, {}, {}
        for s in range(n + OFF[2]):
            i = s
            if i < n:
                cP[i] = []
                for part, first in zip(chunks[i], issue(i)):
                    num, rc, acc, give, ready, rs, r2, r1, rz, fin = part
                    if give is None:
                        cP[i].append((None, None))
                        continue
                    if ready is not None:
                        ready.wait()
                    first.wait_recv()
                    add_rows(acc, 0, rs, 16 * rc)
                    over = self.go(acc.at[band(4 * rc, p.dp3), :], r2.at[1], num, 2, p.n2)
                    cP[i].append((self.go(acc.at[band(4 * rc, p.dp2), :], r2.at[0], num, 1, p.n2), over))
            i = s - OFF[0]
            if 0 <= i < n:
                cQ[i] = []
                for part, (near, cross) in zip(chunks[i], cP[i]):
                    num, rc, acc, give, ready, rs, r2, r1, rz, fin = part
                    if give is None:
                        ready.wait()
                    else:
                        cross.wait_recv()
                        add_rows(acc, p.dp1 * 4 * rc, r2.at[1], 4 * rc)
                    cQ[i].append(self.go(acc.at[band(4 * rc, p.dp1), :], r1, num, 3, p.n1))
                    if give is not None:
                        near.wait_recv()
                        add_rows(acc, p.dp * 4 * rc, r2.at[0], 4 * rc)
            i = s - OFF[1]
            if 0 <= i < n:
                cZ[i] = []
                for part, q in zip(chunks[i], cQ[i]):
                    num, rc, acc, give, ready, rs, r2, r1, rz, fin = part
                    q.wait_recv()
                    add_rows(acc, p.dp * 4 * rc, r1, 4 * rc)
                    cZ[i].append([
                        self.go(acc.at[band(rc, p.dp * 4 + (p.z + j + 1) % 4), :], rz.at[j], num, 4 + j, p.zp[j]) for j in range(3)
                    ])
            i = s - OFF[2]
            if 0 <= i < n:
                for part, zs in zip(chunks[i], cZ[i]):
                    num, rc, acc, give, ready, rs, r2, r1, rz, fin = part
                    for c in zs:
                        c.wait_recv()
                    own = acc[band(rc, p.dp * 4 + p.z), :].astype(f32)
                    for j in range(3):
                        own = own + rz[j].astype(f32)
                    if fin is None:
                        own = jnp.where(p.k == 0, own[:24], own[24:])
                        self.s_vec[...] = own
                    else:
                        fin[...] = own
                    self.squares = self.squares + fold(own)
            yield s + 1


def backward_kernel(
    block, lengths, tokT_h, wqkv_h, dh1_h, qkv_h, dctx_h, ctx_h, lse, vg_i, gwo, gwi, acc_h,
    ig_h, s_qkv, s_out, s_in, s_down, s_vec, total,
    onehot, neg, wq, ig, qkv, dctx, ctx, gq, gvt, vg,
    qa, ka, va, da, kT, dqT, dka, dva, tokT,
    acc_a, rs_a, r2_a, r1_a, rz_a, acc_d, r1_d, rz_d, acc_v, rs_v, r2_v, r1_v, rz_v,
    fin_a, fin_d, rx_a, rx_d, tile, nb1, nb2, gs, gr, ls, xs, xr, ns, nr, ps, ts, ds,
):
    p = Place()
    k = p.k
    far = 1 - k
    turns = lambda turn, count=1: slice(turn * W3, (turn + count) * W3)
    cols = lambda pair: slice(pair * 128, (pair + 1) * 128)
    early = [pltpu.make_async_copy(tokT_h, tokT, ts.at[0])]
    pairs = {}
    for turn, pair in enumerate(ORDER):
        moves = ((qkv_h, qkv, turns(turn)), (dctx_h, dctx, cols(pair)), (ctx_h, ctx, cols(pair)))
        pairs[pair] = [
            pltpu.make_async_copy(src.at[:, cs], dst.at[:, cs], ps.at[n, pair]) for n, (src, dst, cs) in enumerate(moves)
        ]
    late = [pltpu.make_async_copy(wqkv_h, wq, ts.at[1]), pltpu.make_async_copy(dh1_h, ig, ts.at[2])]
    for c in pairs[0]:
        c.start()
    enter(p.others + p.zp)
    red = Reduce(p, gs, gr, s_vec)

    chunks = []
    for t in range(3):
        loads = Copies([
            pltpu.make_async_copy(acc_h.at[t, band(D, dp), :], acc_d.at[t, band(D, dp), :], ds.at[t, n]) for n, dp in enumerate((p.dp, p.dp1))
        ])
        chunks.append([(t, 192, acc_d.at[t], None, loads, None, None, r1_d.at[t], rz_d.at[t], fin_d.at[t])])
    spots = lambda a: (rs_a.at[a], r2_a.at[a], r1_a.at[a], rz_a.at[a], fin_a.at[a])
    for t in range(5):
        ref, start = (gwi, lambda c: t + 4 * c) if t < 4 else (gwo, lambda c: c)
        load = pltpu.make_async_copy(ref.at[:, half(W3, start(k))], acc_a.at[t], ls.at[t])
        chunks.append([(3 + t, 48, acc_a.at[t], ref.at[:, half(W3, start(far))], load) + spots(t)])
    firsts = {}

    def begin(i):
        if i not in firsts:
            for part in chunks[i]:
                if part[4] is not None:
                    part[4].start()
            firsts[i] = [None if part[3] is None else red.send_first(part) for part in chunks[i]]

    for t in range(3):
        chunks.append([(8 + t, 48, gq.at[t, k], gq.at[t, far], None) + spots(5 + t)])
    chunks[10].append((11, 48, acc_v, gvt, None, rs_v, r2_v, r1_v, rz_v, None))
    for t in range(3):
        chunks[3 + t] += chunks[t]
    sequence = (3, 4, 5, 8, 6, 7, 9, 10)
    ordered = [chunks[i] for i in sequence]
    ready = set(range(3, 8))

    def issue(s):
        for i in sequence[s : s + 3]:
            if i in ready:
                begin(i)
        return firsts[sequence[s]]

    begin(sequence[0])
    begin(sequence[1])

    for c in pairs[3] + early:
        c.start()
    slots = red.slots(ordered, issue)
    place = [0]

    def step():
        place[0] = next(slots, 100)

    back = Back(block, onehot, neg, qa, ka, va, da, kT, dqT, dka, dva)
    masks(lengths, onehot, neg)
    back.start()
    vg[...] = vg_i[...]
    spent = [0.0]
    step()

    def tick(us=1.65):
        spent[0] += us
        if spent[0] >= PACE_BACKWARD and place[0] < len(sequence) and sequence[place[0]] in ready:
            spent[0] -= PACE_BACKWARD
            step()

    for turn, pair in enumerate(ORDER):
        cs = cols(pair)
        for c in pairs[pair]:
            c.wait()
        soon = pairs[ORDER[turn + 2]] if turn + 2 < PAIRS else []
        for c in soon + (late if turn == 2 else []):
            c.start()
        q, key, val = [qkv[:, turn * W3 + j * 128 : turn * W3 + (j + 1) * 128] for j in range(3)]
        dq, dk, dv = back.pair(pair, q, key, val, dctx[:, cs], ctx[:, cs], lse[...], tick)
        for j, part in enumerate((dq, dk, dv)):
            qkv[:, turn * W3 + j * 128 : turn * W3 + (j + 1) * 128] = part
        vg[0:1, cs] = colsum(dq.astype(f32))
        vg[1:2, cs] = colsum(dv.astype(f32))
        t, side = turn // 2, turn % 2
        if turn == 1:
            early[0].wait()
        if side == 1 and t < 2:
            g = nn(tokT[...], qkv[:, turns(2 * t, 2)])
            gq[t, 0] = g[:, :W3].astype(bf)
            gq[t, 1] = g[:, W3:].astype(bf)
            tick(1.6)
            begin(8 + t)
            ready.add(8 + t)
    gq[2, far] = nn(tokT[...], qkv[:, half(W3, 4 + far)]).astype(bf)
    firsts[10] = [red.send_first(chunks[10][0])]
    gvt[...] = jnp.concatenate([vg[...], jnp.zeros((112, D), f32)], axis=0).T.astype(bf)
    acc_v[...] = gvt[...]
    firsts[10].append(red.send_first(chunks[10][1]))
    ready.add(10)
    gq[2, k] = nn(tokT[...], qkv[:, half(W3, 4 + k)]).astype(bf)
    while place[0] < len(sequence) - 1:
        step()
    for c in late:
        c.wait()
    for b in range(4):
        r = slice(b * 256, (b + 1) * 256)
        if b >= 1:
            step()
        dctx[r, :] = (ig[r, :] + nt(qkv[r, :], wq[...])).astype(bf)
    give = pltpu.make_async_copy(dctx, ig_h, ts.at[0])
    give.start()
    for c in slots:
        pass
    cX = []
    for a in range(8):
        cX.append(red.go_x(fin_a.at[a, pl.ds(pl.multiple_of(far * 24, 8), 24), :], rx_a.at[a], xs.at[a], xr.at[a], p.sib))
    for t in range(3):
        cX.append(red.go_x(fin_d.at[t, pl.ds(pl.multiple_of(far * 96, 8), 96), :], rx_d.at[t], xs.at[8 + t], xr.at[8 + t], p.sib))
    part = jnp.sum(jnp.sum(red.squares, axis=1, keepdims=True), axis=0, keepdims=True)
    tile[0] = jnp.broadcast_to(part, (8, 128))
    cN = [red.go_x(tile.at[0], nb1.at[j], ns.at[j], nr.at[j], p.zp[j]) for j in range(3)]
    for c in cN:
        c.wait_recv()
    zsum = jnp.zeros((8, 128), f32)
    for zz in range(4):
        term = tile[0]
        for j in range(3):
            term = jnp.where((p.z + 3 - j) % 4 == zz, nb1[j], term)
        zsum = zsum + term
    tile[1] = zsum
    cN = [red.go_x(tile.at[1], nb2.at[j], ns.at[3 + j], nr.at[3 + j], p.others[j]) for j in range(7)]
    my24 = pl.ds(pl.multiple_of(k * 24, 8), 24)
    for c in cX:
        c.wait_recv()
    for src, side in ((lambda a: fin_a[a, my24, :], k), (lambda a: rx_a[a], far)):
        for t in range(4):
            s_in[:, half(W3, t + 4 * side)] = src(t)
        s_out[:, half(W3, side)] = src(4)
        for t in range(3):
            term = src(5 + t)
            for j in range(3):
                s_qkv[j, :, half(128, 3 * side + t)] = term[:, j * 128 : (j + 1) * 128]
    my96 = pl.ds(pl.multiple_of(k * 96, 8), 96)
    for t in range(3):
        s_down[:, half(128, 3 * k + t)] = fin_d[t, my96, :]
        s_down[:, half(128, 3 * far + t)] = rx_d[t]
    for c in cN:
        c.wait_recv()
    msum = jnp.zeros((8, 128), f32)
    for mm in range(8):
        term = tile[1]
        for j in range(7):
            term = jnp.where((p.m + 7 - j) % 8 == mm, nb2[j], term)
        msum = msum + term
    total[...] = msum
    for c in red.sent:
        c.wait_send()
    give.wait()


def landing(lead, rows, w):
    shapes = ((rows, w), (2, rows // 4, w), (rows // 4, w), (3, rows // 16, w))
    return [pltpu.VMEM(lead + shape, bf) for shape in shapes]


def backward(lengths, tokT, wqkv, dh1, qkv, dctx, ctx, lse, vg, gwo, gwi, acc, block=512):
    vb = lambda *shape: pltpu.VMEM(shape, bf)
    vf = lambda *shape: pltpu.VMEM(shape, f32)
    dma = lambda *shape: pltpu.SemaphoreType.DMA(shape)
    return pl.pallas_call(
        functools.partial(backward_kernel, block),
        in_specs=[SMEM] + [ANY] * 6 + [VM] * 2 + [ANY] * 3,
        out_specs=[ANY] + [VM] * 6,
        out_shape=[S((T, D), bf), S((3, 24, D), f32), S((24, D), f32), S((24, FF), f32), S((96, D), f32), S((24, 128), f32), S((8, 128), f32)],
        scratch_shapes=[
            vb(T, 128), vb(T, 128),
            vb(D, 3 * D), vf(T, D), vb(T, 3 * D), vb(T, D), vf(T, D), vb(3, 2, D, W3), vb(D, 128), vf(16, D),
        ]
        + BACK_SCRATCH + [vb(D, T)]
        + [vb(5, D, W3)] + landing((8,), D, W3) + [vb(3, FF, 128)] + landing((3,), FF, 128)[2:] + [vb(D, 128)] + landing((), D, 128)
        + [
            vf(8, 48, W3), vf(3, 192, 128), vf(8, 24, W3), vf(3, 96, 128), vf(2, 8, 128), vf(3, 8, 128), vf(7, 8, 128),
            dma(12, 7), dma(12, 7), dma(8), dma(11), dma(11), dma(10), dma(10), dma(3, 6), dma(3), dma(3, 2),
        ],
        compiler_params=pltpu.CompilerParams(collective_id=1, has_side_effects=True, vmem_limit_bytes=62 * MIB),
        name="backward",
    )(lengths, tokT, wqkv, dh1, qkv, dctx, ctx, lse, vg, gwo, gwi, acc)


def gelu_parts(x):
    e = jnp.exp(x * x * (-0.5))
    t = 1.0 / (1.0 + (0.3275911 * 0.7071067811865476) * jnp.abs(x))
    poly = 0.5 * 1.061405429
    for a in (-1.453152027, 1.421413741, -0.284496736, 0.254829592):
        poly = 0.5 * a + t * poly
    tail = t * poly * e
    return jnp.where(x >= 0, 1.0 - tail, tail), e * 0.3989422804014327


def norm_forward(h):
    c = h - jnp.mean(h, axis=1, keepdims=True)
    r = lax.rsqrt(jnp.mean(c * c, axis=1, keepdims=True) + norm_epsilon)
    return c * r, r


def norm_backward(dy, xh, r, g):
    dx = dy * g
    return r * (dx - jnp.mean(dx, axis=1, keepdims=True) - xh * jnp.mean(dx * xh, axis=1, keepdims=True))


def ffn_kernel(
    block, tok, ctx, cot, vec, wo_h, wi_h, w2_h, out_o, dh1_o, dctx_o, vg_o, gwo_h, gwi_h, gw2_h,
    wo, wi, w2, cb, x1b, hb, gp, dfb, dhp, dab, stage, tr, insem, outsem,
):
    loads = [
        pltpu.make_async_copy(wo_h, wo, insem.at[0]),
        pltpu.make_async_copy(wi_h, wi, insem.at[1]),
        pltpu.make_async_copy(w2_h, w2, insem.at[2]),
    ]
    for c in loads:
        c.start()
    vg_o[...] = jnp.zeros_like(vg_o)
    row = lambda i: vec[i : i + 1, :]
    for c in loads:
        c.wait()

    def one_block(b, carry):
        r = pl.ds(pl.multiple_of(b * block, block), block)
        c = ctx[r, :].astype(bf)
        cb[r, :] = c
        xh1, r1 = norm_forward(tok[r, :].astype(f32) + (nn(c, wo[...]) + row(2)))
        x1 = xh1 * row(4) + row(5)
        xb = x1.astype(bf)
        x1b[r, :] = xb
        acc = x1 + row(3)
        for j in range(4):
            cs = slice(j * D, (j + 1) * D)
            hp = nn(xb, wi[:, cs]) + row(8 + j)
            big, dense = gelu_parts(hp)
            h = (hp * big).astype(bf)
            hb[r, cs] = h
            gp[:, cs] = big + hp * dense
            acc = acc + nn(h, w2[cs, :])
        xh2, r2 = norm_forward(acc)
        out_o[r, :] = (xh2 * row(6) + row(7)).astype(bf)
        dy = cot[r, :].astype(f32)
        vg_o[6:7, :] += colsum(dy * xh2)
        vg_o[7:8, :] += colsum(dy)
        dh2 = norm_backward(dy, xh2, r2, row(6))
        df = dh2.astype(bf)
        dfb[r, :] = df
        vg_o[3:4, :] += colsum(df.astype(f32))
        dx1 = dh2
        for j in range(4):
            cs = slice(j * D, (j + 1) * D)
            dh = (gp[:, cs] * nt(df, w2[cs, :])).astype(bf)
            dhp[r, cs] = dh
            vg_o[8 + j : 9 + j, :] += colsum(dh.astype(f32))
            dx1 = dx1 + nt(dh, wi[:, cs])
        vg_o[4:5, :] += colsum(dx1 * xh1)
        vg_o[5:6, :] += colsum(dx1)
        dh1 = norm_backward(dx1, xh1, r1, row(4))
        dh1_o[r, :] = dh1
        da = dh1.astype(bf)
        dab[r, :] = da
        vg_o[2:3, :] += colsum(da.astype(f32))
        dctx_o[r, :] = nt(da, wo[...]).astype(bf)
        return carry

    lax.fori_loop(0, T // block, one_block, 0)
    outs = []

    def emit(val, dst):
        i = len(outs)
        if i >= 2:
            outs[i - 2].wait()
        stage[i % 2] = val.astype(bf)
        c = pltpu.make_async_copy(stage.at[i % 2], dst, outsem.at[i % 2])
        c.start()
        outs.append(c)

    for j in range(4):
        cs = slice(j * D, (j + 1) * D)
        emit(tn(hb[:, cs], dfb[...]), gw2_h.at[cs, :])
    tr[...] = x1b[...].T
    for j in range(4):
        cs = slice(j * D, (j + 1) * D)
        emit(nn(tr[...], dhp[:, cs]), gwi_h.at[:, cs])
    emit(tn(cb[...], dab[...]), gwo_h)
    outs[7].wait()
    outs[8].wait()


def feed_forward(tok, ctx, cot, vec, wo, wi, w2, block=256):
    return pl.pallas_call(
        functools.partial(ffn_kernel, block),
        in_specs=[VM] * 4 + [ANY] * 3,
        out_specs=[VM] * 4 + [ANY] * 3,
        out_shape=[
            S((T, D), bf), S((T, D), f32), S((T, D), bf), S((16, D), f32), S((D, D), bf), S((D, FF), bf), S((FF, D), bf),
        ],
        scratch_shapes=[
            pltpu.VMEM((D, D), bf), pltpu.VMEM((D, FF), bf), pltpu.VMEM((FF, D), bf), pltpu.VMEM((T, D), bf),
            pltpu.VMEM((T, D), bf), pltpu.VMEM((T, FF), bf), pltpu.VMEM((block, FF), f32), pltpu.VMEM((T, D), bf),
            pltpu.VMEM((T, FF), bf), pltpu.VMEM((T, D), bf), pltpu.VMEM((2, D, D), bf), pltpu.VMEM((D, T), bf),
            pltpu.SemaphoreType.DMA((3,)), pltpu.SemaphoreType.DMA((2,)),
        ],
        compiler_params=pltpu.CompilerParams(vmem_limit_bytes=60 * MIB),
        name="feed_forward",
    )(tok, ctx, cot, vec, wo, wi, w2)


def middle_kernel(
    block, cot_h, vec_h, wo_h, wi_h, w2_h, hb_h, gp_h, xh_h, sd, hbT_h, xbT_h, lowT_h, out_h, dh1_h, dctx_h, vg, gwo_h, gwi_h, acc_h,
    vec, wo, wi, w2, out, cot, xh1, hb, gp, hT, dfb, dh, da, gw2, rs, r2, ls, os, xs, xr, gs,
):
    p = Place()
    k = p.k
    far = 1 - k
    top, low_part = slice(0, T // 2), slice(T // 2, T)
    xbT, lowT, go = hT.at[0:D, :], hT.at[D : 2 * D, :], hT.at[2 * D : 3 * D, 0:D]
    moves = [(w2_h, w2), (vec_h, vec)]
    for part in (top, low_part):
        moves += [(src.at[part, :], dst.at[part, :]) for src, dst in ((hb_h, hb), (xh_h, xh1), (cot_h, cot))]
    moves += [(hbT_h, hT), (gp_h, gp), (wi_h, wi), (wo_h, wo), (xbT_h, xbT), (lowT_h, lowT)]
    loads = [pltpu.make_async_copy(src, dst, ls.at[i]) for i, (src, dst) in enumerate(moves)]

    def start(first, last):
        for c in loads[first:last]:
            c.start()

    def arrive(first, last):
        for c in loads[first:last]:
            c.wait()

    start(0, 5)
    enter([p.sib, p.n2])
    vg[...] = jnp.zeros_like(vg)
    row = lambda i: vec[i : i + 1, :]
    rows = [slice(b * block, (b + 1) * block) for b in range(T // block)]
    quarter = [slice(j * D, (j + 1) * D) for j in range(4)]
    outs = []

    def give(src, dst):
        outs.append(pltpu.make_async_copy(src, dst, os.at[len(outs)]))
        outs[-1].start()

    arrive(0, 5)
    start(5, 12)
    for r in rows:
        if r.start == T // 2:
            arrive(5, 8)
        acc = xh1[r, :] * row(4) + row(5) + (nn(hb[r, :], w2[...]) + row(3))
        xh2, r2d = norm_forward(acc)
        out[r, :] = (xh2 * row(6) + row(7)).astype(bf)
        dy = cot[r, :].astype(f32)
        vg[6:7, :] += colsum(dy * xh2)
        vg[7:8, :] += colsum(dy)
        dh2 = norm_backward(dy, xh2, r2d, row(6))
        dh[r, :] = dh2
        df = dh2.astype(bf)
        dfb[r, :] = df
        vg[3:4, :] += colsum(df.astype(f32))
    give(out, out_h)
    arrive(8, 9)
    sent, swaps, near, cross = [], [], [], []

    def go_to(src, dst, t, j, peer):
        c = rcopy(src, dst, xs.at[t, j], xr.at[t, j], peer)
        c.start()
        sent.append(c)
        return c

    for t in range(3):
        both = jnp.concatenate([dfb[:, t * 128 : (t + 1) * 128], dfb[:, (t + 3) * 128 : (t + 4) * 128]], axis=1)
        for cs in quarter:
            g = nn(hT[cs, :], both).astype(bf)
            gw2[t, 0, cs, :] = g[:, :128]
            gw2[t, 1, cs, :] = g[:, 128:]
        swaps.append(go_to(gw2.at[t, far], rs.at[t], t, 0, p.sib))

    def over(t):
        mine = gw2.at[t, k]
        swaps[t].wait_recv()
        add_rows(mine, 0, rs.at[t], FF)
        cross.append(go_to(mine.at[band(D, p.dp3), :], r2.at[t, 1], t, 1, p.n2))
        near.append(go_to(mine.at[band(D, p.dp2), :], r2.at[t, 0], t, 2, p.n2))

    def back(t):
        mine = gw2.at[t, k]
        for n, (c, dp) in enumerate(((near[t], p.dp), (cross[t], p.dp1))):
            c.wait_recv()
            add_rows(mine, dp * D, r2.at[t, n], D)
            outs.append(pltpu.make_async_copy(mine.at[band(D, dp), :], acc_h.at[t, band(D, dp), :], gs.at[t, n]))
            outs[-1].start()

    arrive(9, 12)
    start(12, 14)
    for b, r in enumerate(rows):
        if b < 3:
            over(b)
        else:
            back(0)
        df = dfb[r, :]
        for j, cs in enumerate(quarter):
            low = (gp[r, cs] * nt(df, w2[cs, :])).astype(bf)
            hb[r, cs] = low
            vg[8 + j : 9 + j, :] += colsum(low.astype(f32))
        dx1 = dh[r, :] + nt(hb[r, :], wi[...])
        xh = xh1[r, :]
        vg[4:5, :] += colsum(dx1 * xh)
        vg[5:6, :] += colsum(dx1)
        dh1 = norm_backward(dx1, xh, sd[r, 0:1], row(4))
        dh[r, :] = dh1
        low = dh1.astype(bf)
        da[r, :] = low
        vg[2:3, :] += colsum(low.astype(f32))
        cot[r, :] = nt(low, wo[...]).astype(bf)
    give(dh, dh1_h)
    give(cot, dctx_h)
    back(1)
    back(2)
    arrive(12, 14)
    for cs in quarter:
        wi[:, cs] = nn(xbT[...], hb[:, cs]).astype(bf)
    give(wi, gwi_h)
    go[...] = nn(lowT[...], da[...]).astype(bf)
    give(go, gwo_h)
    for c in sent:
        c.wait_send()
    for c in outs:
        c.wait()


def middle(cot, vec, wo, wi, w2, hb, gp, xh, sd, hbT, xbT, lowT, block=256):
    vb = lambda *shape: pltpu.VMEM(shape, bf)
    vf = lambda *shape: pltpu.VMEM(shape, f32)
    dma = lambda *shape: pltpu.SemaphoreType.DMA(shape)
    return pl.pallas_call(
        functools.partial(middle_kernel, block),
        in_specs=[ANY] * 8 + [VM] + [ANY] * 3,
        out_specs=[ANY] * 3 + [VM] + [ANY] * 3,
        out_shape=[
            S((T, D), bf), S((T, D), f32), S((T, D), bf), S((16, D), f32), S((D, D), bf), S((D, FF), bf), S((3, FF, 128), bf),
        ],
        scratch_shapes=[
            vf(128, D), vb(D, D), vb(D, FF), vb(FF, D), vb(T, D), vb(T, D), vf(T, D),
            vb(T, FF), vf(T, FF), vb(FF, T), vb(T, D), vf(T, D), vb(T, D),
            vb(3, 2, FF, 128), vb(3, FF, 128), vb(3, 2, D, 128), dma(14), dma(11), dma(3, 3), dma(3, 3), dma(3, 2),
        ],
        compiler_params=pltpu.CompilerParams(collective_id=2, has_side_effects=True, vmem_limit_bytes=62 * MIB),
        name="middle",
    )(cot, vec, wo, wi, w2, hb, gp, xh, sd, hbT, xbT, lowT)


def adam_step(weight, gradient, first_old, second_old, decay_rate, step_rate):
    first_new = moment_decay * first_old + (1.0 - moment_decay) * gradient
    second_new = square_decay * second_old + (1.0 - square_decay) * gradient * gradient
    first_hat = first_new / (1.0 - moment_decay**STEP)
    second_hat = second_new / (1.0 - square_decay**STEP)
    weight_new = weight - step_rate * (first_hat / (jnp.sqrt(second_hat) + adam_epsilon) + decay_rate * weight)
    return (weight_new, first_new, second_new)


def update_kernel(total, ig_h, *refs):
    hbm, outs, bufs, sem, osem = refs[0:20], refs[20:37], refs[37:58], refs[58], refs[59]
    ig_o, norm_o, new_h = outs[0], outs[1], outs[2:17]
    g, w, m, u, ig = bufs[0:5], bufs[5:10], bufs[10:15], bufs[15:20], bufs[20]
    order = [i + 5 * j for i in (2, 3, 0, 1, 4) for j in range(4)]
    loads = {i: pltpu.make_async_copy(hbm[i], bufs[i], sem.at[i]) for i in order}
    through = pltpu.make_async_copy(ig_h, ig, sem.at[20])
    for i in order:
        loads[i].start()
    through.start()
    norm = jnp.sqrt(total[...])
    norm_o[0, 0] = norm[0, 0]
    factor = jnp.minimum(1.0, clip_limit / (norm + 1e-06))[0:1, 0:1]
    gone = []

    def give(src, dst):
        gone.append(pltpu.make_async_copy(src, dst, osem.at[len(gone)]))
        gone[-1].start()

    for i in (2, 3, 0, 1, 4):
        for j in range(4):
            loads[i + 5 * j].wait()
        if i < 4:
            new = adam_step(w[i][...], factor * g[i][...], m[i][...], u[i][...], weight_decay, learn_rate)
        else:
            wide = jnp.concatenate([g[4][...], jnp.zeros((104, 128), f32)], axis=0).T[:12, :24]
            new = adam_step(w[4][...], factor * wide, m[4][...], u[4][...], 0.0, vector_rate)
        for j, (place, val) in enumerate(zip((w, m, u), new)):
            place[i][...] = val
            give(place[i], new_h[i + 5 * j])
        if i == 2:
            through.wait()
            give(ig, ig_o)
    for c in gone:
        c.wait()


def update(total, input_grad, weights, grads, firsts, seconds):
    arrays = (*grads, *weights, *firsts, *seconds)
    shapes = [S(w.shape, f32) for w in weights]
    return pl.pallas_call(
        update_kernel,
        in_specs=[VM] + [ANY] * 21,
        out_specs=[ANY, SMEM] + [ANY] * 15,
        out_shape=[S(input_grad.shape, bf), S((1, 1), f32)] + shapes * 3,
        scratch_shapes=[pltpu.VMEM(a.shape, f32) for a in arrays]
        + [pltpu.VMEM(input_grad.shape, bf), pltpu.SemaphoreType.DMA((21,)), pltpu.SemaphoreType.DMA((16,))],
        compiler_params=pltpu.CompilerParams(vmem_limit_bytes=62 * MIB),
        name="clip_and_update",
    )(total, input_grad, *grads, *weights, *firsts, *seconds)


def segment_ids(lengths):
    bounds = jnp.cumsum(lengths, axis=-1)
    places = jnp.arange(T, dtype=jnp.int32)
    return jnp.sum((places[:, None] >= bounds[None, :]).astype(jnp.int32), axis=-1)


def pairs_last(a):
    return a.reshape(3, D, PAIRS, 128).transpose(1, 2, 0, 3).reshape(D, 3 * D)


def per_device(
    small, tokens, cotangent, lengths, qkv_weight, out_weight, in_weight, down_weight, vectors,
    qkv_first, out_first, in_first, down_first, vec_first, qkv_second, out_second, in_second, down_second, vec_second,
):
    weights = (qkv_weight, out_weight, in_weight, down_weight, vectors)
    firsts = (qkv_first, out_first, in_first, down_first, vec_first)
    seconds = (qkv_second, out_second, in_second, down_second, vec_second)
    axes = ("dp", "fsdp")
    if small:
        wqkv, wo, wi, w2, vec, qkv, ctx, lse, hb, gp, xh, sd, tokT, lowT, xbT, hbT = forward(tokens, lengths, weights)
        result, dh1, dctx, vg, gwo, gwi, acc = middle(cotangent, vec, wo, wi, w2, hb, gp, xh, sd, hbT, xbT, lowT)
        ig, *grads, total = backward(lengths, tokT, wqkv, dh1, qkv, dctx, ctx, lse, vg, gwo, gwi, acc)
        updated = update(total, ig, weights, grads, firsts, seconds)
        return (result, updated[0], updated[1].reshape(()), *updated[2:])
    seg = segment_ids(lengths[0])
    lane = jnp.arange(128)
    match = seg[:, None] == lane[None, :]
    onehot = match.astype(bf)
    neg = jnp.where(match | (lane >= lengths.shape[1])[None, :], 0.0, -1e30).astype(bf)
    gather = lambda a, axis: lax.all_gather(a.astype(bf), axes, axis=axis, tiled=True)
    wqkv = pairs_last(gather(qkv_weight, 1))
    wo, wi, w2 = gather(out_weight, 0), gather(in_weight, 0), gather(down_weight, 0)
    vec = jnp.concatenate([gather(vectors, 1).astype(f32), jnp.zeros((4, D), f32)], axis=0)
    bias = jnp.stack([vec[0], jnp.zeros_like(vec[0]), vec[1]]).reshape(3, PAIRS, 128).transpose(1, 0, 2).reshape(1, 3 * D)
    q, k, v, ctx, lse = attend(tokens, wqkv, bias, onehot, neg)
    result, dh1, dctx, vg, gwo, gwi, gw2 = feed_forward(tokens, ctx, cotangent, vec, wo, wi, w2)
    gqkv, input_grad, vg_qv = attend_back(tokens, wqkv, dh1, q, k, v, dctx, ctx, lse, onehot, neg)
    vg = vg + vg_qv
    scatter = lambda a, axis: lax.psum_scatter(a.astype(f32), axes, scatter_dimension=axis, tiled=True)
    gqkv = gqkv.reshape(D, PAIRS, 3, 128).transpose(2, 0, 1, 3).reshape(3, D, D)
    grads = (scatter(gqkv, 1), scatter(gwo, 0), scatter(gwi, 0), scatter(gw2, 0), scatter(vg[:12], 1))
    grad_norm = jnp.sqrt(lax.psum(sum(jnp.sum(g * g) for g in grads), axes))
    factor = jnp.minimum(1.0, clip_limit / (grad_norm + 1e-06))
    updated = []
    for i in range(5):
        rates = (0.0, vector_rate) if i == 4 else (weight_decay, learn_rate)
        updated.append(adam_step(weights[i], factor * grads[i], firsts[i], seconds[i], *rates))
    return (result, input_grad, grad_norm, *[u[j] for j in range(3) for u in updated])


def solution(mesh):
    rows = P(("dp", "fsdp"), None)
    deep = P(None, ("dp", "fsdp"), None)
    wide = P(None, ("dp", "fsdp"))
    group = (deep, rows, rows, rows, wide)
    small = mesh.shape["dp"] == 4 and mesh.shape["fsdp"] == 8
    return jax.shard_map(
        functools.partial(per_device, small),
        mesh=mesh,
        in_specs=(rows, rows, rows) + group * 3,
        out_specs=(rows, rows, P()) + group * 3,
        check_vma=False,
    )
```
